256 devices in a mesh: panel: 2 (over y_hi), colat: 8 (over x, core), lon: 16 (over z, y_lo).
Axes of the slice: x: 4, y: 4 (y_hi: 2, y_lo: 2; y = y_hi * 2 + y_lo), z: 8, core: 2. Of those that a mesh axis runs over, the one named last changes fastest.
Arguments:
- state: float32 [2, 7, 256, 16384], P('panel', None, 'colat', 'lon'), may hold values from -6 to 6
- spin: float32 [2, 256, 512], P('panel', 'colat', 'lon'), may hold values from -1 to 1
- donor_device: int32 [4, 1536], replicated, may hold values from 0 to 127, as said below
- donor_row: int32 [4, 1536], replicated, may hold values from 0 to 31, as said below
- donor_col: int32 [4, 1536], replicated, may hold values from 0 to 31, as said below
- corner_weights: float32 [4, 1536], replicated, may hold values from 0 to 1, as said below
- border_angle: float32 [1536], replicated, may hold values from -3.8 to 3.8, as said below
Outputs:
- advanced: float32 [2, 7, 256, 16384], P('panel', None, 'colat', 'lon')
The draws below stay inside these ranges and needn't reach their ends.
Inputs may be any that keep to these rules, and one draw needn't show every extreme that they name: `donor_device`: devices of a panel are numbered colatitude block * 16 + longitude block. The four corners c = 0, 1, 2, 3 of a border point are the cells (i, j), (i+1, j), (i, j+1), (i+1, j+1) of one square of the other panel, never in that panel's border rows or columns. `donor_row`: local row of the corner named by donor_device. `donor_col`: local column of the corner named by donor_device. `corner_weights`: bilinear weights: the four of a border point are products of (1 - a or a) and (1 - s or s) and sum to one. `border_angle`: angle in radians.
All inputs are finite; a program needn't handle non-finite values.
Results may differ from the reference program's by a relative error of at most 0.00016.
Values sent between devices are 32-bit elements; how exact they have to be, the bound alone decides.
A program may use at most 64 MiB of HBM per device.

```python
import jax
import jax.numpy as jnp

FIELDS = 7
CTH = 32
CPH = 32
NR = 32
NTH = 256
NPH = 512
NB = 1536
N_LON = 16


def panel_geometry():
    row_step = jnp.pi / (2.0 * NTH)
    col_step = 1.5 * jnp.pi / NPH
    row_angles = jnp.pi / 4 + (jnp.arange(NTH, dtype=jnp.float32) + 0.5) * row_step
    col_angles = -0.75 * jnp.pi + (jnp.arange(NPH, dtype=jnp.float32) + 0.5) * col_step
    polar = jnp.concatenate([jnp.full((NPH,), row_angles[0]), jnp.full((NPH,), row_angles[-1]), row_angles, row_angles])
    azimuth = jnp.concatenate([col_angles, col_angles, jnp.full((NTH,), col_angles[0]), jnp.full((NTH,), col_angles[-1])])
    coord_x = jnp.sin(polar) * jnp.cos(azimuth)
    coord_y = jnp.sin(polar) * jnp.sin(azimuth)
    coord_z = jnp.cos(polar)
    other_x = -coord_x
    other_y = coord_z
    other_z = coord_y
    other_polar = jnp.arccos(jnp.clip(other_z, -1.0, 1.0))
    other_azimuth = jnp.arctan2(other_y, other_x)
    row_place = (other_polar - jnp.pi / 4) / row_step - 0.5
    col_place = (other_azimuth + 0.75 * jnp.pi) / col_step - 0.5
    row_base = jnp.clip(jnp.floor(row_place), 1, NTH - 3)
    col_base = jnp.clip(jnp.floor(col_place), 1, NPH - 3)
    row_frac = jnp.clip(row_place - row_base, 0.0, 1.0)
    col_frac = jnp.clip(col_place - col_base, 0.0, 1.0)
    other_theta_x = jnp.cos(other_polar) * jnp.cos(other_azimuth)
    other_theta_y = jnp.cos(other_polar) * jnp.sin(other_azimuth)
    other_theta_z = -jnp.sin(other_polar)
    back_x = -other_theta_x
    back_y = other_theta_z
    back_z = other_theta_y
    theta_dot = jnp.cos(polar) * jnp.cos(azimuth) * back_x + jnp.cos(polar) * jnp.sin(azimuth) * back_y - jnp.sin(polar) * back_z
    phi_dot = -jnp.sin(azimuth) * back_x + jnp.cos(azimuth) * back_y
    base_angle = jnp.arctan2(phi_dot, theta_dot)
    return (row_base.astype(jnp.int32), col_base.astype(jnp.int32), row_frac.astype(jnp.float32), col_frac.astype(jnp.float32), base_angle.astype(jnp.float32))


def corner_cells(key):
    row_base, col_base, row_frac, col_frac, base_angle = panel_geometry()
    row_key, col_key = jax.random.split(key)
    row_shift = jax.random.randint(row_key, (NB,), -1, 2)
    col_shift = jax.random.randint(col_key, (NB,), -1, 2)
    base_row = jnp.clip(jnp.asarray(row_base) + row_shift, 1, NTH - 3).astype(jnp.int32)
    base_col = jnp.clip(jnp.asarray(col_base) + col_shift, 1, NPH - 3).astype(jnp.int32)
    far_row = NTH // CTH // 2 * CTH
    base_row = base_row.at[1].set(far_row).at[2].set(1)
    base_col = base_col.at[1].set(1).at[2].set(1)
    row_step = jnp.array([0, 1, 0, 1], jnp.int32)
    col_step = jnp.array([0, 0, 1, 1], jnp.int32)
    return (base_row[None, :] + row_step[:, None], base_col[None, :] + col_step[:, None])


def draw_donor_device(key, part):
    row_cells, col_cells = corner_cells(key)
    return (row_cells // CTH * (NPH // CPH) + col_cells // CPH).astype(jnp.int32)


def draw_donor_row(key, part):
    row_cells, col_cells = corner_cells(key)
    return (row_cells % CTH).astype(jnp.int32)


def draw_donor_col(key, part):
    row_cells, col_cells = corner_cells(key)
    return (col_cells % CPH).astype(jnp.int32)


def bilinear(key, spread, lower_end, upper_end):
    row_base, col_base, row_frac, col_frac, base_angle = panel_geometry()
    first_key, second_key = jax.random.split(key)
    along_a = jnp.clip(jnp.asarray(row_frac) + jax.random.uniform(first_key, (NB,), jnp.float32, -spread, spread), lower_end, upper_end)
    along_b = jnp.clip(jnp.asarray(col_frac) + jax.random.uniform(second_key, (NB,), jnp.float32, -spread, spread), lower_end, upper_end)
    return jnp.stack([(1.0 - along_a) * (1.0 - along_b), along_a * (1.0 - along_b), (1.0 - along_a) * along_b, along_a * along_b])


def draw_corner_weights(key, part):
    key = jax.random.fold_in(key, 7)
    return bilinear(key, 0.25, 0.02, 0.98)


def turned_angle(key, spread):
    row_base, col_base, row_frac, col_frac, base_angle = panel_geometry()
    return jnp.asarray(base_angle) + jax.random.uniform(key, (NB,), jnp.float32, -spread, spread)


def draw_border_angle(key, part):
    key = jax.random.fold_in(key, 11)
    return turned_angle(key, 0.3)


def levels(stream_key, extent, cuts, low, high):
    def one(dim, parts):
        draws = jax.random.uniform(jax.random.fold_in(jax.random.fold_in(stream_key, 6), dim), (parts,), jnp.float32, low / len(cuts), high / len(cuts))
        return jnp.repeat(jnp.exp(draws), extent[dim] // parts).reshape((-1,) + (1,) * (len(extent) - dim - 1))

    gain = one(*cuts[0])
    for cut in cuts[1:]:
        gain = gain * one(*cut)
    return gain


def centred(rng, dims, scale, limit, cuts=(), kind=jnp.bfloat16):
    entries = jax.random.normal(rng, dims, jnp.float32) * scale
    if len(cuts) > 0:
        entries = levels(rng, dims, cuts, -0.22, 0.18) * entries
    return jnp.clip(entries, min=-limit, max=limit).astype(kind)


def setup_inputs(seed: int = 0) -> dict:
    arg_keys = jax.random.split(jax.random.key(seed), 8)
    state = centred(arg_keys[0], (2, FIELDS, NTH, NPH * NR), 1.0, 6.0, ((0, 2), (2, 8), (3, 16)), jnp.float32)
    spin = jnp.clip(jax.random.uniform(arg_keys[1], (2, NTH, NPH), jnp.float32, -1.0, 1.0) * levels(arg_keys[1], (2, NTH, NPH), ((0, 2), (1, 8), (2, 16)), -0.4, 0.0), -1.0, 1.0)
    donor_device = draw_donor_device(jax.random.fold_in(arg_keys[7], 71), 0)
    donor_row = draw_donor_row(jax.random.fold_in(arg_keys[7], 71), 0)
    donor_col = draw_donor_col(jax.random.fold_in(arg_keys[7], 71), 0)
    corner_weights = draw_corner_weights(jax.random.fold_in(arg_keys[7], 71), 0)
    border_angle = draw_border_angle(jax.random.fold_in(arg_keys[7], 71), 0)
    return dict(state=state, spin=spin, donor_device=donor_device, donor_row=donor_row, donor_col=donor_col, corner_weights=corner_weights, border_angle=border_angle)


viscosity = 0.3
conduction = 0.4
resistance = 0.5
buoyancy = 1.0
timestep = 0.2


def field_rates(fields, north_cells, south_cells, west_cells, east_cells, upper_cells, lower_cells, metric_t, metric_p, spin_cells):
    colat_slope = metric_t * (0.5 * (south_cells - north_cells))
    lon_slope = metric_p * (0.5 * (east_cells - west_cells))
    radial_slope = 0.5 * (upper_cells - lower_cells)
    laplace = metric_t * metric_t * (south_cells + north_cells - 2.0 * fields) + metric_p * metric_p * (east_cells + west_cells - 2.0 * fields) + (upper_cells + lower_cells - 2.0 * fields)
    advected = fields[0] * colat_slope + fields[1] * lon_slope + fields[2] * radial_slope
    stretched = fields[4] * colat_slope + fields[5] * lon_slope + fields[6] * radial_slope
    diffuse_rate = jnp.array([viscosity, viscosity, viscosity, conduction, resistance, resistance, resistance], jnp.float32)
    diffuse_rate = diffuse_rate.reshape((7,) + (1,) * (fields.ndim - 1))
    base_rate = diffuse_rate * laplace - advected
    return jnp.stack([
        base_rate[0] + stretched[4] + spin_cells * fields[1],
        base_rate[1] + stretched[5] - spin_cells * fields[0],
        base_rate[2] + stretched[6] + buoyancy * fields[3],
        base_rate[3],
        base_rate[4] + stretched[0],
        base_rate[5] + stretched[1],
        base_rate[6] + stretched[2]])


def panel_rates(fields, metric_t, metric_p, spin_cells):
    padded = jnp.pad(fields, ((0, 0), (1, 1), (1, 1), (0, 0)))
    north_cells = padded[:, :-2, 1:-1]
    south_cells = padded[:, 2:, 1:-1]
    west_cells = padded[:, 1:-1, :-2]
    east_cells = padded[:, 1:-1, 2:]
    upper_cells = jnp.concatenate([fields[..., 1:], fields[..., -1:]], axis=-1)
    lower_cells = jnp.concatenate([fields[..., :1], fields[..., :-1]], axis=-1)
    return field_rates(fields, north_cells, south_cells, west_cells, east_cells, upper_cells, lower_cells, metric_t, metric_p, spin_cells)


def reference(state, spin, donor_device, donor_row, donor_col, corner_weights, border_angle):
    fields = state.reshape(2, FIELDS, NTH, NPH, NR)
    row_number = jnp.arange(NTH, dtype=jnp.float32)
    colat_angle = jnp.pi / 4 + (row_number + 0.5) * (jnp.pi / (2.0 * NTH))
    shells = jnp.arange(NR, dtype=jnp.float32)
    inv_radius = 1.0 / (1.0 + 0.25 * (shells + 0.5) / NR)
    metric_t = inv_radius[None, None, :]
    metric_p = inv_radius[None, None, :] / jnp.sin(colat_angle)[:, None, None]
    rows_global = (donor_device // N_LON) * CTH + donor_row
    cols_global = (donor_device % N_LON) * CPH + donor_col
    cosine = jnp.cos(border_angle)[:, None]
    sine_part = jnp.sin(border_angle)[:, None]

    def all_rates(current):
        return jnp.stack([panel_rates(current[side], metric_t, metric_p, spin[side][:, :, None]) for side in range(2)])

    def border_values(other_panel):
        values = jnp.zeros((FIELDS, NB, NR), jnp.float32)
        for corner in range(4):
            picked = other_panel[:, rows_global[corner], cols_global[corner], :]
            values = values + corner_weights[corner][None, :, None] * picked
        return jnp.stack([
            cosine * values[0] - sine_part * values[1],
            sine_part * values[0] + cosine * values[1],
            values[2],
            values[3],
            cosine * values[4] - sine_part * values[5],
            sine_part * values[4] + cosine * values[5],
            values[6]])

    def place_border(panel_fields, values):
        top_row = values[:, 0:NPH]
        bottom_row = values[:, NPH:2 * NPH]
        left_col = values[:, 2 * NPH:2 * NPH + NTH]
        right_col = values[:, 2 * NPH + NTH:]
        panel_fields = panel_fields.at[:, 0].set(top_row).at[:, NTH - 1].set(bottom_row)
        left_col = left_col.at[:, 0].set(0.5 * (left_col[:, 0] + top_row[:, 0]))
        left_col = left_col.at[:, NTH - 1].set(0.5 * (left_col[:, NTH - 1] + bottom_row[:, 0]))
        right_col = right_col.at[:, 0].set(0.5 * (right_col[:, 0] + top_row[:, NPH - 1]))
        right_col = right_col.at[:, NTH - 1].set(0.5 * (right_col[:, NTH - 1] + bottom_row[:, NPH - 1]))
        return panel_fields.at[:, :, 0].set(left_col).at[:, :, NPH - 1].set(right_col)

    def fill(current):
        yin_panel = place_border(current[0], border_values(current[1]))
        yang_panel = place_border(current[1], border_values(current[0]))
        return jnp.stack([yin_panel, yang_panel])

    middle = fill(fields + 0.5 * timestep * all_rates(fields))
    advanced = fill(fields + timestep * all_rates(middle))
    return advanced.reshape(2, FIELDS, NTH, NPH * NR)
```

```python
import functools

import jax
import jax.numpy as jnp
from jax import lax
from jax.experimental import pallas as pl
from jax.experimental.pallas import tpu as pltpu
from jax.sharding import PartitionSpec as P

MESH = pl.DeviceIdType.MESH
F32, BF16, I32 = jnp.float32, jnp.bfloat16, jnp.int32
ROWS, COLS, WIDTH, LANES = 32, 32, 1024, 128
POINTS, HUBS, SLOTS, SEGMENTS = 1536, 16, 4, 48
DIFFUSE = (0.3, 0.3, 0.3, 0.4, 0.5, 0.5, 0.5)


def iota(shape, dim):
    return lax.broadcasted_iota(I32, shape, dim)


def flag01(cond):
    return jnp.where(cond, 1.0, 0.0).astype(BF16)


def split2(x):
    hi = x.astype(BF16)
    return hi, (x - hi.astype(F32)).astype(BF16)


def split3(x):
    hi, rest = x.astype(BF16), None
    rest = x - hi.astype(F32)
    mid = rest.astype(BF16)
    return hi, mid, (rest - mid.astype(F32)).astype(BF16)


def dot(a, b):
    return lax.dot_general(a, b, (((1,), (0,)), ((), ())), preferred_element_type=F32)


def dot_t(a, b):
    return lax.dot_general(a, b, (((1,), (1,)), ((), ())), preferred_element_type=F32)


def step_kernel(
    state, spin, device, drow, dcol, weights, angle, out, worst,
    ext, rowsend, rowrecv, colsend, colrecv, p1send, p1recv, p2send, p2recv, summed, spread, spinx,
    lhs_ref, pick_ref, halo_ss, halo_rs, p1_ss, p1_rs, p2_ss, p2_rs, ready,
):
    panel, colat, lon = (lax.axis_index(a) for a in ("panel", "colat", "lon"))
    plane, y_lo = lon // 2, lon % 2
    hub = colat * 2 + y_lo
    other = 1 - panel

    barrier = pltpu.get_barrier_semaphore()

    def greet(**where):
        pl.semaphore_signal(barrier, inc=1, device_id=where, device_id_type=MESH)

    def peer(h):
        return dict(colat=h // 2, lon=plane * 2 + h % 2)

    @pl.loop(1, 32)
    def _(f):
        t = (panel * 16 + hub + f) % 32
        h = t % 16
        greet(panel=t // 16, colat=h // 2, lon=plane * 2 + h % 2)

    @pl.loop(1, 8)
    def _(f):
        greet(lon=((plane + f) % 8) * 2 + y_lo)

    north, south = (colat + 7) % 8, (colat + 1) % 8
    west, east = (lon + 15) % 16, (lon + 1) % 16
    greet(lon=west)
    greet(lon=east)

    lane = iota((1, LANES), 1)
    group = lane // 32
    shell = lane % 32

    def pack_halo(ref, base, rnd):
        for side, row in ((0, 0), (1, ROWS - 1)):
            for f in range(7):
                rowsend[rnd, side, f : f + 1, :] = ref[f, row : row + 1, base : base + WIDTH]
            rowsend[rnd, side, 7:8, :] = jnp.zeros((1, WIDTH), F32)
        for side, tile, have in ((0, base, 0), (1, base + WIDTH - LANES, 3)):
            for half, fields in ((0, range(4)), (1, range(4, 7))):
                total = jnp.zeros((ROWS, LANES), F32)
                for f in fields:
                    moved = pltpu.roll(ref[f, :, tile : tile + LANES], 32 * ((f % 4 - have) % 4), 1)
                    total = jnp.where(group == f % 4, moved, total)
                colsend[rnd, side, half] = total

    def halo_copies(rnd):
        def copy(src, dst, i, **where):
            return pltpu.make_async_remote_copy(
                src_ref=src, dst_ref=dst, send_sem=halo_ss.at[rnd, i], recv_sem=halo_rs.at[rnd, i],
                device_id=where, device_id_type=MESH,
            )

        return [
            copy(rowsend.at[rnd, 0], rowrecv.at[rnd, 1], 0, colat=north),
            copy(rowsend.at[rnd, 1], rowrecv.at[rnd, 0], 1, colat=south),
            copy(colsend.at[rnd, 0], colrecv.at[rnd, 1], 2, lon=west),
            copy(colsend.at[rnd, 1], colrecv.at[rnd, 0], 3, lon=east),
        ]

    pack_halo(state, 0, 0)
    pl.semaphore_wait(barrier, 31 + 7 + 2)
    halos0 = halo_copies(0)
    for copy in halos0:
        copy.start()

    @pl.loop(1, 8)
    def _(f):
        pl.semaphore_signal(
            ready, inc=1, device_id=dict(lon=((plane + f) % 8) * 2 + y_lo), device_id_type=MESH
        )

    grow = (device[0:1, :] // 16) * ROWS + drow[0:1, :]
    gcol = (device[0:1, :] % 16) * COLS + dcol[0:1, :]
    along_row = weights[1:2, :] + weights[3:4, :]
    along_row0 = weights[0:1, :] + weights[2:3, :]
    along_col = weights[2:3, :] + weights[3:4, :]
    along_col0 = weights[0:1, :] + weights[1:2, :]

    def held(rr, cc):
        return (rr >= -1) & (rr < ROWS) & (cc >= -1) & (cc < COLS)

    rr, cc = grow - colat * ROWS, gcol - lon * COLS
    mine_row = jnp.where(held(rr, cc), 1.0, 0.0)
    mine = jnp.concatenate([mine_row[:, t * LANES : (t + 1) * LANES] for t in range(12)], axis=0)
    mine = jnp.concatenate([mine, jnp.zeros((4, LANES), F32)], axis=0).astype(BF16)
    up, down = iota((LANES, LANES), 0), iota((LANES, LANES), 1)
    same = up % HUBS == down % HUBS
    before = dot(mine, flag01(same & (up < down)))
    whole = dot(mine, flag01(same)).astype(BF16)
    earlier = dot(flag01(iota((16, 16), 0) > iota((16, 16), 1)), whole)
    rank = before + earlier
    rank_row = jnp.concatenate([rank[t : t + 1, :] for t in range(12)], axis=1)
    point = iota((1, POINTS), 1)
    slot = jnp.where(
        (mine_row > 0.0) & (rank_row < SLOTS),
        (point % HUBS) * SLOTS + rank_row.astype(I32),
        -1,
    )
    slot_row = iota((LANES, 1), 0)
    chosen = flag01(slot == (slot_row // 8) * SLOTS + slot_row % SLOTS)
    cell = iota((ROWS, 1), 0)
    row_w = jnp.where(cell == rr, along_row0, 0.0) + jnp.where(cell == rr + 1, along_row, 0.0)
    col_w = jnp.where(cell == cc, along_col0, 0.0) + jnp.where(cell == cc + 1, along_col, 0.0)
    row_hi, row_lo = split2(row_w)
    col_hi, col_lo = split2(col_w)
    lhs_ref[...] = dot_t(chosen, jnp.concatenate([row_hi, row_lo, row_hi, row_hi * 0], axis=0)).astype(BF16)
    cols = dot_t(chosen, jnp.concatenate([col_hi, col_lo, col_lo * 0, col_lo * 0], axis=0)).astype(BF16)
    cell4 = iota((LANES, WIDTH), 0)
    expand = flag01((cell4 % 32 == iota((LANES, WIDTH), 1) // 32))
    spread[...] = dot(cols, expand)
    spin_parts = jnp.concatenate(list(split3(spin[0])) + [jnp.zeros((ROWS, COLS), BF16)], axis=1)
    spinx[...] = dot(spin_parts, expand)

    out_row = iota((192, 1), 0)
    my_lane = ((out_row // 2) % 8) * HUBS + hub

    def column(values):
        tall = jnp.concatenate(
            [jnp.broadcast_to(values[:, t * LANES : (t + 1) * LANES], (16, LANES)) for t in range(12)], axis=0
        )
        return jnp.sum(jnp.where(lane == my_lane, tall, 0), axis=1, keepdims=True)

    source = lane // 8
    s_rr = column(grow) - (source // 2) * ROWS
    s_cc = column(gcol) - (plane * 2 + source % 2) * COLS
    has = held(s_rr, s_cc)
    count_row, count_col = iota((192, 192), 0), iota((192, 192), 1)
    seen = dot(flag01((count_col // 2 < count_row // 2) & (count_col % 2 == 0)), flag01(has))
    take = has & (seen.astype(I32) == lane % SLOTS) & (out_row % 2 == (lane % 8) // SLOTS)
    pick_ref[...] = flag01(take)

    every = iota((LANES, 1), 0)
    counts = dot_t(
        flag01(held(grow - (every // 16) * ROWS, gcol - (every % 16) * COLS)),
        flag01(iota((LANES, 1), 0) == point % HUBS),
    )
    worst[...] = jnp.broadcast_to(jnp.max(counts), (8, LANES))

    row_id = iota((ROWS, 1), 0)
    inv_radius = 1.0 / (1.0 + 0.25 * (shell.astype(F32) + 0.5) / 32)
    theta = jnp.pi / 4 + ((colat * ROWS + row_id).astype(F32) + 0.5) * (jnp.pi / 512.0)
    metric_p = inv_radius / jnp.sin(theta)

    def rate(rnd, base_ref, base_off, dst, dst_off, dt):
        mt, mp = inv_radius, metric_p
        mt2, mp2 = mt * mt, mp * mp
        centre = 2.0 * (mt2 + mp2 + 1.0)
        half_t, half_p = (0.5 * dt) * mt, (0.5 * dt) * mp

        @pl.loop(0, 8)
        def _(t):
            off = pl.multiple_of(t * LANES, LANES)

            def tile(f, k):
                return ext[rnd, f, :, pl.ds(pl.multiple_of(off + k * LANES, LANES), LANES)]

            ut, up_, ur, temp, bt, bp, br = (tile(f, 1) for f in range(7))
            fields = (ut, up_, ur, temp, bt, bp, br)
            at, ap, ar = ut * half_t, up_ * half_p, ur * (0.5 * dt)
            st, sp, sr = bt * half_t, bp * half_p, br * (0.5 * dt)
            spin_dt = spinx[:, pl.ds(off, LANES)] * dt
            base, stretch = [], []
            for f, c in enumerate(fields):
                up_row = rowrecv[rnd, 0, f : f + 1, pl.ds(off, LANES)] * jnp.where(colat > 0, 1.0, 0.0)
                down_row = rowrecv[rnd, 1, f : f + 1, pl.ds(off, LANES)] * jnp.where(colat < 7, 1.0, 0.0)
                n = jnp.where(row_id == 0, up_row, pltpu.roll(c, 1, 0))
                s = jnp.where(row_id == ROWS - 1, down_row, pltpu.roll(c, ROWS - 1, 0))
                w = pltpu.roll(jnp.where(group == 3, tile(f, 0), c), 32, 1)
                e = pltpu.roll(jnp.where(group == 0, tile(f, 2), c), 96, 1)
                u = jnp.where(shell == 31, c, pltpu.roll(c, 127, 1))
                d = jnp.where(shell == 0, c, pltpu.roll(c, 1, 1))
                laplace = mt2 * (s + n) + mp2 * (e + w) + (u + d) - centre * c
                sn, ew, ud = s - n, e - w, u - d
                base.append((DIFFUSE[f] * dt) * laplace - (at * sn + ap * ew + ar * ud))
                stretch.append(st * sn + sp * ew + sr * ud if f != 3 else None)
            add = [
                stretch[4] + spin_dt * up_,
                stretch[5] - spin_dt * ut,
                stretch[6] + dt * temp,
                None,
                stretch[0],
                stretch[1],
                stretch[2],
            ]
            for f in range(7):
                value = base_ref[f, :, pl.ds(pl.multiple_of(base_off + off, LANES), LANES)] + base[f]
                if add[f] is not None:
                    value = value + add[f]
                dst[f, :, pl.ds(pl.multiple_of(dst_off + off, LANES), LANES)] = value

    def unpack_halo(rnd):
        for side, tile, goal in ((0, 0, 3), (1, LANES + WIDTH, 0)):
            for f in range(7):
                have = colrecv[rnd, side, f // 4]
                inside = (lon > 0) if side == 0 else (lon < 15)
                ext[rnd, f, :, tile : tile + LANES] = pltpu.roll(
                    have, 32 * ((goal - f % 4) % 4), 1
                ) * jnp.where(inside, 1.0, 0.0)

    def send_points(ref, base, rnd):
        total = jnp.zeros((LANES, LANES), F32)
        lhs = lhs_ref[...][:, :96]
        row_half = (slot_row % 8) // SLOTS
        for f in range(7):
            hi, lo = split2(ref[f, :, base : base + WIDTH])
            rows = dot(lhs, jnp.concatenate([hi, hi, lo], axis=0))
            folded = jnp.zeros((LANES, LANES), F32)
            for t in range(8):
                folded += rows[:, t * LANES : (t + 1) * LANES] * spread[:, t * LANES : (t + 1) * LANES]
            folded += pltpu.roll(folded, 32, 1)
            folded += pltpu.roll(folded, 64, 1)
            total = jnp.where((group == f % 4) & (row_half == f // 4), folded, total)
        p1send[rnd] = total.reshape(HUBS, 8, LANES)
        p1recv[rnd, hub] = p1send[rnd, hub]

        @pl.loop(1, HUBS)
        def _(f):
            h = (hub + f) % HUBS
            pltpu.make_async_remote_copy(
                src_ref=p1send.at[rnd, h], dst_ref=p1recv.at[rnd, hub],
                send_sem=p1_ss.at[rnd], recv_sem=p1_rs.at[rnd],
                device_id=peer(h), device_id_type=MESH,
            ).start()

    def wait_bytes(ref, sem):
        pltpu.make_async_copy(ref, ref, sem).wait()

    def relay(rnd):
        wait_bytes(p1recv.at[rnd, pl.ds(0, HUBS - 1)], p1_rs.at[rnd])
        parts = jnp.concatenate(split3(p1recv[rnd].reshape(LANES, LANES)), axis=0)
        pick = pick_ref[...]
        picked = dot(jnp.concatenate([pick, pick, pick], axis=1), parts)
        for s in range(SEGMENTS):
            p2send[rnd, s] = picked[4 * s : 4 * s + 4, :]
        if rnd == 0:
            pl.semaphore_wait(ready, 7)

        def send(s, kind, to_colat, to_lon):
            pltpu.make_async_remote_copy(
                src_ref=p2send.at[rnd, s], dst_ref=p2recv.at[rnd, kind, plane * HUBS + hub],
                send_sem=p2_ss.at[rnd], recv_sem=p2_rs.at[rnd, kind],
                device_id=dict(panel=other, colat=to_colat, lon=to_lon), device_id_type=MESH,
            ).start()

        @pl.loop(0, 16)
        def _(i):
            send(i, 0, 0, i)
            send(16 + i, 1, 7, i)

        @pl.loop(0, 8)
        def _(i):
            send(32 + i, 2, i, 0)
            send(40 + i, 3, i, 15)

    edges = [
        (colat == 0, lon),
        (colat == 7, 16 + lon),
        (lon == 0, 32 + colat),
        (lon == 15, 40 + colat),
    ]

    def place(rnd, ref, base):
        line = iota((64, 1), 0)
        line_point = 16 * ((line // 2) % 2) + line // 4
        from_row = iota((64, 64), 0)
        from_col = iota((64, 64), 1)
        for kind, (here, segment) in enumerate(edges):

            @pl.when(here)
            def _():
                wait_bytes(p2recv.at[rnd, kind], p2_rs.at[rnd, kind])
                total = p2recv[rnd, kind, 0:HUBS]
                for z in range(1, 8):
                    total = total + p2recv[rnd, kind, z * HUBS : (z + 1) * HUBS]
                for h in range(HUBS):
                    summed[4 * h : 4 * h + 4, :] = total[h]
                x = summed[...]
                own = angle[:, pl.ds(pl.multiple_of((segment // 4) * LANES, LANES), LANES)]
                own = jnp.where(lane == (segment % 4) * 32 + line_point, own, 0.0)
                own = jnp.sum(own, axis=1, keepdims=True)
                cosine, sine = jnp.cos(own), jnp.sin(own)
                cosine = jnp.where(group < 2, cosine, 1.0)
                swap = jnp.where(group == 0, -pltpu.roll(x, 96, 1), pltpu.roll(x, 32, 1))
                x = cosine * x + jnp.where(group < 2, sine, 0.0) * swap
                part = from_row // 32
                at = from_row % 32
                j = at if kind >= 2 else 4 * (at % 8) + at // 8
                perm = flag01(from_col == 4 * (j % 16) + 2 * (j // 16) + part)
                x = dot(jnp.concatenate([perm, perm, perm], axis=1), jnp.concatenate(split3(x), axis=0))
                for f in range(7):
                    block = x[32 * (f // 4) : 32 * (f // 4) + 32]
                    if kind < 2:
                        row = 0 if kind == 0 else ROWS - 1
                        tiles = jnp.zeros((8, LANES), F32)
                        for g in range(4):
                            moved = pltpu.roll(block[8 * g : 8 * g + 8], 32 * ((g - f % 4) % 4), 1)
                            tiles = jnp.where(group == g, moved, tiles)
                        for t in range(8):
                            ref[f, row : row + 1, base + t * LANES : base + (t + 1) * LANES] = tiles[t : t + 1]
                    else:
                        goal, off = (0, base) if kind == 2 else (3, base + WIDTH - LANES)
                        moved = pltpu.roll(block, 32 * ((goal - f % 4) % 4), 1)
                        now = ref[f, :, off : off + LANES]
                        corner = ((row_id == 0) & (colat == 0)) | ((row_id == ROWS - 1) & (colat == 7))
                        blend = jnp.where(corner, 0.5 * (moved + now), moved)
                        ref[f, :, off : off + LANES] = jnp.where(group == goal, blend, now)

    for f in range(7):
        ext[0, f, :, LANES : LANES + WIDTH] = state[f]
    for copy in halos0:
        copy.wait_recv()
    unpack_halo(0)
    rate(0, state, 0, ext.at[1], LANES, 0.1)
    send_points(ext.at[1], LANES, 0)
    pack_halo(ext.at[1], LANES, 1)
    halos1 = halo_copies(1)
    for copy in halos1:
        copy.start()
    relay(0)
    for copy in halos1:
        copy.wait_recv()
    unpack_halo(1)
    place(0, ext.at[1], LANES)
    rate(1, state, 0, out, 0, 0.2)
    send_points(out, 0, 1)
    relay(1)
    place(1, out, 0)
    for copy in halos0 + halos1:
        copy.wait_send()
    for rnd in range(2):
        wait_bytes(p1send.at[rnd, pl.ds(0, HUBS - 1)], p1_ss.at[rnd])
        wait_bytes(p2send.at[rnd], p2_ss.at[rnd])


def fast_step(state, spin, device, drow, dcol, weights, angle):
    vmem = pl.BlockSpec(memory_space=pltpu.VMEM)
    scratch = lambda *shape: pltpu.VMEM(shape, F32)
    return pl.pallas_call(
        step_kernel,
        out_shape=(
            jax.ShapeDtypeStruct((7, ROWS, WIDTH), F32),
            jax.ShapeDtypeStruct((8, LANES), F32),
        ),
        in_specs=[vmem] * 7,
        out_specs=(vmem, vmem),
        scratch_shapes=[
            scratch(2, 7, ROWS, WIDTH + 2 * LANES),
            scratch(2, 2, 8, WIDTH),
            scratch(2, 2, 8, WIDTH),
            scratch(2, 2, 2, ROWS, LANES),
            scratch(2, 2, 2, ROWS, LANES),
            scratch(2, HUBS, 8, LANES),
            scratch(2, HUBS, 8, LANES),
            scratch(2, SEGMENTS, 4, LANES),
            scratch(2, 4, 8 * HUBS, 4, LANES),
            scratch(64, LANES),
            scratch(LANES, WIDTH),
            scratch(ROWS, WIDTH),
            pltpu.VMEM((LANES, LANES), BF16),
            pltpu.VMEM((192, LANES), BF16),
            pltpu.SemaphoreType.DMA((2, 4)),
            pltpu.SemaphoreType.DMA((2, 4)),
            pltpu.SemaphoreType.DMA((2,)),
            pltpu.SemaphoreType.DMA((2,)),
            pltpu.SemaphoreType.DMA((2,)),
            pltpu.SemaphoreType.DMA((2, 4)),
            pltpu.SemaphoreType.REGULAR,
        ],
        compiler_params=pltpu.CompilerParams(
            collective_id=0, has_side_effects=True, vmem_limit_bytes=48 * 2**20
        ),
        name="dynamo_step",
    )(state, spin, device, drow, dcol, weights, angle)


FIELDS = 7
NR = 32


viscosity = 0.3
conduction = 0.4
resistance = 0.5
buoyancy = 1.0
timestep = 0.2


def with_halo(block, sides, width):
    for axis, dim in sides:
        count = lax.axis_size(axis)
        forward = [(i, i + 1) for i in range(count - 1)]
        backward = [(target, source) for source, target in forward]
        low = lax.ppermute(
            lax.slice_in_dim(block, block.shape[dim] - width, None, axis=dim), axis, forward
        )
        high = lax.ppermute(lax.slice_in_dim(block, 0, width, axis=dim), axis, backward)
        block = jnp.concatenate([low, block, high], axis=dim)
    return block


def partner(value, axis, distance):
    mask = 2**distance
    pairs = [(source, source ^ mask) for source in range(lax.axis_size(axis))]
    return lax.ppermute(value, axis, pairs)


def field_rates(
    fields,
    north_cells,
    south_cells,
    west_cells,
    east_cells,
    upper_cells,
    lower_cells,
    metric_t,
    metric_p,
    spin_cells,
):
    colat_slope = metric_t * (0.5 * (south_cells - north_cells))
    lon_slope = metric_p * (0.5 * (east_cells - west_cells))
    radial_slope = 0.5 * (upper_cells - lower_cells)
    laplace = (
        metric_t * metric_t * (south_cells + north_cells - 2.0 * fields)
        + metric_p * metric_p * (east_cells + west_cells - 2.0 * fields)
        + (upper_cells + lower_cells - 2.0 * fields)
    )
    advected = fields[0] * colat_slope + fields[1] * lon_slope + fields[2] * radial_slope
    stretched = fields[4] * colat_slope + fields[5] * lon_slope + fields[6] * radial_slope
    diffuse_rate = jnp.array(
        [viscosity, viscosity, viscosity, conduction, resistance, resistance, resistance],
        jnp.float32,
    )
    diffuse_rate = diffuse_rate.reshape((7,) + (1,) * (fields.ndim - 1))
    base_rate = diffuse_rate * laplace - advected
    return jnp.stack(
        [
            base_rate[0] + stretched[4] + spin_cells * fields[1],
            base_rate[1] + stretched[5] - spin_cells * fields[0],
            base_rate[2] + stretched[6] + buoyancy * fields[3],
            base_rate[3],
            base_rate[4] + stretched[0],
            base_rate[5] + stretched[1],
            base_rate[6] + stretched[2],
        ]
    )


def slot_map(colat_block, lon_block, lat_rows, lon_cells, n_colat, n_lon):
    slot_count = 2 * (lat_rows + lon_cells)
    lat_total = lat_rows * n_colat
    lon_total = lon_cells * n_lon
    slot_ids = jnp.arange(slot_count, dtype=jnp.int32)[None, :]
    colat_block = colat_block[:, None]
    lon_block = lon_block[:, None]
    is_top = slot_ids < lon_cells
    is_bottom = (slot_ids >= lon_cells) & (slot_ids < 2 * lon_cells)
    is_left = (slot_ids >= 2 * lon_cells) & (slot_ids < 2 * lon_cells + lat_rows)
    along_lon = lon_block * lon_cells + slot_ids
    along_lat = colat_block * lat_rows + slot_ids - 2 * lon_cells
    index_map = jnp.where(
        is_top,
        along_lon,
        jnp.where(
            is_bottom,
            lon_total + along_lon - lon_cells,
            jnp.where(
                is_left, 2 * lon_total + along_lat, 2 * lon_total + lat_total + along_lat - lat_rows
            ),
        ),
    )
    return index_map


def general_step(state, spin, donor_device, donor_row, donor_col, corner_weights, border_angle):
    fields = state[0]
    lat_rows = fields.shape[1]
    width = fields.shape[2]
    lon_cells = width // NR
    n_colat = lax.axis_size("colat")
    n_lon = lax.axis_size("lon")
    colat_block = lax.axis_index("colat")
    lon_block = lax.axis_index("lon")
    shell_index = jnp.arange(width, dtype=jnp.int32) % NR
    shell_float = shell_index.astype(jnp.float32)
    inv_radius = 1.0 / (1.0 + 0.25 * (shell_float + 0.5) / NR)
    row_number = (colat_block * lat_rows + jnp.arange(lat_rows, dtype=jnp.int32)).astype(
        jnp.float32
    )
    colat_angle = jnp.pi / 4 + (row_number + 0.5) * (jnp.pi / (2.0 * (lat_rows * n_colat)))
    metric_p = inv_radius[None, :] / jnp.sin(colat_angle)[:, None]
    spin_cells = jnp.repeat(spin[0], NR, axis=1)
    own_slots = slot_map(
        jnp.reshape(colat_block, (1,)),
        jnp.reshape(lon_block, (1,)),
        lat_rows,
        lon_cells,
        n_colat,
        n_lon,
    )[0]
    slot_angle = jnp.take(border_angle, own_slots)
    cosine = jnp.cos(slot_angle)
    sine_part = jnp.sin(slot_angle)
    cell_index = donor_row * lon_cells + donor_col
    is_mine = donor_device == colat_block * n_lon + lon_block
    per_device = FIELDS * NR

    def tendency(current):
        colat_ext = with_halo(current, (("colat", 1),), 1)
        lon_ext = with_halo(current, (("lon", 2),), NR)
        north_cells = colat_ext[:, :-2]
        south_cells = colat_ext[:, 2:]
        west_cells = lon_ext[:, :, : -2 * NR]
        east_cells = lon_ext[:, :, 2 * NR :]
        upper_cells = jnp.where(
            shell_index == NR - 1,
            current,
            jnp.concatenate([current[..., 1:], current[..., -1:]], axis=-1),
        )
        lower_cells = jnp.where(
            shell_index == 0,
            current,
            jnp.concatenate([current[..., :1], current[..., :-1]], axis=-1),
        )
        return field_rates(
            current,
            north_cells,
            south_cells,
            west_cells,
            east_cells,
            upper_cells,
            lower_cells,
            inv_radius,
            metric_p,
            spin_cells,
        )

    def border_terms_of(source):
        flat_block = (
            source.reshape(FIELDS, lat_rows, lon_cells, NR)
            .transpose(0, 3, 1, 2)
            .reshape(per_device, lat_rows * lon_cells)
        )
        summed = jnp.zeros((per_device, donor_row.shape[1]), jnp.float32)
        for corner in range(4):
            weight = jnp.where(is_mine[corner], corner_weights[corner], 0.0)
            summed = summed + jnp.take(flat_block, cell_index[corner], axis=1) * weight[None, :]
        return summed

    def rotate(picked):
        return jnp.stack(
            [
                cosine * picked[0] - sine_part * picked[1],
                sine_part * picked[0] + cosine * picked[1],
                picked[2],
                picked[3],
                cosine * picked[4] - sine_part * picked[5],
                sine_part * picked[4] + cosine * picked[5],
                picked[6],
            ]
        )

    def place_border(target, turned):
        top_row = turned[:, :, 0:lon_cells].transpose(0, 2, 1).reshape(FIELDS, width)
        bottom_row = (
            turned[:, :, lon_cells : 2 * lon_cells].transpose(0, 2, 1).reshape(FIELDS, width)
        )
        left_col = turned[:, :, 2 * lon_cells : 2 * lon_cells + lat_rows].transpose(0, 2, 1)
        right_col = turned[:, :, 2 * lon_cells + lat_rows :].transpose(0, 2, 1)
        target = target.at[:, 0, :].set(jnp.where(colat_block == 0, top_row, target[:, 0, :]))
        target = target.at[:, lat_rows - 1, :].set(
            jnp.where(colat_block == n_colat - 1, bottom_row, target[:, lat_rows - 1, :])
        )
        row_ids = jnp.arange(lat_rows)
        edge_row = (row_ids == 0) & (colat_block == 0) | (row_ids == lat_rows - 1) & (
            colat_block == n_colat - 1
        )
        current = target[:, :, 0:NR]
        blended = jnp.where(edge_row[None, :, None], 0.5 * (left_col + current), left_col)
        target = target.at[:, :, 0:NR].set(jnp.where(lon_block == 0, blended, current))
        current = target[:, :, width - NR :]
        blended = jnp.where(edge_row[None, :, None], 0.5 * (right_col + current), right_col)
        target = target.at[:, :, width - NR :].set(
            jnp.where(lon_block == n_lon - 1, blended, current)
        )
        return target

    def overset(target):
        source = partner(target, "panel", 0)
        summed_all = lax.psum(border_terms_of(source), ("colat", "lon"))
        picked = jnp.take(summed_all, own_slots, axis=1)
        turned = rotate(picked.reshape(FIELDS, NR, -1))
        return place_border(target, turned)

    tendency_now = tendency(fields)
    middle = overset(fields + 0.5 * timestep * tendency_now)
    tendency_now = tendency(middle)
    advanced = overset(fields + timestep * tendency_now)
    return advanced[None]


def on_device(state, spin, donor_device, donor_row, donor_col, corner_weights, border_angle):
    fast, worst = fast_step(
        state[0], spin, donor_device, donor_row, donor_col, corner_weights, border_angle[None]
    )
    return lax.cond(
        worst[0, 0] > SLOTS,
        lambda: general_step(
            state, spin, donor_device, donor_row, donor_col, corner_weights, border_angle
        ),
        lambda: fast[None],
    )


def solution(mesh):
    placed = (P("panel", None, "colat", "lon"), P("panel", "colat", "lon"), P(), P(), P(), P(), P())
    return jax.shard_map(
        on_device,
        mesh=mesh,
        in_specs=placed,
        out_specs=P("panel", None, "colat", "lon"),
        check_vma=False,
    )
```

```python
import functools

import jax
import jax.numpy as jnp
from jax import lax
from jax.experimental import pallas as pl
from jax.experimental.pallas import tpu as pltpu
from jax.sharding import PartitionSpec as P

MESH = pl.DeviceIdType.MESH
F32, BF16, I32 = jnp.float32, jnp.bfloat16, jnp.int32
ROWS, COLS, WIDTH, LANES = 32, 32, 1024, 128
POINTS, HUBS, SLOTS, SEGMENTS = 1536, 16, 4, 48
DIFFUSE = (0.3, 0.3, 0.3, 0.4, 0.5, 0.5, 0.5)


def iota(shape, dim):
    return lax.broadcasted_iota(I32, shape, dim)


def flag01(cond):
    return jnp.where(cond, 1.0, 0.0).astype(BF16)


def split2(x):
    hi = x.astype(BF16)
    return hi, (x - hi.astype(F32)).astype(BF16)


def split3(x):
    hi, rest = x.astype(BF16), None
    rest = x - hi.astype(F32)
    mid = rest.astype(BF16)
    return hi, mid, (rest - mid.astype(F32)).astype(BF16)


def dot(a, b):
    return lax.dot_general(a, b, (((1,), (0,)), ((), ())), preferred_element_type=F32)


def dot_t(a, b):
    return lax.dot_general(a, b, (((1,), (1,)), ((), ())), preferred_element_type=F32)


def step_kernel(
    rounds,
    state, spin, device, drow, dcol, weights, angle, out, worst,
    ext, rowsend, rowrecv, colsend, colrecv, p1send, p1recv, p2send, p2recv, summed, spread, spinx,
    lhs_ref, pick_ref, hub_sum, halo_ss, halo_rs, p1_ss, p1_rs, p2_ss, p2_rs, ready,
):
    panel, colat, lon = (lax.axis_index(a) for a in ("panel", "colat", "lon"))
    plane, y_lo = lon // 2, lon % 2
    hub = colat * 2 + y_lo
    other = 1 - panel

    barrier = pltpu.get_barrier_semaphore()

    def greet(**where):
        pl.semaphore_signal(barrier, inc=1, device_id=where, device_id_type=MESH)

    def peer(h):
        return dict(colat=h // 2, lon=plane * 2 + h % 2)

    @pl.loop(1, 32)
    def _(f):
        t = (panel * 16 + hub + f) % 32
        h = t % 16
        greet(panel=t // 16, colat=h // 2, lon=plane * 2 + h % 2)

    @pl.loop(1, 8)
    def _(f):
        greet(lon=((plane + f) % 8) * 2 + y_lo)

    north, south = (colat + 7) % 8, (colat + 1) % 8
    west, east = (lon + 15) % 16, (lon + 1) % 16
    greet(lon=west)
    greet(lon=east)

    lane = iota((1, LANES), 1)
    group = lane // 32
    shell = lane % 32

    def pack_halo(ref, base, rnd):
        for side, row in ((0, 0), (1, ROWS - 1)):
            for f in range(7):
                rowsend[rnd, side, f : f + 1, :] = ref[f, row : row + 1, base : base + WIDTH]
            rowsend[rnd, side, 7:8, :] = jnp.zeros((1, WIDTH), F32)
        for side, tile, have in ((0, base, 0), (1, base + WIDTH - LANES, 3)):
            for half, fields in ((0, range(4)), (1, range(4, 7))):
                total = jnp.zeros((ROWS, LANES), F32)
                for f in fields:
                    moved = pltpu.roll(ref[f, :, tile : tile + LANES], 32 * ((f % 4 - have) % 4), 1)
                    total = jnp.where(group == f % 4, moved, total)
                colsend[rnd, side, half] = total

    def halo_copies(rnd):
        def copy(src, dst, i, **where):
            return pltpu.make_async_remote_copy(
                src_ref=src, dst_ref=dst, send_sem=halo_ss.at[rnd, i], recv_sem=halo_rs.at[rnd, i],
                device_id=where, device_id_type=MESH,
            )

        return [
            copy(rowsend.at[rnd, 0], rowrecv.at[rnd, 1], 0, colat=north),
            copy(rowsend.at[rnd, 1], rowrecv.at[rnd, 0], 1, colat=south),
            copy(colsend.at[rnd, 0], colrecv.at[rnd, 1], 2, lon=west),
            copy(colsend.at[rnd, 1], colrecv.at[rnd, 0], 3, lon=east),
        ]

    pack_halo(state, 0, 0)
    pl.semaphore_wait(barrier, 31 + 7 + 2)
    halos0 = halo_copies(0)
    for copy in halos0:
        copy.start()

    @pl.loop(1, 8)
    def _(f):
        pl.semaphore_signal(
            ready, inc=1, device_id=dict(lon=((plane + f) % 8) * 2 + y_lo), device_id_type=MESH
        )

    grow = (device[0:1, :] // 16) * ROWS + drow[0:1, :]
    gcol = (device[0:1, :] % 16) * COLS + dcol[0:1, :]
    along_row = weights[1:2, :] + weights[3:4, :]
    along_row0 = weights[0:1, :] + weights[2:3, :]
    along_col = weights[2:3, :] + weights[3:4, :]
    along_col0 = weights[0:1, :] + weights[1:2, :]

    def held(rr, cc):
        return (rr >= -1) & (rr < ROWS) & (cc >= -1) & (cc < COLS)

    rr, cc = grow - colat * ROWS, gcol - lon * COLS
    mine_row = jnp.where(held(rr, cc), 1.0, 0.0)
    mine = jnp.concatenate([mine_row[:, t * LANES : (t + 1) * LANES] for t in range(12)], axis=0)
    mine = jnp.concatenate([mine, jnp.zeros((4, LANES), F32)], axis=0).astype(BF16)
    up, down = iota((LANES, LANES), 0), iota((LANES, LANES), 1)
    same = up % HUBS == down % HUBS
    before = dot(mine, flag01(same & (up < down)))
    whole = dot(mine, flag01(same)).astype(BF16)
    earlier = dot(flag01(iota((16, 16), 0) > iota((16, 16), 1)), whole)
    rank = before + earlier
    rank_row = jnp.concatenate([rank[t : t + 1, :] for t in range(12)], axis=1)
    point = iota((1, POINTS), 1)
    slot_row = iota((LANES, 1), 0)
    cell = iota((ROWS, 1), 0)
    row_w = jnp.where(cell == rr, along_row0, 0.0) + jnp.where(cell == rr + 1, along_row, 0.0)
    col_w = jnp.where(cell == cc, along_col0, 0.0) + jnp.where(cell == cc + 1, along_col, 0.0)
    row_hi, row_lo = split2(row_w)
    col_hi, col_lo = split2(col_w)
    row_parts = jnp.concatenate([row_hi, row_lo, row_hi, row_hi * 0], axis=0)
    col_parts = jnp.concatenate([col_hi, col_lo, col_lo * 0, col_lo * 0], axis=0)
    cell4 = iota((LANES, WIDTH), 0)
    expand = flag01((cell4 % 32 == iota((LANES, WIDTH), 1) // 32))

    def fill_slots(turn):
        order = rank_row.astype(I32) - turn * SLOTS
        slot = jnp.where(
            (mine_row > 0.0) & (order >= 0) & (order < SLOTS), (point % HUBS) * SLOTS + order, -1
        )
        chosen = flag01(slot == (slot_row // 8) * SLOTS + slot_row % SLOTS)
        lhs_ref[...] = dot_t(chosen, row_parts).astype(BF16)
        spread[...] = dot(dot_t(chosen, col_parts).astype(BF16), expand)

    spin_parts = jnp.concatenate(list(split3(spin[0])) + [jnp.zeros((ROWS, COLS), BF16)], axis=1)
    spinx[...] = dot(spin_parts, expand)

    out_row = iota((192, 1), 0)
    my_lane = ((out_row // 2) % 8) * HUBS + hub

    def column(values):
        tall = jnp.concatenate(
            [jnp.broadcast_to(values[:, t * LANES : (t + 1) * LANES], (16, LANES)) for t in range(12)], axis=0
        )
        return jnp.sum(jnp.where(lane == my_lane, tall, 0), axis=1, keepdims=True)

    source = lane // 8
    s_rr = column(grow) - (source // 2) * ROWS
    s_cc = column(gcol) - (plane * 2 + source % 2) * COLS
    has = held(s_rr, s_cc)
    count_row, count_col = iota((192, 192), 0), iota((192, 192), 1)
    seen = dot(flag01((count_col // 2 < count_row // 2) & (count_col % 2 == 0)), flag01(has))

    def fill_picks(turn):
        slot = seen.astype(I32) - turn * SLOTS
        take = has & (slot == lane % SLOTS) & (out_row % 2 == (lane % 8) // SLOTS)
        pick_ref[...] = flag01(take)

    if rounds == 1:
        fill_slots(0)
        fill_picks(0)

    every = iota((LANES, 1), 0)
    counts = dot_t(
        flag01(held(grow - (every // 16) * ROWS, gcol - (every % 16) * COLS)),
        flag01(iota((LANES, 1), 0) == point % HUBS),
    )
    worst[...] = jnp.broadcast_to(jnp.max(counts), (8, LANES))

    row_id = iota((ROWS, 1), 0)
    inv_radius = 1.0 / (1.0 + 0.25 * (shell.astype(F32) + 0.5) / 32)
    theta = jnp.pi / 4 + ((colat * ROWS + row_id).astype(F32) + 0.5) * (jnp.pi / 512.0)
    metric_p = inv_radius / jnp.sin(theta)

    def rate(rnd, base_ref, base_off, dst, dst_off, dt):
        mt, mp = inv_radius, metric_p
        mt2, mp2 = mt * mt, mp * mp
        centre = 2.0 * (mt2 + mp2 + 1.0)
        half_t, half_p = (0.5 * dt) * mt, (0.5 * dt) * mp

        @pl.loop(0, 8)
        def _(t):
            off = pl.multiple_of(t * LANES, LANES)

            def tile(f, k):
                return ext[rnd, f, :, pl.ds(pl.multiple_of(off + k * LANES, LANES), LANES)]

            ut, up_, ur, temp, bt, bp, br = (tile(f, 1) for f in range(7))
            fields = (ut, up_, ur, temp, bt, bp, br)
            at, ap, ar = ut * half_t, up_ * half_p, ur * (0.5 * dt)
            st, sp, sr = bt * half_t, bp * half_p, br * (0.5 * dt)
            spin_dt = spinx[:, pl.ds(off, LANES)] * dt
            base, stretch = [], []
            for f, c in enumerate(fields):
                up_row = rowrecv[rnd, 0, f : f + 1, pl.ds(off, LANES)] * jnp.where(colat > 0, 1.0, 0.0)
                down_row = rowrecv[rnd, 1, f : f + 1, pl.ds(off, LANES)] * jnp.where(colat < 7, 1.0, 0.0)
                n = jnp.where(row_id == 0, up_row, pltpu.roll(c, 1, 0))
                s = jnp.where(row_id == ROWS - 1, down_row, pltpu.roll(c, ROWS - 1, 0))
                w = pltpu.roll(jnp.where(group == 3, tile(f, 0), c), 32, 1)
                e = pltpu.roll(jnp.where(group == 0, tile(f, 2), c), 96, 1)
                u = jnp.where(shell == 31, c, pltpu.roll(c, 127, 1))
                d = jnp.where(shell == 0, c, pltpu.roll(c, 1, 1))
                laplace = mt2 * (s + n) + mp2 * (e + w) + (u + d) - centre * c
                sn, ew, ud = s - n, e - w, u - d
                base.append((DIFFUSE[f] * dt) * laplace - (at * sn + ap * ew + ar * ud))
                stretch.append(st * sn + sp * ew + sr * ud if f != 3 else None)
            add = [
                stretch[4] + spin_dt * up_,
                stretch[5] - spin_dt * ut,
                stretch[6] + dt * temp,
                None,
                stretch[0],
                stretch[1],
                stretch[2],
            ]
            for f in range(7):
                value = base_ref[f, :, pl.ds(pl.multiple_of(base_off + off, LANES), LANES)] + base[f]
                if add[f] is not None:
                    value = value + add[f]
                dst[f, :, pl.ds(pl.multiple_of(dst_off + off, LANES), LANES)] = value

    def unpack_halo(rnd):
        for side, tile, goal in ((0, 0, 3), (1, LANES + WIDTH, 0)):
            for f in range(7):
                have = colrecv[rnd, side, f // 4]
                inside = (lon > 0) if side == 0 else (lon < 15)
                ext[rnd, f, :, tile : tile + LANES] = pltpu.roll(
                    have, 32 * ((goal - f % 4) % 4), 1
                ) * jnp.where(inside, 1.0, 0.0)

    def send_points(ref, base, rnd):
        row_half = (slot_row % 8) // SLOTS

        def turn_points(turn):
            total = jnp.zeros((LANES, LANES), F32)
            lhs = lhs_ref[...][:, :96]
            for f in range(7):
                hi, lo = split2(ref[f, :, base : base + WIDTH])
                rows = dot(lhs, jnp.concatenate([hi, hi, lo], axis=0))
                folded = jnp.zeros((LANES, LANES), F32)
                for t in range(8):
                    folded += rows[:, t * LANES : (t + 1) * LANES] * spread[:, t * LANES : (t + 1) * LANES]
                folded += pltpu.roll(folded, 32, 1)
                folded += pltpu.roll(folded, 64, 1)
                total = jnp.where((group == f % 4) & (row_half == f // 4), folded, total)
            p1send[rnd, turn] = total.reshape(HUBS, 8, LANES)
            p1recv[rnd, turn, hub] = p1send[rnd, turn, hub]

            @pl.loop(1, HUBS)
            def _(f):
                h = (hub + f) % HUBS
                pltpu.make_async_remote_copy(
                    src_ref=p1send.at[rnd, turn, h], dst_ref=p1recv.at[rnd, turn, hub],
                    send_sem=p1_ss.at[rnd, turn], recv_sem=p1_rs.at[rnd, turn],
                    device_id=peer(h), device_id_type=MESH,
                ).start()

        if rounds == 1:
            turn_points(0)
        else:

            @pl.loop(0, rounds)
            def _(turn):
                fill_slots(turn)
                turn_points(turn)

    def wait_bytes(ref, sem):
        pltpu.make_async_copy(ref, ref, sem).wait()

    def relay(rnd):
        def turn_sum(turn):
            wait_bytes(p1recv.at[rnd, turn, pl.ds(0, HUBS - 1)], p1_rs.at[rnd, turn])
            parts = jnp.concatenate(split3(p1recv[rnd, turn].reshape(LANES, LANES)), axis=0)
            pick = pick_ref[...]
            return dot(jnp.concatenate([pick, pick, pick], axis=1), parts)

        if rounds == 1:
            picked = turn_sum(0)
        else:
            hub_sum[...] = jnp.zeros_like(hub_sum)

            @pl.loop(0, rounds)
            def _(turn):
                fill_picks(turn)
                hub_sum[...] += turn_sum(turn)

            picked = hub_sum[...]
        for s in range(SEGMENTS):
            p2send[rnd, s] = picked[4 * s : 4 * s + 4, :]
        if rnd == 0:
            pl.semaphore_wait(ready, 7)

        def send(s, kind, to_colat, to_lon):
            pltpu.make_async_remote_copy(
                src_ref=p2send.at[rnd, s], dst_ref=p2recv.at[rnd, kind, plane * HUBS + hub],
                send_sem=p2_ss.at[rnd], recv_sem=p2_rs.at[rnd, kind],
                device_id=dict(panel=other, colat=to_colat, lon=to_lon), device_id_type=MESH,
            ).start()

        @pl.loop(0, 16)
        def _(i):
            send(i, 0, 0, i)
            send(16 + i, 1, 7, i)

        @pl.loop(0, 8)
        def _(i):
            send(32 + i, 2, i, 0)
            send(40 + i, 3, i, 15)

    edges = [
        (colat == 0, lon),
        (colat == 7, 16 + lon),
        (lon == 0, 32 + colat),
        (lon == 15, 40 + colat),
    ]

    def place(rnd, ref, base):
        line = iota((64, 1), 0)
        line_point = 16 * ((line // 2) % 2) + line // 4
        from_row = iota((64, 64), 0)
        from_col = iota((64, 64), 1)
        for kind, (here, segment) in enumerate(edges):

            @pl.when(here)
            def _():
                wait_bytes(p2recv.at[rnd, kind], p2_rs.at[rnd, kind])
                total = p2recv[rnd, kind, 0:HUBS]
                for z in range(1, 8):
                    total = total + p2recv[rnd, kind, z * HUBS : (z + 1) * HUBS]
                for h in range(HUBS):
                    summed[4 * h : 4 * h + 4, :] = total[h]
                x = summed[...]
                own = angle[:, pl.ds(pl.multiple_of((segment // 4) * LANES, LANES), LANES)]
                own = jnp.where(lane == (segment % 4) * 32 + line_point, own, 0.0)
                own = jnp.sum(own, axis=1, keepdims=True)
                cosine, sine = jnp.cos(own), jnp.sin(own)
                cosine = jnp.where(group < 2, cosine, 1.0)
                swap = jnp.where(group == 0, -pltpu.roll(x, 96, 1), pltpu.roll(x, 32, 1))
                x = cosine * x + jnp.where(group < 2, sine, 0.0) * swap
                part = from_row // 32
                at = from_row % 32
                j = at if kind >= 2 else 4 * (at % 8) + at // 8
                perm = flag01(from_col == 4 * (j % 16) + 2 * (j // 16) + part)
                x = dot(jnp.concatenate([perm, perm, perm], axis=1), jnp.concatenate(split3(x), axis=0))
                for f in range(7):
                    block = x[32 * (f // 4) : 32 * (f // 4) + 32]
                    if kind < 2:
                        row = 0 if kind == 0 else ROWS - 1
                        tiles = jnp.zeros((8, LANES), F32)
                        for g in range(4):
                            moved = pltpu.roll(block[8 * g : 8 * g + 8], 32 * ((g - f % 4) % 4), 1)
                            tiles = jnp.where(group == g, moved, tiles)
                        for t in range(8):
                            ref[f, row : row + 1, base + t * LANES : base + (t + 1) * LANES] = tiles[t : t + 1]
                    else:
                        goal, off = (0, base) if kind == 2 else (3, base + WIDTH - LANES)
                        moved = pltpu.roll(block, 32 * ((goal - f % 4) % 4), 1)
                        now = ref[f, :, off : off + LANES]
                        corner = ((row_id == 0) & (colat == 0)) | ((row_id == ROWS - 1) & (colat == 7))
                        blend = jnp.where(corner, 0.5 * (moved + now), moved)
                        ref[f, :, off : off + LANES] = jnp.where(group == goal, blend, now)

    for f in range(7):
        ext[0, f, :, LANES : LANES + WIDTH] = state[f]
    for copy in halos0:
        copy.wait_recv()
    unpack_halo(0)
    rate(0, state, 0, ext.at[1], LANES, 0.1)
    send_points(ext.at[1], LANES, 0)
    pack_halo(ext.at[1], LANES, 1)
    halos1 = halo_copies(1)
    for copy in halos1:
        copy.start()
    relay(0)
    for copy in halos1:
        copy.wait_recv()
    unpack_halo(1)
    place(0, ext.at[1], LANES)
    rate(1, state, 0, out, 0, 0.2)
    send_points(out, 0, 1)
    relay(1)
    place(1, out, 0)
    for copy in halos0 + halos1:
        copy.wait_send()
    for rnd in range(2):
        for turn in range(rounds):
            wait_bytes(p1send.at[rnd, turn, pl.ds(0, HUBS - 1)], p1_ss.at[rnd, turn])
        wait_bytes(p2send.at[rnd], p2_ss.at[rnd])


def step(rounds, state, spin, device, drow, dcol, weights, angle):
    vmem = pl.BlockSpec(memory_space=pltpu.VMEM)
    scratch = lambda *shape: pltpu.VMEM(shape, F32)
    return pl.pallas_call(
        functools.partial(step_kernel, rounds),
        out_shape=(
            jax.ShapeDtypeStruct((7, ROWS, WIDTH), F32),
            jax.ShapeDtypeStruct((8, LANES), F32),
        ),
        in_specs=[vmem] * 7,
        out_specs=(vmem, vmem),
        scratch_shapes=[
            scratch(2, 7, ROWS, WIDTH + 2 * LANES),
            scratch(2, 2, 8, WIDTH),
            scratch(2, 2, 8, WIDTH),
            scratch(2, 2, 2, ROWS, LANES),
            scratch(2, 2, 2, ROWS, LANES),
            scratch(2, rounds, HUBS, 8, LANES),
            scratch(2, rounds, HUBS, 8, LANES),
            scratch(2, SEGMENTS, 4, LANES),
            scratch(2, 4, 8 * HUBS, 4, LANES),
            scratch(64, LANES),
            scratch(LANES, WIDTH),
            scratch(ROWS, WIDTH),
            pltpu.VMEM((LANES, LANES), BF16),
            pltpu.VMEM((192, LANES), BF16),
            scratch(192, LANES),
            pltpu.SemaphoreType.DMA((2, 4)),
            pltpu.SemaphoreType.DMA((2, 4)),
            pltpu.SemaphoreType.DMA((2, rounds)),
            pltpu.SemaphoreType.DMA((2, rounds)),
            pltpu.SemaphoreType.DMA((2,)),
            pltpu.SemaphoreType.DMA((2, 4)),
            pltpu.SemaphoreType.REGULAR,
        ],
        compiler_params=pltpu.CompilerParams(
            collective_id=0 if rounds == 1 else 1, has_side_effects=True, vmem_limit_bytes=48 * 2**20
        ),
        name="dynamo_step" if rounds == 1 else "general_step",
    )(state, spin, device, drow, dcol, weights, angle)


def on_device(state, spin, donor_device, donor_row, donor_col, corner_weights, border_angle):
    args = (state[0], spin, donor_device, donor_row, donor_col, corner_weights, border_angle[None])
    fast, worst = step(1, *args)
    turns = POINTS // HUBS // SLOTS
    advanced = lax.cond(worst[0, 0] > SLOTS, lambda: step(turns, *args)[0], lambda: fast)
    return advanced[None]


def solution(mesh):
    placed = (P("panel", None, "colat", "lon"), P("panel", "colat", "lon"), P(), P(), P(), P(), P())
    return jax.shard_map(
        on_device,
        mesh=mesh,
        in_specs=placed,
        out_specs=P("panel", None, "colat", "lon"),
        check_vma=False,
    )
```

```python
import functools

import jax
import jax.numpy as jnp
from jax import lax
from jax.experimental import pallas as pl
from jax.experimental.pallas import tpu as pltpu
from jax.sharding import PartitionSpec as P

MESH = pl.DeviceIdType.MESH
F32, BF16, I32 = jnp.float32, jnp.bfloat16, jnp.int32
ROWS, COLS, WIDTH, LANES = 32, 32, 1024, 128
HELD = 64
POINTS, HUBS, SLOTS, SEGMENTS = 1536, 16, 4, 48
DIFFUSE = (0.3, 0.3, 0.3, 0.4, 0.5, 0.5, 0.5)


def iota(shape, dim):
    return lax.broadcasted_iota(I32, shape, dim)


def flag01(cond):
    return jnp.where(cond, 1.0, 0.0).astype(BF16)


def split2(x):
    hi = x.astype(BF16)
    return hi, (x - hi.astype(F32)).astype(BF16)


def split3(x):
    hi, rest = x.astype(BF16), None
    rest = x - hi.astype(F32)
    mid = rest.astype(BF16)
    return hi, mid, (rest - mid.astype(F32)).astype(BF16)


def dot(a, b):
    return lax.dot_general(a, b, (((1,), (0,)), ((), ())), preferred_element_type=F32)


def dot_t(a, b):
    return lax.dot_general(a, b, (((1,), (1,)), ((), ())), preferred_element_type=F32)


def step_kernel(
    rounds,
    state, spin, device, drow, dcol, weights, angle, out, overfull,
    ext, rowsend, rowrecv, colsend, colrecv, p1send, p1recv, p2send, p2recv, summed, spread, spinx,
    lhs_ref, pick_ref, hub_sum, halo_ss, halo_rs, p1_ss, p1_rs, p2_ss, p2_rs, ready,
):
    panel, colat, lon = (lax.axis_index(a) for a in ("panel", "colat", "lon"))
    plane, y_lo = lon // 2, lon % 2
    hub = colat * 2 + y_lo
    other = 1 - panel

    barrier = pltpu.get_barrier_semaphore()

    def greet(**where):
        pl.semaphore_signal(barrier, inc=1, device_id=where, device_id_type=MESH)

    def peer(h):
        return dict(colat=h // 2, lon=plane * 2 + h % 2)

    @pl.loop(1, 32)
    def _(f):
        t = (panel * 16 + hub + f) % 32
        h = t % 16
        greet(panel=t // 16, colat=h // 2, lon=plane * 2 + h % 2)

    @pl.loop(1, 8)
    def _(f):
        greet(lon=((plane + f) % 8) * 2 + y_lo)

    north, south = (colat + 7) % 8, (colat + 1) % 8
    west, east = (lon + 15) % 16, (lon + 1) % 16
    greet(lon=west)
    greet(lon=east)

    lane = iota((1, LANES), 1)
    group = lane // 32
    shell = lane % 32

    def pack_halo(ref, base, rnd):
        for side, row in ((0, 0), (1, ROWS - 1)):
            for f in range(7):
                rowsend[rnd, side, f : f + 1, :] = ref[f, row : row + 1, base : base + WIDTH]
            rowsend[rnd, side, 7:8, :] = jnp.zeros((1, WIDTH), F32)
        for side, tile, have in ((0, base, 0), (1, base + WIDTH - LANES, 3)):
            for half, fields in ((0, range(4)), (1, range(4, 7))):
                total = jnp.zeros((ROWS, LANES), F32)
                for f in fields:
                    moved = pltpu.roll(ref[f, :, tile : tile + LANES], 32 * ((f % 4 - have) % 4), 1)
                    total = jnp.where(group == f % 4, moved, total)
                colsend[rnd, side, half] = total

    def halo_copies(rnd):
        def copy(src, dst, i, **where):
            return pltpu.make_async_remote_copy(
                src_ref=src, dst_ref=dst, send_sem=halo_ss.at[rnd, i], recv_sem=halo_rs.at[rnd, i],
                device_id=where, device_id_type=MESH,
            )

        return [
            copy(rowsend.at[rnd, 0], rowrecv.at[rnd, 1], 0, colat=north),
            copy(rowsend.at[rnd, 1], rowrecv.at[rnd, 0], 1, colat=south),
            copy(colsend.at[rnd, 0], colrecv.at[rnd, 1], 2, lon=west),
            copy(colsend.at[rnd, 1], colrecv.at[rnd, 0], 3, lon=east),
        ]

    grow = (device[0:1, :] // 16) * ROWS + drow[0:1, :]
    gcol = (device[0:1, :] % 16) * COLS + dcol[0:1, :]
    along_row = weights[1:2, :] + weights[3:4, :]
    along_row0 = weights[0:1, :] + weights[2:3, :]
    along_col = weights[2:3, :] + weights[3:4, :]
    along_col0 = weights[0:1, :] + weights[1:2, :]

    def held(rr, cc):
        return (rr >= -1) & (rr < ROWS) & (cc >= -1) & (cc < COLS)

    rr, cc = grow - colat * ROWS, gcol - lon * COLS
    mine_row = jnp.where(held(rr, cc), 1.0, 0.0)
    mine = jnp.concatenate([mine_row[:, t * LANES : (t + 1) * LANES] for t in range(12)], axis=0)
    mine = jnp.concatenate([mine, jnp.zeros((4, LANES), F32)], axis=0).astype(BF16)
    up, down = iota((LANES, LANES), 0), iota((LANES, LANES), 1)
    same = up % HUBS == down % HUBS
    before = dot(mine, flag01(same & (up < down)))
    whole = dot(mine, flag01(same)).astype(BF16)
    earlier = dot(flag01(iota((16, 16), 0) > iota((16, 16), 1)), whole)
    rank = before + earlier
    rank_row = jnp.concatenate([rank[t : t + 1, :] for t in range(12)], axis=1)
    point = iota((1, POINTS), 1)
    slot_row = iota((HELD, 1), 0)
    cell = iota((ROWS, 1), 0)
    row_w = jnp.where(cell == rr, along_row0, 0.0) + jnp.where(cell == rr + 1, along_row, 0.0)
    col_w = jnp.where(cell == cc, along_col0, 0.0) + jnp.where(cell == cc + 1, along_col, 0.0)
    row_hi, row_lo = split2(row_w)
    col_hi, col_lo = split2(col_w)
    row_parts = jnp.concatenate([row_hi, row_lo, row_hi, row_hi * 0], axis=0)
    col_parts = jnp.concatenate([col_hi, col_lo, col_lo * 0, col_lo * 0], axis=0)
    cell4 = iota((LANES, WIDTH), 0)
    expand = flag01((cell4 % 32 == iota((LANES, WIDTH), 1) // 32))

    def fill_slots(turn):
        order = rank_row.astype(I32) - turn * SLOTS
        slot = jnp.where(
            (mine_row > 0.0) & (order >= 0) & (order < SLOTS), (point % HUBS) * SLOTS + order, -1
        )
        chosen = flag01(slot == slot_row)
        lhs_ref[...] = dot_t(chosen, row_parts).astype(BF16)
        spread[...] = dot(dot_t(chosen, col_parts).astype(BF16), expand)

    spin_parts = jnp.concatenate(list(split3(spin[0])) + [jnp.zeros((ROWS, COLS), BF16)], axis=1)
    spinx[...] = dot(spin_parts, expand)

    out_row = iota((192, 1), 0)
    my_lane = ((out_row // 2) % 8) * HUBS + hub

    def column(values):
        tall = jnp.concatenate(
            [jnp.broadcast_to(values[:, t * LANES : (t + 1) * LANES], (16, LANES)) for t in range(12)], axis=0
        )
        return jnp.sum(jnp.where(lane == my_lane, tall, 0), axis=1, keepdims=True)

    source = lane // 8
    s_rr = column(grow) - (source // 2) * ROWS
    s_cc = column(gcol) - (plane * 2 + source % 2) * COLS
    has = held(s_rr, s_cc)
    count_row, count_col = iota((192, 192), 0), iota((192, 192), 1)
    seen = dot(flag01((count_col // 2 < count_row // 2) & (count_col % 2 == 0)), flag01(has))

    def fill_picks(turn):
        slot = seen.astype(I32) - turn * SLOTS
        take = has & (slot == lane % SLOTS) & (out_row % 2 == (lane % 8) // SLOTS)
        pick_ref[...] = flag01(take)

    if rounds == 1:
        fill_slots(0)
        fill_picks(0)

    every = iota((LANES, 1), 0)
    counts = dot_t(
        flag01(held(grow - (every // 16) * ROWS, gcol - (every % 16) * COLS)),
        flag01(iota((LANES, 1), 0) == point % HUBS),
    )
    overfull[0, 0] = jnp.where(jnp.max(counts) > SLOTS, 1, 0)

    row_id = iota((ROWS, 1), 0)
    inv_radius = 1.0 / (1.0 + 0.25 * (shell.astype(F32) + 0.5) / 32)
    theta = jnp.pi / 4 + ((colat * ROWS + row_id).astype(F32) + 0.5) * (jnp.pi / 512.0)
    metric_p = inv_radius / jnp.sin(theta)

    def rate(rnd, base_ref, base_off, dst, dst_off, dt):
        mt, mp = inv_radius, metric_p
        mt2, mp2 = mt * mt, mp * mp
        centre = 2.0 * (mt2 + mp2 + 1.0)
        half_t, half_p = (0.5 * dt) * mt, (0.5 * dt) * mp

        @pl.loop(0, 8)
        def _(t):
            off = pl.multiple_of(t * LANES, LANES)

            def tile(f, k):
                return ext[rnd, f, :, pl.ds(pl.multiple_of(off + k * LANES, LANES), LANES)]

            ut, up_, ur, temp, bt, bp, br = (tile(f, 1) for f in range(7))
            fields = (ut, up_, ur, temp, bt, bp, br)
            at, ap, ar = ut * half_t, up_ * half_p, ur * (0.5 * dt)
            st, sp, sr = bt * half_t, bp * half_p, br * (0.5 * dt)
            spin_dt = spinx[:, pl.ds(off, LANES)] * dt
            base, stretch = [], []
            for f, c in enumerate(fields):
                n = jnp.where(row_id == 0, 0.0, pltpu.roll(c, 1, 0))
                s = jnp.where(row_id == ROWS - 1, 0.0, pltpu.roll(c, ROWS - 1, 0))
                w = pltpu.roll(jnp.where(group == 3, tile(f, 0), c), 32, 1)
                e = pltpu.roll(jnp.where(group == 0, tile(f, 2), c), 96, 1)
                u = jnp.where(shell == 31, c, pltpu.roll(c, 127, 1))
                d = jnp.where(shell == 0, c, pltpu.roll(c, 1, 1))
                laplace = mt2 * (s + n) + mp2 * (e + w) + (u + d) - centre * c
                sn, ew, ud = s - n, e - w, u - d
                base.append((DIFFUSE[f] * dt) * laplace - (at * sn + ap * ew + ar * ud))
                stretch.append(st * sn + sp * ew + sr * ud if f != 3 else None)
            add = [
                stretch[4] + spin_dt * up_,
                stretch[5] - spin_dt * ut,
                stretch[6] + dt * temp,
                None,
                stretch[0],
                stretch[1],
                stretch[2],
            ]
            for f in range(7):
                value = base_ref[f, :, pl.ds(pl.multiple_of(base_off + off, LANES), LANES)] + base[f]
                if add[f] is not None:
                    value = value + add[f]
                dst[f, :, pl.ds(pl.multiple_of(dst_off + off, LANES), LANES)] = value

    edges = [
        (colat == 0, lon),
        (colat == 7, 16 + lon),
        (lon == 0, 32 + colat),
        (lon == 15, 40 + colat),
    ]

    field_id = iota((8, 1), 0)
    diffuse = jnp.where(field_id < 3, DIFFUSE[0], jnp.where(field_id == 3, DIFFUSE[3], DIFFUSE[6]))

    def add_row(rnd, dst, dst_off, dt, row, sign, values):
        for t in range(8):
            tile = slice(LANES + t * LANES, LANES + (t + 1) * LANES)
            v = values(t)
            at = ext[rnd, 0, row : row + 1, tile] * (inv_radius * (0.5 * dt * sign))
            st = ext[rnd, 4, row : row + 1, tile] * (inv_radius * (0.5 * dt * sign))
            change = (dt * diffuse * (inv_radius * inv_radius) - at) * v + st * pltpu.roll(v, 4, 0)
            for f in range(7):
                place_at = (f, slice(row, row + 1), slice(dst_off + t * LANES, dst_off + (t + 1) * LANES))
                dst[place_at] += change[f : f + 1]

    def add_col(rnd, dst, dst_off, dt, t, sign, values):
        tile = slice(LANES + t * LANES, LANES + (t + 1) * LANES)
        ap = ext[rnd, 1, :, tile] * (metric_p * (0.5 * dt * sign))
        sp = ext[rnd, 5, :, tile] * (metric_p * (0.5 * dt * sign))
        spread_p = metric_p * metric_p * dt
        vs = [values(f) for f in range(7)]
        for f in range(7):
            change = (DIFFUSE[f] * spread_p - ap) * vs[f]
            if f != 3:
                change = change + sp * vs[(f + 4) % 8]
            place_at = (f, slice(None), slice(dst_off + t * LANES, dst_off + (t + 1) * LANES))
            dst[place_at] += change

    def add_halos(rnd, dst, dst_off, dt):
        def recv_row(side):
            return lambda t: rowrecv[rnd, side, :, t * LANES : (t + 1) * LANES]

        def recv_col(side, goal):
            def values(f):
                moved = pltpu.roll(colrecv[rnd, side, f // 4], 32 * ((goal - f % 4) % 4), 1)
                return jnp.where(group == goal, moved, 0.0)

            return values

        pl.when(colat > 0)(lambda: add_row(rnd, dst, dst_off, dt, 0, -1.0, recv_row(0)))
        pl.when(colat < 7)(lambda: add_row(rnd, dst, dst_off, dt, ROWS - 1, 1.0, recv_row(1)))
        pl.when(lon > 0)(lambda: add_col(rnd, dst, dst_off, dt, 0, -1.0, recv_col(0, 0)))
        pl.when(lon < 15)(lambda: add_col(rnd, dst, dst_off, dt, 7, 1.0, recv_col(1, 3)))

    def clear_border(ref, base):
        for kind, row in ((0, 0), (1, ROWS - 1)):

            @pl.when(edges[kind][0])
            def _():
                for f in range(7):
                    ref[f, row : row + 1, base : base + WIDTH] = jnp.zeros((1, WIDTH), F32)

        for kind, off, goal in ((2, base, 0), (3, base + WIDTH - LANES, 3)):

            @pl.when(edges[kind][0])
            def _():
                for f in range(7):
                    ref[f, :, off : off + LANES] = jnp.where(group == goal, 0.0, ref[f, :, off : off + LANES])

    def add_border(dst, dst_off, dt):
        def ext_row(row):
            def values(t):
                tile = slice(LANES + t * LANES, LANES + (t + 1) * LANES)
                rows = [ext[1, f, row : row + 1, tile] for f in range(7)]
                return jnp.concatenate(rows + [jnp.zeros((1, LANES), F32)], axis=0)

            return values

        def ext_col(t, shift, goal):
            def values(f):
                have = ext[1, f, :, LANES + t * LANES : LANES + (t + 1) * LANES]
                return jnp.where(group == goal, pltpu.roll(have, shift, 1), 0.0)

            return values

        pl.when(colat == 0)(lambda: add_row(1, dst, dst_off, dt, 1, -1.0, ext_row(0)))
        pl.when(colat == 7)(lambda: add_row(1, dst, dst_off, dt, ROWS - 2, 1.0, ext_row(ROWS - 1)))
        pl.when(lon == 0)(lambda: add_col(1, dst, dst_off, dt, 0, -1.0, ext_col(0, 32, 1)))
        pl.when(lon == 15)(lambda: add_col(1, dst, dst_off, dt, 7, 1.0, ext_col(7, 96, 2)))

    def send_points(ref, base, rnd):
        low_rows = iota((8, 1), 0) < SLOTS

        def turn_points(turn):
            halves = [jnp.zeros((HELD, LANES), F32) for _ in range(2)]
            lhs = lhs_ref[...][:, :96]
            for f in range(7):
                hi, lo = split2(ref[f, :, base : base + WIDTH])
                rows = dot(lhs, jnp.concatenate([hi, hi, lo], axis=0))
                folded = jnp.zeros((HELD, LANES), F32)
                for t in range(8):
                    folded += rows[:, t * LANES : (t + 1) * LANES] * spread[:, t * LANES : (t + 1) * LANES]
                folded += pltpu.roll(folded, 32, 1)
                folded += pltpu.roll(folded, 64, 1)
                halves[f // 4] = jnp.where(group == f % 4, folded, halves[f // 4])
            for v in range(HUBS // 2):
                first, second = (part[8 * v : 8 * v + 8] for part in halves)
                p1send[rnd, turn, 2 * v] = jnp.where(low_rows, first, pltpu.roll(second, SLOTS, 0))
                p1send[rnd, turn, 2 * v + 1] = jnp.where(low_rows, pltpu.roll(first, SLOTS, 0), second)
            p1recv[rnd, turn, hub] = p1send[rnd, turn, hub]

            @pl.loop(1, HUBS)
            def _(f):
                h = (hub + f) % HUBS
                pltpu.make_async_remote_copy(
                    src_ref=p1send.at[rnd, turn, h], dst_ref=p1recv.at[rnd, turn, hub],
                    send_sem=p1_ss.at[rnd, turn], recv_sem=p1_rs.at[rnd, turn],
                    device_id=peer(h), device_id_type=MESH,
                ).start()

        if rounds == 1:
            turn_points(0)
        else:

            @pl.loop(0, rounds)
            def _(turn):
                fill_slots(turn)
                turn_points(turn)

    def wait_bytes(ref, sem):
        pltpu.make_async_copy(ref, ref, sem).wait()

    def relay(rnd):
        def turn_sum(turn):
            wait_bytes(p1recv.at[rnd, turn, pl.ds(0, HUBS - 1)], p1_rs.at[rnd, turn])
            parts = jnp.concatenate(split3(p1recv[rnd, turn].reshape(LANES, LANES)), axis=0)
            pick = pick_ref[...]
            return dot(jnp.concatenate([pick, pick, pick], axis=1), parts)

        if rounds == 1:
            picked = turn_sum(0)
        else:
            hub_sum[...] = jnp.zeros_like(hub_sum)

            @pl.loop(0, rounds)
            def _(turn):
                fill_picks(turn)
                hub_sum[...] += turn_sum(turn)

            picked = hub_sum[...]
        for s in range(SEGMENTS):
            p2send[rnd, s] = picked[4 * s : 4 * s + 4, :]
        if rnd == 0:
            pl.semaphore_wait(ready, 7)

        def send(s, kind, to_colat, to_lon):
            pltpu.make_async_remote_copy(
                src_ref=p2send.at[rnd, s], dst_ref=p2recv.at[rnd, kind, plane * HUBS + hub],
                send_sem=p2_ss.at[rnd], recv_sem=p2_rs.at[rnd, kind],
                device_id=dict(panel=other, colat=to_colat, lon=to_lon), device_id_type=MESH,
            ).start()

        @pl.loop(0, 16)
        def _(i):
            send(i, 0, 0, i)
            send(16 + i, 1, 7, i)

        @pl.loop(0, 8)
        def _(i):
            send(32 + i, 2, i, 0)
            send(40 + i, 3, i, 15)

    def place(rnd, ref, base):
        line = iota((64, 1), 0)
        line_point = 16 * ((line // 2) % 2) + line // 4
        from_row = iota((64, 64), 0)
        from_col = iota((64, 64), 1)
        for kind, (here, segment) in enumerate(edges):

            @pl.when(here)
            def _():
                wait_bytes(p2recv.at[rnd, kind], p2_rs.at[rnd, kind])
                total = p2recv[rnd, kind, 0:HUBS]
                for z in range(1, 8):
                    total = total + p2recv[rnd, kind, z * HUBS : (z + 1) * HUBS]
                for h in range(HUBS):
                    summed[4 * h : 4 * h + 4, :] = total[h]
                x = summed[...]
                own = angle[pl.ds(pl.multiple_of((segment // 4) * LANES, LANES), LANES)].reshape(1, LANES)
                own = jnp.where(lane == (segment % 4) * 32 + line_point, own, 0.0)
                own = jnp.sum(own, axis=1, keepdims=True)
                cosine, sine = jnp.cos(own), jnp.sin(own)
                cosine = jnp.where(group < 2, cosine, 1.0)
                swap = jnp.where(group == 0, -pltpu.roll(x, 96, 1), pltpu.roll(x, 32, 1))
                x = cosine * x + jnp.where(group < 2, sine, 0.0) * swap
                part = from_row // 32
                at = from_row % 32
                j = at if kind >= 2 else 4 * (at % 8) + at // 8
                perm = flag01(from_col == 4 * (j % 16) + 2 * (j // 16) + part)
                x = dot(jnp.concatenate([perm, perm, perm], axis=1), jnp.concatenate(split3(x), axis=0))
                for f in range(7):
                    block = x[32 * (f // 4) : 32 * (f // 4) + 32]
                    if kind < 2:
                        row = 0 if kind == 0 else ROWS - 1
                        tiles = jnp.zeros((8, LANES), F32)
                        for g in range(4):
                            moved = pltpu.roll(block[8 * g : 8 * g + 8], 32 * ((g - f % 4) % 4), 1)
                            tiles = jnp.where(group == g, moved, tiles)
                        for t in range(8):
                            ref[f, row : row + 1, base + t * LANES : base + (t + 1) * LANES] = tiles[t : t + 1]
                    else:
                        goal, off = (0, base) if kind == 2 else (3, base + WIDTH - LANES)
                        moved = pltpu.roll(block, 32 * ((goal - f % 4) % 4), 1)
                        now = ref[f, :, off : off + LANES]
                        corner = ((row_id == 0) & (colat == 0)) | ((row_id == ROWS - 1) & (colat == 7))
                        blend = jnp.where(corner, 0.5 * (moved + now), moved)
                        ref[f, :, off : off + LANES] = jnp.where(group == goal, blend, now)

    for f in range(7):
        ext[0, f, :, LANES : LANES + WIDTH] = state[f]
        for rnd in range(2):
            ext[rnd, f, :, :LANES] = jnp.zeros((ROWS, LANES), F32)
            ext[rnd, f, :, LANES + WIDTH :] = jnp.zeros((ROWS, LANES), F32)
    pack_halo(state, 0, 0)
    pl.semaphore_wait(barrier, 31 + 7 + 2)
    halos0 = halo_copies(0)
    for copy in halos0:
        copy.start()

    @pl.loop(1, 8)
    def _(f):
        pl.semaphore_signal(
            ready, inc=1, device_id=dict(lon=((plane + f) % 8) * 2 + y_lo), device_id_type=MESH
        )

    rate(0, state, 0, ext.at[1], LANES, 0.1)
    for copy in halos0:
        copy.wait_recv()
    add_halos(0, ext.at[1], LANES, 0.1)
    clear_border(ext.at[1], LANES)
    send_points(ext.at[1], LANES, 0)
    pack_halo(ext.at[1], LANES, 1)
    halos1 = halo_copies(1)
    for copy in halos1:
        copy.start()
    relay(0)
    rate(1, state, 0, out, 0, 0.2)
    for copy in halos1:
        copy.wait_recv()
    add_halos(1, out, 0, 0.2)
    place(0, ext.at[1], LANES)
    add_border(out, 0, 0.2)
    send_points(out, 0, 1)
    relay(1)
    place(1, out, 0)
    for copy in halos0 + halos1:
        copy.wait_send()
    for rnd in range(2):
        for turn in range(rounds):
            wait_bytes(p1send.at[rnd, turn, pl.ds(0, HUBS - 1)], p1_ss.at[rnd, turn])
        wait_bytes(p2send.at[rnd], p2_ss.at[rnd])


def step(rounds, state, spin, device, drow, dcol, weights, angle):
    vmem = pl.BlockSpec(memory_space=pltpu.VMEM)
    scratch = lambda *shape: pltpu.VMEM(shape, F32)
    return pl.pallas_call(
        functools.partial(step_kernel, rounds),
        out_shape=(
            jax.ShapeDtypeStruct((7, ROWS, WIDTH), F32),
            jax.ShapeDtypeStruct((1, 1), I32),
        ),
        in_specs=[vmem] * 7,
        out_specs=(vmem, pl.BlockSpec(memory_space=pltpu.SMEM)),
        scratch_shapes=[
            scratch(2, 7, ROWS, WIDTH + 2 * LANES),
            scratch(2, 2, 8, WIDTH),
            scratch(2, 2, 8, WIDTH),
            scratch(2, 2, 2, ROWS, LANES),
            scratch(2, 2, 2, ROWS, LANES),
            scratch(2, rounds, HUBS, 8, LANES),
            scratch(2, rounds, HUBS, 8, LANES),
            scratch(2, SEGMENTS, 4, LANES),
            scratch(2, 4, 8 * HUBS, 4, LANES),
            scratch(64, LANES),
            scratch(HELD, WIDTH),
            scratch(ROWS, WIDTH),
            pltpu.VMEM((HELD, LANES), BF16),
            pltpu.VMEM((192, LANES), BF16),
            scratch(192, LANES),
            pltpu.SemaphoreType.DMA((2, 4)),
            pltpu.SemaphoreType.DMA((2, 4)),
            pltpu.SemaphoreType.DMA((2, rounds)),
            pltpu.SemaphoreType.DMA((2, rounds)),
            pltpu.SemaphoreType.DMA((2,)),
            pltpu.SemaphoreType.DMA((2, 4)),
            pltpu.SemaphoreType.REGULAR,
        ],
        compiler_params=pltpu.CompilerParams(
            collective_id=0 if rounds == 1 else 1, has_side_effects=True, vmem_limit_bytes=48 * 2**20
        ),
        name="dynamo_step" if rounds == 1 else "general_step",
    )(state, spin, device, drow, dcol, weights, angle)


def on_device(state, spin, donor_device, donor_row, donor_col, corner_weights, border_angle):
    args = (state[0], spin, donor_device, donor_row, donor_col, corner_weights, border_angle)
    fast, overfull = step(1, *args)
    turns = POINTS // HUBS // SLOTS
    advanced = lax.cond(overfull[0, 0] > 0, lambda: step(turns, *args)[0], lambda: fast)
    return advanced[None]


def solution(mesh):
    placed = (P("panel", None, "colat", "lon"), P("panel", "colat", "lon"), P(), P(), P(), P(), P())
    return jax.shard_map(
        on_device,
        mesh=mesh,
        in_specs=placed,
        out_specs=P("panel", None, "colat", "lon"),
        check_vma=False,
    )
```

```python
import functools

import jax
import jax.numpy as jnp
from jax import lax
from jax.experimental import pallas as pl
from jax.experimental.pallas import tpu as pltpu
from jax.sharding import PartitionSpec as P

MESH = pl.DeviceIdType.MESH
F32, BF16, I32 = jnp.float32, jnp.bfloat16, jnp.int32
ROWS, COLS, WIDTH, LANES = 32, 32, 1024, 128
HELD = 64
POINTS, HUBS, SLOTS, SEGMENTS = 1536, 32, 2, 48
PARCEL = 2 * SLOTS
DIFFUSE = (0.3, 0.3, 0.3, 0.4, 0.5, 0.5, 0.5)


def iota(shape, dim):
    return lax.broadcasted_iota(I32, shape, dim)


def flag01(cond):
    return jnp.where(cond, 1.0, 0.0).astype(BF16)


def split2(x):
    hi = x.astype(BF16)
    return hi, (x - hi.astype(F32)).astype(BF16)


def split3(x):
    hi, rest = x.astype(BF16), None
    rest = x - hi.astype(F32)
    mid = rest.astype(BF16)
    return hi, mid, (rest - mid.astype(F32)).astype(BF16)


def dot(a, b):
    return lax.dot_general(a, b, (((1,), (0,)), ((), ())), preferred_element_type=F32)


def dot_t(a, b):
    return lax.dot_general(a, b, (((1,), (1,)), ((), ())), preferred_element_type=F32)


def step_kernel(
    rounds,
    state, spin, device, drow, dcol, weights, angle, out, overfull,
    ext, rowsend, rowrecv, colsend, colrecv, p1send, p1recv, p2send, p2recv, summed, spread, spinx,
    lhs_ref, pick_ref, hub_sum, halo_ss, halo_rs, p1_ss, p1_rs, p2_ss, p2_rs, state_sem, ready, all_in,
):
    panel, colat, lon = (lax.axis_index(a) for a in ("panel", "colat", "lon"))
    plane, y_lo = lon // 2, lon % 2
    pair, odd = plane // 2, plane % 2
    hub = (colat * 2 + y_lo) * 2 + odd
    other = 1 - panel

    barrier = pltpu.get_barrier_semaphore()

    def greet(**where):
        pl.semaphore_signal(barrier, inc=1, device_id=where, device_id_type=MESH)

    def peer(h):
        return dict(colat=h // 4, lon=(pair * 2 + h % 2) * 2 + (h // 2) % 2)

    def across(f):
        return dict(lon=(((pair + f) % 4) * 2 + odd) * 2 + y_lo)

    whole_state = pltpu.make_async_copy(state, ext.at[0, :, :, pl.ds(LANES, WIDTH)], state_sem)
    whole_state.start()

    @pl.loop(1, HUBS)
    def _(f):
        greet(**peer((hub + f) % HUBS))

    @pl.loop(1, 4)
    def _(f):
        greet(**across(f))

    greet(panel=other)
    north, south = (colat + 7) % 8, (colat + 1) % 8
    west, east = (lon + 15) % 16, (lon + 1) % 16
    greet(lon=west)
    greet(lon=east)

    lane = iota((1, LANES), 1)
    group = lane // 32
    shell = lane % 32

    def pack_halo(ref, base, rnd):
        for side, row in ((0, 0), (1, ROWS - 1)):
            for f in range(7):
                rowsend[rnd, side, f : f + 1, :] = ref[f, row : row + 1, base : base + WIDTH]
            rowsend[rnd, side, 7:8, :] = jnp.zeros((1, WIDTH), F32)
        for side, tile, have in ((0, base, 0), (1, base + WIDTH - LANES, 3)):
            for half, fields in ((0, range(4)), (1, range(4, 7))):
                total = jnp.zeros((ROWS, LANES), F32)
                for f in fields:
                    moved = pltpu.roll(ref[f, :, tile : tile + LANES], 32 * ((f % 4 - have) % 4), 1)
                    total = jnp.where(group == f % 4, moved, total)
                colsend[rnd, side, half] = total

    def halo_copies(rnd):
        def copy(src, dst, i, **where):
            return pltpu.make_async_remote_copy(
                src_ref=src, dst_ref=dst, send_sem=halo_ss.at[rnd, i], recv_sem=halo_rs.at[rnd, i],
                device_id=where, device_id_type=MESH,
            )

        return [
            copy(rowsend.at[rnd, 0], rowrecv.at[rnd, 1], 0, colat=north),
            copy(rowsend.at[rnd, 1], rowrecv.at[rnd, 0], 1, colat=south),
            copy(colsend.at[rnd, 0], colrecv.at[rnd, 1], 2, lon=west),
            copy(colsend.at[rnd, 1], colrecv.at[rnd, 0], 3, lon=east),
        ]

    grow = (device[0:1, :] // 16) * ROWS + drow[0:1, :]
    gcol = (device[0:1, :] % 16) * COLS + dcol[0:1, :]
    along_row = weights[1:2, :] + weights[3:4, :]
    along_row0 = weights[0:1, :] + weights[2:3, :]
    along_col = weights[2:3, :] + weights[3:4, :]
    along_col0 = weights[0:1, :] + weights[1:2, :]

    def held(rr, cc):
        return (rr >= -1) & (rr < ROWS) & (cc >= -1) & (cc < COLS)

    rr, cc = grow - colat * ROWS, gcol - lon * COLS
    mine_row = jnp.where(held(rr, cc), 1.0, 0.0)
    mine = jnp.concatenate([mine_row[:, t * LANES : (t + 1) * LANES] for t in range(12)], axis=0)
    mine = jnp.concatenate([mine, jnp.zeros((4, LANES), F32)], axis=0).astype(BF16)
    up, down = iota((LANES, LANES), 0), iota((LANES, LANES), 1)
    same = up % HUBS == down % HUBS
    before = dot(mine, flag01(same & (up < down)))
    whole = dot(mine, flag01(same)).astype(BF16)
    earlier = dot(flag01(iota((16, 16), 0) > iota((16, 16), 1)), whole)
    rank = before + earlier
    rank_row = jnp.concatenate([rank[t : t + 1, :] for t in range(12)], axis=1)
    point = iota((1, POINTS), 1)
    slot_row = iota((HELD, 1), 0)
    cell = iota((ROWS, 1), 0)
    row_w = jnp.where(cell == rr, along_row0, 0.0) + jnp.where(cell == rr + 1, along_row, 0.0)
    col_w = jnp.where(cell == cc, along_col0, 0.0) + jnp.where(cell == cc + 1, along_col, 0.0)
    row_hi, row_lo = split2(row_w)
    col_hi, col_lo = split2(col_w)
    row_parts = jnp.concatenate([row_hi, row_lo, row_hi, row_hi * 0], axis=0)
    col_parts = jnp.concatenate([col_hi, col_lo, col_lo * 0, col_lo * 0], axis=0)
    cell4 = iota((LANES, WIDTH), 0)
    expand = flag01((cell4 % 32 == iota((LANES, WIDTH), 1) // 32))

    def fill_slots(turn):
        order = rank_row.astype(I32) - turn * SLOTS
        slot = jnp.where(
            (mine_row > 0.0) & (order >= 0) & (order < SLOTS), (point % HUBS) * SLOTS + order, -1
        )
        chosen = flag01(slot == slot_row)
        lhs_ref[...] = dot_t(chosen, row_parts).astype(BF16)
        spread[...] = dot(dot_t(chosen, col_parts).astype(BF16), expand)

    spin_parts = jnp.concatenate(list(split3(spin[0])) + [jnp.zeros((ROWS, COLS), BF16)], axis=1)
    spinx[...] = dot(spin_parts, expand)

    out_row = iota((2 * SEGMENTS, 1), 0)
    my_lane = ((out_row // 2) % 4) * HUBS + hub

    def column(values):
        tall = jnp.concatenate(
            [jnp.broadcast_to(values[:, t * LANES : (t + 1) * LANES], (8, LANES)) for t in range(12)], axis=0
        )
        return jnp.sum(jnp.where(lane == my_lane, tall, 0), axis=1, keepdims=True)

    parcel_lane = iota((1, HUBS * PARCEL), 1)
    source = parcel_lane // PARCEL
    s_rr = column(grow) - (source // 4) * ROWS
    s_cc = column(gcol) - ((pair * 2 + source % 2) * 2 + (source // 2) % 2) * COLS
    has = held(s_rr, s_cc)
    count_row, count_col = (iota((2 * SEGMENTS, 2 * SEGMENTS), d) for d in range(2))
    seen = dot(flag01((count_col // 2 < count_row // 2) & (count_col % 2 == 0)), flag01(has))

    def fill_picks(turn):
        slot = seen.astype(I32) - turn * SLOTS
        take = has & (slot == parcel_lane % SLOTS) & (out_row % 2 == (parcel_lane % PARCEL) // SLOTS)
        pick_ref[...] = flag01(take)

    if rounds == 1:
        fill_slots(0)
        fill_picks(0)

    every = iota((LANES, 1), 0)
    counts = dot_t(
        flag01(held(grow - (every // 16) * ROWS, gcol - (every % 16) * COLS)),
        flag01(iota((LANES, 1), 0) == point % HUBS),
    )
    overfull[0, 0] = jnp.where(jnp.max(counts) > SLOTS, 1, 0)

    row_id = iota((ROWS, 1), 0)
    inv_radius = 1.0 / (1.0 + 0.25 * (shell.astype(F32) + 0.5) / 32)
    theta = jnp.pi / 4 + ((colat * ROWS + row_id).astype(F32) + 0.5) * (jnp.pi / 512.0)
    metric_p = inv_radius / jnp.sin(theta)

    def rate(rnd, base_ref, base_off, dst, dst_off, dt):
        mt, mp = inv_radius, metric_p
        mt2, mp2 = mt * mt, mp * mp
        centre = 2.0 * (mt2 + mp2 + 1.0)
        half_t, half_p = (0.5 * dt) * mt, (0.5 * dt) * mp

        @pl.loop(0, 8)
        def _(t):
            off = pl.multiple_of(t * LANES, LANES)

            def tile(f, k):
                return ext[rnd, f, :, pl.ds(pl.multiple_of(off + k * LANES, LANES), LANES)]

            ut, up_, ur, temp, bt, bp, br = (tile(f, 1) for f in range(7))
            fields = (ut, up_, ur, temp, bt, bp, br)
            at, ap, ar = ut * half_t, up_ * half_p, ur * (0.5 * dt)
            st, sp, sr = bt * half_t, bp * half_p, br * (0.5 * dt)
            spin_dt = spinx[:, pl.ds(off, LANES)] * dt
            base, stretch = [], []
            for f, c in enumerate(fields):
                n = jnp.where(row_id == 0, 0.0, pltpu.roll(c, 1, 0))
                s = jnp.where(row_id == ROWS - 1, 0.0, pltpu.roll(c, ROWS - 1, 0))
                w = pltpu.roll(jnp.where(group == 3, tile(f, 0), c), 32, 1)
                e = pltpu.roll(jnp.where(group == 0, tile(f, 2), c), 96, 1)
                u = jnp.where(shell == 31, c, pltpu.roll(c, 127, 1))
                d = jnp.where(shell == 0, c, pltpu.roll(c, 1, 1))
                laplace = mt2 * (s + n) + mp2 * (e + w) + (u + d) - centre * c
                sn, ew, ud = s - n, e - w, u - d
                base.append((DIFFUSE[f] * dt) * laplace - (at * sn + ap * ew + ar * ud))
                stretch.append(st * sn + sp * ew + sr * ud if f != 3 else None)
            add = [
                stretch[4] + spin_dt * up_,
                stretch[5] - spin_dt * ut,
                stretch[6] + dt * temp,
                None,
                stretch[0],
                stretch[1],
                stretch[2],
            ]
            for f in range(7):
                value = base_ref[f, :, pl.ds(pl.multiple_of(base_off + off, LANES), LANES)] + base[f]
                if add[f] is not None:
                    value = value + add[f]
                dst[f, :, pl.ds(pl.multiple_of(dst_off + off, LANES), LANES)] = value

    edges = [
        (colat == 0, lon),
        (colat == 7, 16 + lon),
        (lon == 0, 32 + colat),
        (lon == 15, 40 + colat),
    ]

    field_id = iota((8, 1), 0)
    diffuse = jnp.where(field_id < 3, DIFFUSE[0], jnp.where(field_id == 3, DIFFUSE[3], DIFFUSE[6]))

    def add_row(rnd, dst, dst_off, dt, row, sign, values):
        for t in range(8):
            tile = slice(LANES + t * LANES, LANES + (t + 1) * LANES)
            v = values(t)
            at = ext[rnd, 0, row : row + 1, tile] * (inv_radius * (0.5 * dt * sign))
            st = ext[rnd, 4, row : row + 1, tile] * (inv_radius * (0.5 * dt * sign))
            change = (dt * diffuse * (inv_radius * inv_radius) - at) * v + st * pltpu.roll(v, 4, 0)
            for f in range(7):
                place_at = (f, slice(row, row + 1), slice(dst_off + t * LANES, dst_off + (t + 1) * LANES))
                dst[place_at] += change[f : f + 1]

    def add_col(rnd, dst, dst_off, dt, t, sign, values):
        tile = slice(LANES + t * LANES, LANES + (t + 1) * LANES)
        ap = ext[rnd, 1, :, tile] * (metric_p * (0.5 * dt * sign))
        sp = ext[rnd, 5, :, tile] * (metric_p * (0.5 * dt * sign))
        spread_p = metric_p * metric_p * dt
        vs = [values(f) for f in range(7)]
        for f in range(7):
            change = (DIFFUSE[f] * spread_p - ap) * vs[f]
            if f != 3:
                change = change + sp * vs[(f + 4) % 8]
            place_at = (f, slice(None), slice(dst_off + t * LANES, dst_off + (t + 1) * LANES))
            dst[place_at] += change

    def add_halos(rnd, dst, dst_off, dt):
        def recv_row(side):
            return lambda t: rowrecv[rnd, side, :, t * LANES : (t + 1) * LANES]

        def recv_col(side, goal):
            def values(f):
                moved = pltpu.roll(colrecv[rnd, side, f // 4], 32 * ((goal - f % 4) % 4), 1)
                return jnp.where(group == goal, moved, 0.0)

            return values

        pl.when(colat > 0)(lambda: add_row(rnd, dst, dst_off, dt, 0, -1.0, recv_row(0)))
        pl.when(colat < 7)(lambda: add_row(rnd, dst, dst_off, dt, ROWS - 1, 1.0, recv_row(1)))
        pl.when(lon > 0)(lambda: add_col(rnd, dst, dst_off, dt, 0, -1.0, recv_col(0, 0)))
        pl.when(lon < 15)(lambda: add_col(rnd, dst, dst_off, dt, 7, 1.0, recv_col(1, 3)))

    def clear_border(ref, base):
        for kind, row in ((0, 0), (1, ROWS - 1)):

            @pl.when(edges[kind][0])
            def _():
                for f in range(7):
                    ref[f, row : row + 1, base : base + WIDTH] = jnp.zeros((1, WIDTH), F32)

        for kind, off, goal in ((2, base, 0), (3, base + WIDTH - LANES, 3)):

            @pl.when(edges[kind][0])
            def _():
                for f in range(7):
                    ref[f, :, off : off + LANES] = jnp.where(group == goal, 0.0, ref[f, :, off : off + LANES])

    def add_border(dst, dst_off, dt):
        def ext_row(row):
            def values(t):
                tile = slice(LANES + t * LANES, LANES + (t + 1) * LANES)
                rows = [ext[1, f, row : row + 1, tile] for f in range(7)]
                return jnp.concatenate(rows + [jnp.zeros((1, LANES), F32)], axis=0)

            return values

        def ext_col(t, shift, goal):
            def values(f):
                have = ext[1, f, :, LANES + t * LANES : LANES + (t + 1) * LANES]
                return jnp.where(group == goal, pltpu.roll(have, shift, 1), 0.0)

            return values

        pl.when(colat == 0)(lambda: add_row(1, dst, dst_off, dt, 1, -1.0, ext_row(0)))
        pl.when(colat == 7)(lambda: add_row(1, dst, dst_off, dt, ROWS - 2, 1.0, ext_row(ROWS - 1)))
        pl.when(lon == 0)(lambda: add_col(1, dst, dst_off, dt, 0, -1.0, ext_col(0, 32, 1)))
        pl.when(lon == 15)(lambda: add_col(1, dst, dst_off, dt, 7, 1.0, ext_col(7, 96, 2)))

    def send_points(ref, base, rnd):
        def turn_points(turn):
            halves = [jnp.zeros((HELD, LANES), F32) for _ in range(2)]
            lhs = lhs_ref[...][:, :96]
            for f in range(7):
                hi, lo = split2(ref[f, :, base : base + WIDTH])
                rows = dot(lhs, jnp.concatenate([hi, hi, lo], axis=0))
                folded = jnp.zeros((HELD, LANES), F32)
                for t in range(8):
                    folded += rows[:, t * LANES : (t + 1) * LANES] * spread[:, t * LANES : (t + 1) * LANES]
                folded += pltpu.roll(folded, 32, 1)
                folded += pltpu.roll(folded, 64, 1)
                halves[f // 4] = jnp.where(group == f % 4, folded, halves[f // 4])
            for h in range(HUBS):
                for half in range(2):
                    p1send[rnd, turn, h, half * SLOTS : (half + 1) * SLOTS, :] = halves[half][
                        h * SLOTS : (h + 1) * SLOTS
                    ]
            p1recv[rnd, turn, hub] = p1send[rnd, turn, hub]

            @pl.loop(1, HUBS)
            def _(f):
                h = (hub + f) % HUBS
                pltpu.make_async_remote_copy(
                    src_ref=p1send.at[rnd, turn, h], dst_ref=p1recv.at[rnd, turn, hub],
                    send_sem=p1_ss.at[rnd, turn], recv_sem=p1_rs.at[rnd, turn],
                    device_id=peer(h), device_id_type=MESH,
                ).start()

        if rounds == 1:
            turn_points(0)
        else:

            @pl.loop(0, rounds)
            def _(turn):
                fill_slots(turn)
                turn_points(turn)

    def wait_bytes(ref, sem):
        pltpu.make_async_copy(ref, ref, sem).wait()

    def relay(rnd):
        def turn_sum(turn):
            wait_bytes(p1recv.at[rnd, turn, pl.ds(0, HUBS - 1)], p1_rs.at[rnd, turn])
            parts = jnp.concatenate(split3(p1recv[rnd, turn].reshape(HUBS * PARCEL, LANES)), axis=0)
            pick = pick_ref[...]
            return dot(jnp.concatenate([pick, pick, pick], axis=1), parts)

        if rounds == 1:
            picked = turn_sum(0)
        else:
            hub_sum[...] = jnp.zeros_like(hub_sum)

            @pl.loop(0, rounds)
            def _(turn):
                fill_picks(turn)
                hub_sum[...] += turn_sum(turn)

            picked = hub_sum[...]
        for s in range(SEGMENTS):
            p2send[rnd, s] = picked[2 * s : 2 * s + 2, :]
        if rnd == 0:
            pl.semaphore_wait(all_in, 1)

        def send(s, kind, to_colat, to_lon):
            pltpu.make_async_remote_copy(
                src_ref=p2send.at[rnd, s], dst_ref=p2recv.at[rnd, kind, pair * HUBS + hub],
                send_sem=p2_ss.at[rnd], recv_sem=p2_rs.at[rnd, kind],
                device_id=dict(panel=other, colat=to_colat, lon=to_lon), device_id_type=MESH,
            ).start()

        @pl.loop(0, 16)
        def _(i):
            send(i, 0, 0, i)
            send(16 + i, 1, 7, i)

        @pl.loop(0, 8)
        def _(i):
            send(32 + i, 2, i, 0)
            send(40 + i, 3, i, 15)

    def place(rnd, ref, base):
        line = iota((64, 1), 0)
        line_point = line // 2
        from_row = iota((64, 64), 0)
        from_col = iota((64, 64), 1)
        for kind, (here, segment) in enumerate(edges):

            @pl.when(here)
            def _():
                wait_bytes(p2recv.at[rnd, kind], p2_rs.at[rnd, kind])
                total = p2recv[rnd, kind, 0:HUBS]
                for z in range(1, 4):
                    total = total + p2recv[rnd, kind, z * HUBS : (z + 1) * HUBS]
                for h in range(HUBS):
                    summed[2 * h : 2 * h + 2, :] = total[h]
                x = summed[...]
                own = angle[pl.ds(pl.multiple_of((segment // 4) * LANES, LANES), LANES)].reshape(1, LANES)
                own = jnp.where(lane == (segment % 4) * 32 + line_point, own, 0.0)
                own = jnp.sum(own, axis=1, keepdims=True)
                cosine, sine = jnp.cos(own), jnp.sin(own)
                cosine = jnp.where(group < 2, cosine, 1.0)
                swap = jnp.where(group == 0, -pltpu.roll(x, 96, 1), pltpu.roll(x, 32, 1))
                x = cosine * x + jnp.where(group < 2, sine, 0.0) * swap
                part = from_row // 32
                at = from_row % 32
                j = at if kind >= 2 else 4 * (at % 8) + at // 8
                perm = flag01(from_col == 2 * j + part)
                x = dot(jnp.concatenate([perm, perm, perm], axis=1), jnp.concatenate(split3(x), axis=0))
                for f in range(7):
                    block = x[32 * (f // 4) : 32 * (f // 4) + 32]
                    if kind < 2:
                        row = 0 if kind == 0 else ROWS - 1
                        tiles = jnp.zeros((8, LANES), F32)
                        for g in range(4):
                            moved = pltpu.roll(block[8 * g : 8 * g + 8], 32 * ((g - f % 4) % 4), 1)
                            tiles = jnp.where(group == g, moved, tiles)
                        for t in range(8):
                            ref[f, row : row + 1, base + t * LANES : base + (t + 1) * LANES] = tiles[t : t + 1]
                    else:
                        goal, off = (0, base) if kind == 2 else (3, base + WIDTH - LANES)
                        moved = pltpu.roll(block, 32 * ((goal - f % 4) % 4), 1)
                        now = ref[f, :, off : off + LANES]
                        corner = ((row_id == 0) & (colat == 0)) | ((row_id == ROWS - 1) & (colat == 7))
                        blend = jnp.where(corner, 0.5 * (moved + now), moved)
                        ref[f, :, off : off + LANES] = jnp.where(group == goal, blend, now)

    for f in range(7):
        for rnd in range(2):
            ext[rnd, f, :, :LANES] = jnp.zeros((ROWS, LANES), F32)
            ext[rnd, f, :, LANES + WIDTH :] = jnp.zeros((ROWS, LANES), F32)
    whole_state.wait()
    pack_halo(ext.at[0], LANES, 0)
    pl.semaphore_wait(barrier, 31 + 3 + 1 + 2)
    halos0 = halo_copies(0)
    for copy in halos0:
        copy.start()

    @pl.loop(1, 4)
    def _(f):
        pl.semaphore_signal(ready, inc=1, device_id=across(f), device_id_type=MESH)

    rate(0, ext.at[0], LANES, ext.at[1], LANES, 0.1)
    for copy in halos0:
        copy.wait_recv()
    add_halos(0, ext.at[1], LANES, 0.1)
    clear_border(ext.at[1], LANES)
    send_points(ext.at[1], LANES, 0)
    pl.semaphore_wait(ready, 3)
    pl.semaphore_signal(all_in, inc=1, device_id=dict(panel=other), device_id_type=MESH)
    pack_halo(ext.at[1], LANES, 1)
    halos1 = halo_copies(1)
    for copy in halos1:
        copy.start()
    relay(0)
    rate(1, ext.at[0], LANES, out, 0, 0.2)
    for copy in halos1:
        copy.wait_recv()
    add_halos(1, out, 0, 0.2)
    place(0, ext.at[1], LANES)
    add_border(out, 0, 0.2)
    send_points(out, 0, 1)
    relay(1)
    place(1, out, 0)
    for copy in halos0 + halos1:
        copy.wait_send()
    for rnd in range(2):
        for turn in range(rounds):
            wait_bytes(p1send.at[rnd, turn, pl.ds(0, HUBS - 1)], p1_ss.at[rnd, turn])
        wait_bytes(p2send.at[rnd], p2_ss.at[rnd])


def step(rounds, state, spin, device, drow, dcol, weights, angle):
    vmem = pl.BlockSpec(memory_space=pltpu.VMEM)
    scratch = lambda *shape: pltpu.VMEM(shape, F32)
    return pl.pallas_call(
        functools.partial(step_kernel, rounds),
        out_shape=(
            jax.ShapeDtypeStruct((7, ROWS, WIDTH), F32),
            jax.ShapeDtypeStruct((1, 1), I32),
        ),
        in_specs=[pl.BlockSpec(memory_space=pl.ANY)] + [vmem] * 6,
        out_specs=(vmem, pl.BlockSpec(memory_space=pltpu.SMEM)),
        scratch_shapes=[
            scratch(2, 7, ROWS, WIDTH + 2 * LANES),
            scratch(2, 2, 8, WIDTH),
            scratch(2, 2, 8, WIDTH),
            scratch(2, 2, 2, ROWS, LANES),
            scratch(2, 2, 2, ROWS, LANES),
            scratch(2, rounds, HUBS, PARCEL, LANES),
            scratch(2, rounds, HUBS, PARCEL, LANES),
            scratch(2, SEGMENTS, 2, LANES),
            scratch(2, 4, 4 * HUBS, 2, LANES),
            scratch(64, LANES),
            scratch(HELD, WIDTH),
            scratch(ROWS, WIDTH),
            pltpu.VMEM((HELD, LANES), BF16),
            pltpu.VMEM((2 * SEGMENTS, HUBS * PARCEL), BF16),
            scratch(2 * SEGMENTS, LANES),
            pltpu.SemaphoreType.DMA((2, 4)),
            pltpu.SemaphoreType.DMA((2, 4)),
            pltpu.SemaphoreType.DMA((2, rounds)),
            pltpu.SemaphoreType.DMA((2, rounds)),
            pltpu.SemaphoreType.DMA((2,)),
            pltpu.SemaphoreType.DMA((2, 4)),
            pltpu.SemaphoreType.DMA,
            pltpu.SemaphoreType.REGULAR,
            pltpu.SemaphoreType.REGULAR,
        ],
        compiler_params=pltpu.CompilerParams(
            collective_id=0 if rounds == 1 else 1, has_side_effects=True, vmem_limit_bytes=48 * 2**20
        ),
        name="dynamo_step" if rounds == 1 else "general_step",
    )(state, spin, device, drow, dcol, weights, angle)


def on_device(state, spin, donor_device, donor_row, donor_col, corner_weights, border_angle):
    args = (state[0], spin, donor_device, donor_row, donor_col, corner_weights, border_angle)
    fast, overfull = step(1, *args)
    turns = POINTS // HUBS // SLOTS
    advanced = lax.cond(overfull[0, 0] > 0, lambda: step(turns, *args)[0], lambda: fast)
    return advanced[None]


def solution(mesh):
    placed = (P("panel", None, "colat", "lon"), P("panel", "colat", "lon"), P(), P(), P(), P(), P())
    return jax.shard_map(
        on_device,
        mesh=mesh,
        in_specs=placed,
        out_specs=P("panel", None, "colat", "lon"),
        check_vma=False,
    )
```

```python
import functools

import jax
import jax.numpy as jnp
from jax import lax
from jax.experimental import pallas as pl
from jax.experimental.pallas import tpu as pltpu
from jax.sharding import PartitionSpec as P

MESH = pl.DeviceIdType.MESH
F32, BF16, I32 = jnp.float32, jnp.bfloat16, jnp.int32
ROWS, COLS, WIDTH, LANES = 32, 32, 1024, 128
POINTS, HUBS, SLOTS, PARCEL = 1536, 32, 3, 8
HELD = HUBS * SLOTS
SERVED = 24
DIFFUSE = (0.3, 0.3, 0.3, 0.4, 0.5, 0.5, 0.5)


def iota(shape, dim):
    return lax.broadcasted_iota(I32, shape, dim)


def flag01(cond):
    return jnp.where(cond, 1.0, 0.0).astype(BF16)


def split2(x):
    hi = x.astype(BF16)
    return hi, (x - hi.astype(F32)).astype(BF16)


def split3(x):
    hi, rest = x.astype(BF16), None
    rest = x - hi.astype(F32)
    mid = rest.astype(BF16)
    return hi, mid, (rest - mid.astype(F32)).astype(BF16)


def dot(a, b):
    return lax.dot_general(a, b, (((1,), (0,)), ((), ())), preferred_element_type=F32)


def dot_t(a, b):
    return lax.dot_general(a, b, (((1,), (1,)), ((), ())), preferred_element_type=F32)


def step_kernel(
    rounds,
    state, spin_in, device_in, drow_in, dcol_in, weights_in, angle_in, out, overfull,
    spin, device, drow, dcol, weights, angle, turn_cos, turn_sin, ext, rowsend, rowrecv, colsend, colrecv, p1send, p1recv, p2send, p2recv, summed, spread, spinx,
    lhs_ref, pick_ref, hub_sum, halo_ss, halo_rs, p1_ss, p1_rs, p2_ss, p2_rs, state_sem, table_sems, ready, all_in,
):
    panel, colat, lon = (lax.axis_index(a) for a in ("panel", "colat", "lon"))
    plane, y_lo = lon // 2, lon % 2
    pair, odd = plane // 2, plane % 2
    mix = colat * 2 + odd
    hub = y_lo * 16 + mix
    other = 1 - panel

    barrier = pltpu.get_barrier_semaphore()

    def greet(**where):
        pl.semaphore_signal(barrier, inc=1, device_id=where, device_id_type=MESH)

    def peer(h):
        return dict(colat=(h % 16) // 2, lon=(pair * 2 + h % 2) * 2 + h // 16)

    def across(f):
        return dict(lon=(((pair + f) % 4) * 2 + odd) * 2 + y_lo)

    whole_state = pltpu.make_async_copy(state, ext.at[0, :, :, pl.ds(LANES, WIDTH)], state_sem)
    tables = [
        pltpu.make_async_copy(source, target, table_sems.at[i])
        for i, (source, target) in enumerate(
            zip(
                (device_in, drow_in, dcol_in, weights_in, spin_in, angle_in),
                (device, drow, dcol, weights, spin, angle),
                strict=True,
            )
        )
    ]
    for copy in tables[:4]:
        copy.start()
    whole_state.start()
    for copy in tables[4:]:
        copy.start()

    @pl.loop(1, HUBS)
    def _(f):
        greet(**peer((hub + f) % HUBS))

    @pl.loop(1, 4)
    def _(f):
        greet(**across(f))

    greet(panel=other)
    north, south = (colat + 7) % 8, (colat + 1) % 8
    west, east = (lon + 15) % 16, (lon + 1) % 16
    greet(lon=west)
    greet(lon=east)

    lane = iota((1, LANES), 1)
    group = lane // 32
    shell = lane % 32

    def pack_halo(ref, base, rnd):
        for side, row in ((0, 0), (1, ROWS - 1)):
            for f in range(7):
                rowsend[rnd, side, f : f + 1, :] = ref[f, row : row + 1, base : base + WIDTH]
            rowsend[rnd, side, 7:8, :] = jnp.zeros((1, WIDTH), F32)
        for side, tile, have in ((0, base, 0), (1, base + WIDTH - LANES, 3)):
            for half, fields in ((0, range(4)), (1, range(4, 7))):
                total = jnp.zeros((ROWS, LANES), F32)
                for f in fields:
                    moved = pltpu.roll(ref[f, :, tile : tile + LANES], 32 * ((f % 4 - have) % 4), 1)
                    total = jnp.where(group == f % 4, moved, total)
                colsend[rnd, side, half] = total

    def halo_copies(rnd):
        def copy(src, dst, i, **where):
            return pltpu.make_async_remote_copy(
                src_ref=src, dst_ref=dst, send_sem=halo_ss.at[rnd, i], recv_sem=halo_rs.at[rnd, i],
                device_id=where, device_id_type=MESH,
            )

        return [
            copy(rowsend.at[rnd, 0], rowrecv.at[rnd, 1], 0, colat=north),
            copy(rowsend.at[rnd, 1], rowrecv.at[rnd, 0], 1, colat=south),
            copy(colsend.at[rnd, 0], colrecv.at[rnd, 1], 2, lon=west),
            copy(colsend.at[rnd, 1], colrecv.at[rnd, 0], 3, lon=east),
        ]

    for copy in tables:
        copy.wait()
    grow = (device[0:1, :] // 16) * ROWS + drow[0:1, :]
    gcol = (device[0:1, :] % 16) * COLS + dcol[0:1, :]
    along_row = weights[1:2, :] + weights[3:4, :]
    along_row0 = weights[0:1, :] + weights[2:3, :]
    along_col = weights[2:3, :] + weights[3:4, :]
    along_col0 = weights[0:1, :] + weights[1:2, :]

    def held(rr, cc):
        return (rr >= -1) & (rr < ROWS) & (cc >= -1) & (cc < COLS)

    rr, cc = grow - colat * ROWS, gcol - lon * COLS
    mine_row = jnp.where(held(rr, cc), 1.0, 0.0)
    point = iota((1, POINTS), 1)
    segment_of = point // 32
    side = jnp.where(segment_of < 32, 1 - segment_of % 2, jnp.where(segment_of < 40, 1, 0))
    point_hub = side * 16 + point % 16
    lists = []
    for y in range(2):
        part = jnp.where(side == y, mine_row, 0.0)
        lists += [part[:, t * LANES : (t + 1) * LANES] for t in range(12)] + [jnp.zeros((4, LANES), F32)]
    lists = jnp.concatenate(lists, axis=0).astype(BF16)
    up, down = iota((LANES, LANES), 0), iota((LANES, LANES), 1)
    same = up % 16 == down % 16
    before = dot(lists, flag01(same & (up < down)))
    whole = dot(lists, flag01(same)).astype(BF16)
    up, down = iota((32, 32), 0), iota((32, 32), 1)
    rank = before + dot(flag01((up > down) & (up // 16 == down // 16)), whole)
    ranks = [jnp.concatenate([rank[16 * y + t : 16 * y + t + 1, :] for t in range(12)], axis=1) for y in range(2)]
    rank_row = jnp.where(side == 0, ranks[0], ranks[1])
    slot_row = iota((HELD, 1), 0)
    cell = iota((ROWS, 1), 0)
    row_w = jnp.where(cell == rr, along_row0, 0.0) + jnp.where(cell == rr + 1, along_row, 0.0)
    col_w = jnp.where(cell == cc, along_col0, 0.0) + jnp.where(cell == cc + 1, along_col, 0.0)
    row_hi, row_lo = split2(row_w)
    col_hi, col_lo = split2(col_w)
    row_parts = jnp.concatenate([row_hi, row_lo, row_hi, row_hi * 0], axis=0)
    col_parts = jnp.concatenate([col_hi, col_lo, col_lo * 0, col_lo * 0], axis=0)
    cell4 = iota((LANES, WIDTH), 0)
    expand = flag01((cell4 % 32 == iota((LANES, WIDTH), 1) // 32))

    def fill_slots(turn):
        order = rank_row.astype(I32) - turn * SLOTS
        slot = jnp.where(
            (mine_row > 0.0) & (order >= 0) & (order < SLOTS), point_hub * SLOTS + order, -1
        )
        chosen = flag01(slot == slot_row)
        lhs_ref[...] = dot_t(chosen, row_parts).astype(BF16)
        spread[...] = dot(dot_t(chosen, col_parts).astype(BF16), expand)

    spin_parts = jnp.concatenate(list(split3(spin[0])) + [jnp.zeros((ROWS, COLS), BF16)], axis=1)
    spinx[...] = dot(spin_parts, expand)

    out_row = iota((4 * SERVED, 1), 0)
    served = out_row // 4
    quarter = jnp.where(served < 16, 2 * (served % 2) + 1 - y_lo, served % 4)
    my_lane = 32 * quarter + 16 * ((out_row // 2) % 2) + colat * 2 + odd

    def column(values):
        tiles = [values[:, t * LANES : (t + 1) * LANES] for t in range(12)]
        tall = [jnp.broadcast_to(tile, (8, LANES)) for tile in tiles[:8]]
        tall += [
            jnp.broadcast_to(jnp.where(y_lo == 1, tiles[8 + i], tiles[10 + i]), (16, LANES)) for i in range(2)
        ]
        return jnp.sum(jnp.where(lane == my_lane, jnp.concatenate(tall, axis=0), 0), axis=1, keepdims=True)

    parcel_lane = iota((1, HUBS * PARCEL), 1)
    source = parcel_lane // PARCEL
    s_rr = column(grow) - ((source % 16) // 2) * ROWS
    s_cc = column(gcol) - ((pair * 2 + source % 2) * 2 + source // 16) * COLS
    has = held(s_rr, s_cc)
    count_row, count_col = (iota((4 * SERVED, 4 * SERVED), d) for d in range(2))
    seen = dot(flag01((count_col // 2 < count_row // 2) & (count_col % 2 == 0)), flag01(has))

    def fill_picks(turn):
        slot = seen.astype(I32) - turn * SLOTS
        take = has & (slot == parcel_lane % 4) & (slot < SLOTS) & (out_row % 2 == (parcel_lane % PARCEL) // 4)
        pick_ref[...] = flag01(take)

    if rounds == 1:
        fill_slots(0)
        fill_picks(0)

    every = iota((LANES, 1), 0)
    counts = dot_t(
        flag01(held(grow - (every // 16) * ROWS, gcol - (every % 16) * COLS)),
        flag01(iota((LANES, 1), 0) == point_hub),
    )
    overfull[0, 0] = jnp.where(jnp.max(counts) > SLOTS, 1, 0)

    row_id = iota((ROWS, 1), 0)
    inv_radius = 1.0 / (1.0 + 0.25 * (shell.astype(F32) + 0.5) / 32)
    theta = jnp.pi / 4 + ((colat * ROWS + row_id).astype(F32) + 0.5) * (jnp.pi / 512.0)
    metric_p = inv_radius / jnp.sin(theta)

    def rate(rnd, base_ref, base_off, dst, dst_off, dt):
        mt, mp = inv_radius, metric_p
        mt2, mp2 = mt * mt, mp * mp
        centre = 2.0 * (mt2 + mp2 + 1.0)
        half_t, half_p = (0.5 * dt) * mt, (0.5 * dt) * mp

        @pl.loop(0, 8)
        def _(t):
            off = pl.multiple_of(t * LANES, LANES)

            def tile(f, k):
                return ext[rnd, f, :, pl.ds(pl.multiple_of(off + k * LANES, LANES), LANES)]

            ut, up_, ur, temp, bt, bp, br = (tile(f, 1) for f in range(7))
            fields = (ut, up_, ur, temp, bt, bp, br)
            at, ap, ar = ut * half_t, up_ * half_p, ur * (0.5 * dt)
            st, sp, sr = bt * half_t, bp * half_p, br * (0.5 * dt)
            spin_dt = spinx[:, pl.ds(off, LANES)] * dt
            base, stretch = [], []
            for f, c in enumerate(fields):
                n = jnp.where(row_id == 0, 0.0, pltpu.roll(c, 1, 0))
                s = jnp.where(row_id == ROWS - 1, 0.0, pltpu.roll(c, ROWS - 1, 0))
                w = pltpu.roll(jnp.where(group == 3, tile(f, 0), c), 32, 1)
                e = pltpu.roll(jnp.where(group == 0, tile(f, 2), c), 96, 1)
                u = jnp.where(shell == 31, c, pltpu.roll(c, 127, 1))
                d = jnp.where(shell == 0, c, pltpu.roll(c, 1, 1))
                laplace = mt2 * (s + n) + mp2 * (e + w) + (u + d) - centre * c
                sn, ew, ud = s - n, e - w, u - d
                base.append((DIFFUSE[f] * dt) * laplace - (at * sn + ap * ew + ar * ud))
                stretch.append(st * sn + sp * ew + sr * ud if f != 3 else None)
            add = [
                stretch[4] + spin_dt * up_,
                stretch[5] - spin_dt * ut,
                stretch[6] + dt * temp,
                None,
                stretch[0],
                stretch[1],
                stretch[2],
            ]
            for f in range(7):
                value = base_ref[f, :, pl.ds(pl.multiple_of(base_off + off, LANES), LANES)] + base[f]
                if add[f] is not None:
                    value = value + add[f]
                dst[f, :, pl.ds(pl.multiple_of(dst_off + off, LANES), LANES)] = value

    edges = [
        (colat == 0, lon),
        (colat == 7, 16 + lon),
        (lon == 0, 32 + colat),
        (lon == 15, 40 + colat),
    ]

    field_id = iota((8, 1), 0)
    diffuse = jnp.where(field_id < 3, DIFFUSE[0], jnp.where(field_id == 3, DIFFUSE[3], DIFFUSE[6]))

    def add_row(rnd, dst, dst_off, dt, row, sign, values):
        for t in range(8):
            tile = slice(LANES + t * LANES, LANES + (t + 1) * LANES)
            v = values(t)
            at = ext[rnd, 0, row : row + 1, tile] * (inv_radius * (0.5 * dt * sign))
            st = ext[rnd, 4, row : row + 1, tile] * (inv_radius * (0.5 * dt * sign))
            change = (dt * diffuse * (inv_radius * inv_radius) - at) * v + st * pltpu.roll(v, 4, 0)
            for f in range(7):
                place_at = (f, slice(row, row + 1), slice(dst_off + t * LANES, dst_off + (t + 1) * LANES))
                dst[place_at] += change[f : f + 1]

    def add_col(rnd, dst, dst_off, dt, t, sign, values):
        tile = slice(LANES + t * LANES, LANES + (t + 1) * LANES)
        ap = ext[rnd, 1, :, tile] * (metric_p * (0.5 * dt * sign))
        sp = ext[rnd, 5, :, tile] * (metric_p * (0.5 * dt * sign))
        spread_p = metric_p * metric_p * dt
        vs = [values(f) for f in range(7)]
        for f in range(7):
            change = (DIFFUSE[f] * spread_p - ap) * vs[f]
            if f != 3:
                change = change + sp * vs[(f + 4) % 8]
            place_at = (f, slice(None), slice(dst_off + t * LANES, dst_off + (t + 1) * LANES))
            dst[place_at] += change

    def add_halos(rnd, dst, dst_off, dt):
        def recv_row(side):
            return lambda t: rowrecv[rnd, side, :, t * LANES : (t + 1) * LANES]

        def recv_col(side, goal):
            def values(f):
                moved = pltpu.roll(colrecv[rnd, side, f // 4], 32 * ((goal - f % 4) % 4), 1)
                return jnp.where(group == goal, moved, 0.0)

            return values

        pl.when(colat > 0)(lambda: add_row(rnd, dst, dst_off, dt, 0, -1.0, recv_row(0)))
        pl.when(colat < 7)(lambda: add_row(rnd, dst, dst_off, dt, ROWS - 1, 1.0, recv_row(1)))
        pl.when(lon > 0)(lambda: add_col(rnd, dst, dst_off, dt, 0, -1.0, recv_col(0, 0)))
        pl.when(lon < 15)(lambda: add_col(rnd, dst, dst_off, dt, 7, 1.0, recv_col(1, 3)))

    def clear_border(ref, base):
        for kind, row in ((0, 0), (1, ROWS - 1)):

            @pl.when(edges[kind][0])
            def _():
                for f in range(7):
                    ref[f, row : row + 1, base : base + WIDTH] = jnp.zeros((1, WIDTH), F32)

        for kind, off, goal in ((2, base, 0), (3, base + WIDTH - LANES, 3)):

            @pl.when(edges[kind][0])
            def _():
                for f in range(7):
                    ref[f, :, off : off + LANES] = jnp.where(group == goal, 0.0, ref[f, :, off : off + LANES])

    def add_border(dst, dst_off, dt):
        def ext_row(row):
            def values(t):
                tile = slice(LANES + t * LANES, LANES + (t + 1) * LANES)
                rows = [ext[1, f, row : row + 1, tile] for f in range(7)]
                return jnp.concatenate(rows + [jnp.zeros((1, LANES), F32)], axis=0)

            return values

        def ext_col(t, shift, goal):
            def values(f):
                have = ext[1, f, :, LANES + t * LANES : LANES + (t + 1) * LANES]
                return jnp.where(group == goal, pltpu.roll(have, shift, 1), 0.0)

            return values

        pl.when(colat == 0)(lambda: add_row(1, dst, dst_off, dt, 1, -1.0, ext_row(0)))
        pl.when(colat == 7)(lambda: add_row(1, dst, dst_off, dt, ROWS - 2, 1.0, ext_row(ROWS - 1)))
        pl.when(lon == 0)(lambda: add_col(1, dst, dst_off, dt, 0, -1.0, ext_col(0, 32, 1)))
        pl.when(lon == 15)(lambda: add_col(1, dst, dst_off, dt, 7, 1.0, ext_col(7, 96, 2)))

    def send_points(ref, base, rnd):
        def turn_points(turn):
            halves = [jnp.zeros((HELD, LANES), F32) for _ in range(2)]
            lhs = lhs_ref[...][:, :96]
            for f in range(7):
                hi, lo = split2(ref[f, :, base : base + WIDTH])
                rows = dot(lhs, jnp.concatenate([hi, hi, lo], axis=0))
                folded = jnp.zeros((HELD, LANES), F32)
                for t in range(8):
                    folded += rows[:, t * LANES : (t + 1) * LANES] * spread[:, t * LANES : (t + 1) * LANES]
                folded += pltpu.roll(folded, 32, 1)
                folded += pltpu.roll(folded, 64, 1)
                halves[f // 4] = jnp.where(group == f % 4, folded, halves[f // 4])
            for h in range(HUBS):
                for half in range(2):
                    p1send[rnd, turn, h, half * 4 : half * 4 + SLOTS, :] = halves[half][
                        h * SLOTS : (h + 1) * SLOTS
                    ]
            p1recv[rnd, turn, hub] = p1send[rnd, turn, hub]

            @pl.loop(1, HUBS)
            def _(f):
                h = (hub + f) % HUBS
                pltpu.make_async_remote_copy(
                    src_ref=p1send.at[rnd, turn, h], dst_ref=p1recv.at[rnd, turn, hub],
                    send_sem=p1_ss.at[rnd, turn], recv_sem=p1_rs.at[rnd, turn],
                    device_id=peer(h), device_id_type=MESH,
                ).start()

        if rounds == 1:
            turn_points(0)
        else:

            @pl.loop(0, rounds)
            def _(turn):
                fill_slots(turn)
                turn_points(turn)

    def wait_bytes(ref, sem):
        pltpu.make_async_copy(ref, ref, sem).wait()

    def relay(rnd):
        def turn_sum(turn):
            wait_bytes(p1recv.at[rnd, turn, pl.ds(0, HUBS - 1)], p1_rs.at[rnd, turn])
            parts = jnp.concatenate(split3(p1recv[rnd, turn].reshape(HUBS * PARCEL, LANES)), axis=0)
            pick = pick_ref[...]
            return dot(jnp.concatenate([pick, pick, pick], axis=1), parts)

        if rounds == 1:
            picked = turn_sum(0)
        else:
            hub_sum[...] = jnp.zeros_like(hub_sum)

            @pl.loop(0, rounds)
            def _(turn):
                fill_picks(turn)
                hub_sum[...] += turn_sum(turn)

            picked = hub_sum[...]
        for q in range(SERVED):
            p2send[rnd, q] = picked[4 * q : 4 * q + 4, :]
        if rnd == 0:
            pl.semaphore_wait(all_in, 1)

        def send(q, kind, to_colat, to_lon):
            pltpu.make_async_remote_copy(
                src_ref=p2send.at[rnd, q], dst_ref=p2recv.at[rnd, kind, pair * 16 + mix],
                send_sem=p2_ss.at[rnd], recv_sem=p2_rs.at[rnd, kind],
                device_id=dict(panel=other, colat=to_colat, lon=to_lon), device_id_type=MESH,
            ).start()

        @pl.loop(0, 8)
        def _(i):
            send(i, 0, 0, 2 * i + 1 - y_lo)
            send(8 + i, 1, 7, 2 * i + 1 - y_lo)

        for y, kind, to_lon in ((1, 2, 0), (0, 3, 15)):

            @pl.when(y_lo == y)
            def _():
                @pl.loop(0, 8)
                def _(i):
                    send(16 + i, kind, i, to_lon)

    def make_turns():
        line = iota((64, 1), 0)
        line_point = 16 * ((line // 2) % 2) + line // 4
        for kind, (here, segment) in enumerate(edges):

            @pl.when(here)
            def _():
                own = angle[pl.ds(pl.multiple_of((segment // 4) * LANES, LANES), LANES)].reshape(1, LANES)
                own = jnp.where(lane == (segment % 4) * 32 + line_point, own, 0.0)
                own = jnp.sum(own, axis=1, keepdims=True)
                cosine, sine = jnp.cos(own), jnp.sin(own)
                turn_cos[kind] = jnp.where(group < 2, cosine, 1.0)
                turn_sin[kind] = jnp.where(group == 0, -sine, jnp.where(group == 1, sine, 0.0))

    def place(rnd, ref, base):
        for kind, (here, segment) in enumerate(edges):

            @pl.when(here)
            def _():
                wait_bytes(p2recv.at[rnd, kind], p2_rs.at[rnd, kind])
                total = p2recv[rnd, kind, 0:16]
                for z in range(1, 4):
                    total = total + p2recv[rnd, kind, z * 16 : (z + 1) * 16]
                for h in range(16):
                    summed[4 * h : 4 * h + 4, :] = total[h]
                x = summed[...]
                swap = jnp.where(group == 0, pltpu.roll(x, 96, 1), pltpu.roll(x, 32, 1))
                summed[...] = turn_cos[kind] * x + turn_sin[kind] * swap
                if kind < 2:
                    quads = [
                        [
                            jnp.concatenate(
                                [summed[pl.ds(4 * g + 2 * p + half, 4, stride=16), :] for p in range(2)], axis=0
                            )
                            for g in range(4)
                        ]
                        for half in range(2)
                    ]
                else:
                    columns = [
                        jnp.concatenate([summed[pl.ds(2 * p + half, 16, stride=4), :] for p in range(2)], axis=0)
                        for half in range(2)
                    ]
                for f in range(7):
                    if kind < 2:
                        row = 0 if kind == 0 else ROWS - 1
                        tiles = jnp.zeros((8, LANES), F32)
                        for g in range(4):
                            moved = pltpu.roll(quads[f // 4][g], 32 * ((g - f % 4) % 4), 1)
                            tiles = jnp.where(group == g, moved, tiles)
                        for t in range(8):
                            ref[f, row : row + 1, base + t * LANES : base + (t + 1) * LANES] = tiles[t : t + 1]
                    else:
                        goal, off = (0, base) if kind == 2 else (3, base + WIDTH - LANES)
                        moved = pltpu.roll(columns[f // 4], 32 * ((goal - f % 4) % 4), 1)
                        now = ref[f, :, off : off + LANES]
                        corner = ((row_id == 0) & (colat == 0)) | ((row_id == ROWS - 1) & (colat == 7))
                        blend = jnp.where(corner, 0.5 * (moved + now), moved)
                        ref[f, :, off : off + LANES] = jnp.where(group == goal, blend, now)

    for f in range(7):
        for rnd in range(2):
            ext[rnd, f, :, :LANES] = jnp.zeros((ROWS, LANES), F32)
            ext[rnd, f, :, LANES + WIDTH :] = jnp.zeros((ROWS, LANES), F32)
    p1send[...] = jnp.zeros(p1send.shape, F32)
    whole_state.wait()
    pack_halo(ext.at[0], LANES, 0)
    pl.semaphore_wait(barrier, 31 + 3 + 1 + 2)
    halos0 = halo_copies(0)
    for copy in halos0:
        copy.start()

    @pl.loop(1, 4)
    def _(f):
        pl.semaphore_signal(ready, inc=1, device_id=across(f), device_id_type=MESH)

    rate(0, ext.at[0], LANES, ext.at[1], LANES, 0.1)
    for copy in halos0:
        copy.wait_recv()
    add_halos(0, ext.at[1], LANES, 0.1)
    clear_border(ext.at[1], LANES)
    send_points(ext.at[1], LANES, 0)
    pl.semaphore_wait(ready, 3)
    pl.semaphore_signal(all_in, inc=1, device_id=dict(panel=other), device_id_type=MESH)
    pack_halo(ext.at[1], LANES, 1)
    halos1 = halo_copies(1)
    for copy in halos1:
        copy.start()
    relay(0)
    make_turns()
    rate(1, ext.at[0], LANES, out, 0, 0.2)
    for copy in halos1:
        copy.wait_recv()
    add_halos(1, out, 0, 0.2)
    place(0, ext.at[1], LANES)
    add_border(out, 0, 0.2)
    send_points(out, 0, 1)
    relay(1)
    place(1, out, 0)
    for copy in halos0 + halos1:
        copy.wait_send()
    for rnd in range(2):
        for turn in range(rounds):
            wait_bytes(p1send.at[rnd, turn, pl.ds(0, HUBS - 1)], p1_ss.at[rnd, turn])
        wait_bytes(p2send.at[rnd], p2_ss.at[rnd])


def step(rounds, state, spin, device, drow, dcol, weights, angle):
    vmem = pl.BlockSpec(memory_space=pltpu.VMEM)
    scratch = lambda *shape: pltpu.VMEM(shape, F32)
    return pl.pallas_call(
        functools.partial(step_kernel, rounds),
        out_shape=(
            jax.ShapeDtypeStruct((7, ROWS, WIDTH), F32),
            jax.ShapeDtypeStruct((1, 1), I32),
        ),
        in_specs=[pl.BlockSpec(memory_space=pl.ANY)] * 7,
        out_specs=(vmem, pl.BlockSpec(memory_space=pltpu.SMEM)),
        scratch_shapes=[
            scratch(1, ROWS, COLS),
            pltpu.VMEM((4, POINTS), I32),
            pltpu.VMEM((4, POINTS), I32),
            pltpu.VMEM((4, POINTS), I32),
            scratch(4, POINTS),
            scratch(POINTS),
            scratch(4, 64, LANES),
            scratch(4, 64, LANES),
            scratch(2, 7, ROWS, WIDTH + 2 * LANES),
            scratch(2, 2, 8, WIDTH),
            scratch(2, 2, 8, WIDTH),
            scratch(2, 2, 2, ROWS, LANES),
            scratch(2, 2, 2, ROWS, LANES),
            scratch(2, rounds, HUBS, PARCEL, LANES),
            scratch(2, rounds, HUBS, PARCEL, LANES),
            scratch(2, SERVED, 4, LANES),
            scratch(2, 4, 64, 4, LANES),
            scratch(64, LANES),
            scratch(HELD, WIDTH),
            scratch(ROWS, WIDTH),
            pltpu.VMEM((HELD, LANES), BF16),
            pltpu.VMEM((4 * SERVED, HUBS * PARCEL), BF16),
            scratch(4 * SERVED, LANES),
            pltpu.SemaphoreType.DMA((2, 4)),
            pltpu.SemaphoreType.DMA((2, 4)),
            pltpu.SemaphoreType.DMA((2, rounds)),
            pltpu.SemaphoreType.DMA((2, rounds)),
            pltpu.SemaphoreType.DMA((2,)),
            pltpu.SemaphoreType.DMA((2, 4)),
            pltpu.SemaphoreType.DMA,
            pltpu.SemaphoreType.DMA((6,)),
            pltpu.SemaphoreType.REGULAR,
            pltpu.SemaphoreType.REGULAR,
        ],
        compiler_params=pltpu.CompilerParams(
            collective_id=0 if rounds == 1 else 1, has_side_effects=True, vmem_limit_bytes=48 * 2**20
        ),
        name="dynamo_step" if rounds == 1 else "general_step",
    )(state, spin, device, drow, dcol, weights, angle)


def on_device(state, spin, donor_device, donor_row, donor_col, corner_weights, border_angle):
    args = (state[0], spin, donor_device, donor_row, donor_col, corner_weights, border_angle)
    fast, overfull = step(1, *args)
    turns = -(-POINTS // (HUBS * SLOTS))
    advanced = lax.cond(overfull[0, 0] > 0, lambda: step(turns, *args)[0], lambda: fast)
    return advanced[None]


def solution(mesh):
    placed = (P("panel", None, "colat", "lon"), P("panel", "colat", "lon"), P(), P(), P(), P(), P())
    return jax.shard_map(
        on_device,
        mesh=mesh,
        in_specs=placed,
        out_specs=P("panel", None, "colat", "lon"),
        check_vma=False,
    )
```

```python
import functools

import jax
import jax.numpy as jnp
from jax import lax
from jax.experimental import pallas as pl
from jax.experimental.pallas import tpu as pltpu
from jax.sharding import PartitionSpec as P

MESH = pl.DeviceIdType.MESH
F32, BF16, I32 = jnp.float32, jnp.bfloat16, jnp.int32
ROWS, COLS, WIDTH, LANES = 32, 32, 1024, 128
POINTS, HUBS, SLOTS, PARCEL = 1536, 32, 3, 8
HELD = HUBS * SLOTS
SERVED = 24
PEERS = sorted(
    [(c, k, y, o) for c in range(4) for k in range(2) for y in range(2) for o in range(2) if c or k or y or o],
    key=lambda s: -(min(s[0], 4 - s[0]) + s[2] + s[3]),
)
DIFFUSE = (0.3, 0.3, 0.3, 0.4, 0.5, 0.5, 0.5)


def iota(shape, dim):
    return lax.broadcasted_iota(I32, shape, dim)


def flag01(cond):
    return jnp.where(cond, 1.0, 0.0).astype(BF16)


def split2(x):
    hi = x.astype(BF16)
    return hi, (x - hi.astype(F32)).astype(BF16)


def split3(x):
    hi, rest = x.astype(BF16), None
    rest = x - hi.astype(F32)
    mid = rest.astype(BF16)
    return hi, mid, (rest - mid.astype(F32)).astype(BF16)


def dot(a, b):
    return lax.dot_general(a, b, (((1,), (0,)), ((), ())), preferred_element_type=F32)


def dot_t(a, b):
    return lax.dot_general(a, b, (((1,), (1,)), ((), ())), preferred_element_type=F32)


def step_kernel(
    rounds,
    state, spin_in, device_in, drow_in, dcol_in, weights_in, angle_in, out, overfull,
    spin, device, drow, dcol, weights, angle, turn_cos, turn_sin, ext, rowsend, rowrecv, colsend, colrecv, p1send, p1recv, p2send, p2recv, summed, spread, spinx,
    lhs_ref, pick_ref, hub_sum, halo_ss, halo_rs, p1_ss, p1_rs, p2_ss, p2_rs, state_sem, table_sems, ready, all_in,
):
    panel, colat, lon = (lax.axis_index(a) for a in ("panel", "colat", "lon"))
    plane, y_lo = lon // 2, lon % 2
    pair, odd = plane // 2, plane % 2
    mix = colat * 2 + odd
    hub = y_lo * 16 + mix
    other = 1 - panel

    barrier = pltpu.get_barrier_semaphore()

    def greet(**where):
        pl.semaphore_signal(barrier, inc=1, device_id=where, device_id_type=MESH)

    def peer(h):
        return dict(colat=(h % 16) // 2, lon=(pair * 2 + h % 2) * 2 + h // 16)

    def peer_hub(step):
        chip, core, side_step, odd_step = step
        to_colat = ((colat // 2 + chip) % 4) * 2 + (colat + core) % 2
        return ((y_lo + side_step) % 2) * 16 + to_colat * 2 + (odd + odd_step) % 2

    def across(f):
        return dict(lon=(((pair + f) % 4) * 2 + odd) * 2 + y_lo)

    whole_state = pltpu.make_async_copy(state, ext.at[0, :, :, pl.ds(LANES, WIDTH)], state_sem)
    tables = [
        pltpu.make_async_copy(source, target, table_sems.at[i])
        for i, (source, target) in enumerate(
            zip(
                (device_in, drow_in, dcol_in, weights_in, spin_in, angle_in),
                (device, drow, dcol, weights, spin, angle),
                strict=True,
            )
        )
    ]
    for copy in tables[:4]:
        copy.start()
    whole_state.start()
    for copy in tables[4:]:
        copy.start()

    for step in PEERS:
        greet(**peer(peer_hub(step)))

    @pl.loop(1, 4)
    def _(f):
        greet(**across(f))

    greet(panel=other)
    north, south = (colat + 7) % 8, (colat + 1) % 8
    west, east = (lon + 15) % 16, (lon + 1) % 16
    greet(lon=west)
    greet(lon=east)

    lane = iota((1, LANES), 1)
    group = lane // 32
    shell = lane % 32

    def pack_halo(ref, base, rnd):
        for side, row in ((0, 0), (1, ROWS - 1)):
            for f in range(7):
                rowsend[rnd, side, f : f + 1, :] = ref[f, row : row + 1, base : base + WIDTH]
            rowsend[rnd, side, 7:8, :] = jnp.zeros((1, WIDTH), F32)
        for side, tile, have in ((0, base, 0), (1, base + WIDTH - LANES, 3)):
            for half, fields in ((0, range(4)), (1, range(4, 7))):
                total = jnp.zeros((ROWS, LANES), F32)
                for f in fields:
                    moved = pltpu.roll(ref[f, :, tile : tile + LANES], 32 * ((f % 4 - have) % 4), 1)
                    total = jnp.where(group == f % 4, moved, total)
                colsend[rnd, side, half] = total

    def halo_copies(rnd):
        def copy(src, dst, i, **where):
            return pltpu.make_async_remote_copy(
                src_ref=src, dst_ref=dst, send_sem=halo_ss.at[rnd, i], recv_sem=halo_rs.at[rnd, i],
                device_id=where, device_id_type=MESH,
            )

        return [
            copy(rowsend.at[rnd, 0], rowrecv.at[rnd, 1], 0, colat=north),
            copy(rowsend.at[rnd, 1], rowrecv.at[rnd, 0], 1, colat=south),
            copy(colsend.at[rnd, 0], colrecv.at[rnd, 1], 2, lon=west),
            copy(colsend.at[rnd, 1], colrecv.at[rnd, 0], 3, lon=east),
        ]

    for copy in tables:
        copy.wait()
    grow = (device[0:1, :] // 16) * ROWS + drow[0:1, :]
    gcol = (device[0:1, :] % 16) * COLS + dcol[0:1, :]
    along_row = weights[1:2, :] + weights[3:4, :]
    along_row0 = weights[0:1, :] + weights[2:3, :]
    along_col = weights[2:3, :] + weights[3:4, :]
    along_col0 = weights[0:1, :] + weights[1:2, :]

    def held(rr, cc):
        return (rr >= -1) & (rr < ROWS) & (cc >= -1) & (cc < COLS)

    rr, cc = grow - colat * ROWS, gcol - lon * COLS
    mine_row = jnp.where(held(rr, cc), 1.0, 0.0)
    point = iota((1, POINTS), 1)
    segment_of = point // 32
    side = jnp.where(segment_of < 32, 1 - segment_of % 2, jnp.where(segment_of < 40, 1, 0))
    point_hub = side * 16 + point % 16
    lists = []
    for y in range(2):
        part = jnp.where(side == y, mine_row, 0.0)
        lists += [part[:, t * LANES : (t + 1) * LANES] for t in range(12)] + [jnp.zeros((4, LANES), F32)]
    lists = jnp.concatenate(lists, axis=0).astype(BF16)
    up, down = iota((LANES, LANES), 0), iota((LANES, LANES), 1)
    same = up % 16 == down % 16
    before = dot(lists, flag01(same & (up < down)))
    whole = dot(lists, flag01(same)).astype(BF16)
    up, down = iota((32, 32), 0), iota((32, 32), 1)
    rank = before + dot(flag01((up > down) & (up // 16 == down // 16)), whole)
    ranks = [jnp.concatenate([rank[16 * y + t : 16 * y + t + 1, :] for t in range(12)], axis=1) for y in range(2)]
    rank_row = jnp.where(side == 0, ranks[0], ranks[1])
    slot_row = iota((HELD, 1), 0)
    cell = iota((ROWS, 1), 0)
    row_w = jnp.where(cell == rr, along_row0, 0.0) + jnp.where(cell == rr + 1, along_row, 0.0)
    col_w = jnp.where(cell == cc, along_col0, 0.0) + jnp.where(cell == cc + 1, along_col, 0.0)
    row_hi, row_lo = split2(row_w)
    col_hi, col_lo = split2(col_w)
    row_parts = jnp.concatenate([row_hi, row_lo, row_hi, row_hi * 0], axis=0)
    col_parts = jnp.concatenate([col_hi, col_lo, col_lo * 0, col_lo * 0], axis=0)
    cell4 = iota((LANES, WIDTH), 0)
    expand = flag01((cell4 % 32 == iota((LANES, WIDTH), 1) // 32))

    def fill_slots(turn):
        order = rank_row.astype(I32) - turn * SLOTS
        slot = jnp.where(
            (mine_row > 0.0) & (order >= 0) & (order < SLOTS), point_hub * SLOTS + order, -1
        )
        chosen = flag01(slot == slot_row)
        lhs_ref[...] = dot_t(chosen, row_parts).astype(BF16)
        spread[...] = dot(dot_t(chosen, col_parts).astype(BF16), expand)

    spin_parts = jnp.concatenate(list(split3(spin[0])) + [jnp.zeros((ROWS, COLS), BF16)], axis=1)
    spinx[...] = dot(spin_parts, expand)

    out_row = iota((4 * SERVED, 1), 0)
    served = out_row // 4
    quarter = jnp.where(served < 16, 2 * (served % 2) + 1 - y_lo, served % 4)
    my_lane = 32 * quarter + 16 * ((out_row // 2) % 2) + colat * 2 + odd

    def column(values):
        tiles = [values[:, t * LANES : (t + 1) * LANES] for t in range(12)]
        tall = [jnp.broadcast_to(tile, (8, LANES)) for tile in tiles[:8]]
        tall += [
            jnp.broadcast_to(jnp.where(y_lo == 1, tiles[8 + i], tiles[10 + i]), (16, LANES)) for i in range(2)
        ]
        return jnp.sum(jnp.where(lane == my_lane, jnp.concatenate(tall, axis=0), 0), axis=1, keepdims=True)

    parcel_lane = iota((1, HUBS * PARCEL), 1)
    source = parcel_lane // PARCEL
    s_rr = column(grow) - ((source % 16) // 2) * ROWS
    s_cc = column(gcol) - ((pair * 2 + source % 2) * 2 + source // 16) * COLS
    has = held(s_rr, s_cc)
    count_row, count_col = (iota((4 * SERVED, 4 * SERVED), d) for d in range(2))
    seen = dot(flag01((count_col // 2 < count_row // 2) & (count_col % 2 == 0)), flag01(has))

    def fill_picks(turn):
        slot = seen.astype(I32) - turn * SLOTS
        take = has & (slot == parcel_lane % 4) & (slot < SLOTS) & (out_row % 2 == (parcel_lane % PARCEL) // 4)
        pick_ref[...] = flag01(take)

    if rounds == 1:
        fill_slots(0)
        fill_picks(0)

    every = iota((LANES, 1), 0)
    counts = dot_t(
        flag01(held(grow - (every // 16) * ROWS, gcol - (every % 16) * COLS)),
        flag01(iota((LANES, 1), 0) == point_hub),
    )
    overfull[0, 0] = jnp.where(jnp.max(counts) > SLOTS, 1, 0)

    row_id = iota((ROWS, 1), 0)
    inv_radius = 1.0 / (1.0 + 0.25 * (shell.astype(F32) + 0.5) / 32)
    theta = jnp.pi / 4 + ((colat * ROWS + row_id).astype(F32) + 0.5) * (jnp.pi / 512.0)
    metric_p = inv_radius / jnp.sin(theta)

    def rate(rnd, base_ref, base_off, dst, dst_off, dt):
        mt, mp = inv_radius, metric_p
        mt2, mp2 = mt * mt, mp * mp
        centre = 2.0 * (mt2 + mp2 + 1.0)
        half_t, half_p = (0.5 * dt) * mt, (0.5 * dt) * mp

        @pl.loop(0, 8)
        def _(t):
            off = pl.multiple_of(t * LANES, LANES)

            def tile(f, k):
                return ext[rnd, f, :, pl.ds(pl.multiple_of(off + k * LANES, LANES), LANES)]

            ut, up_, ur, temp, bt, bp, br = (tile(f, 1) for f in range(7))
            fields = (ut, up_, ur, temp, bt, bp, br)
            at, ap, ar = ut * half_t, up_ * half_p, ur * (0.5 * dt)
            st, sp, sr = bt * half_t, bp * half_p, br * (0.5 * dt)
            spin_dt = spinx[:, pl.ds(off, LANES)] * dt
            base, stretch = [], []
            for f, c in enumerate(fields):
                n = jnp.where(row_id == 0, 0.0, pltpu.roll(c, 1, 0))
                s = jnp.where(row_id == ROWS - 1, 0.0, pltpu.roll(c, ROWS - 1, 0))
                w = pltpu.roll(jnp.where(group == 3, tile(f, 0), c), 32, 1)
                e = pltpu.roll(jnp.where(group == 0, tile(f, 2), c), 96, 1)
                u = jnp.where(shell == 31, c, pltpu.roll(c, 127, 1))
                d = jnp.where(shell == 0, c, pltpu.roll(c, 1, 1))
                laplace = mt2 * (s + n) + mp2 * (e + w) + (u + d) - centre * c
                sn, ew, ud = s - n, e - w, u - d
                base.append((DIFFUSE[f] * dt) * laplace - (at * sn + ap * ew + ar * ud))
                stretch.append(st * sn + sp * ew + sr * ud if f != 3 else None)
            add = [
                stretch[4] + spin_dt * up_,
                stretch[5] - spin_dt * ut,
                stretch[6] + dt * temp,
                None,
                stretch[0],
                stretch[1],
                stretch[2],
            ]
            for f in range(7):
                value = base_ref[f, :, pl.ds(pl.multiple_of(base_off + off, LANES), LANES)] + base[f]
                if add[f] is not None:
                    value = value + add[f]
                dst[f, :, pl.ds(pl.multiple_of(dst_off + off, LANES), LANES)] = value

    edges = [
        (colat == 0, lon),
        (colat == 7, 16 + lon),
        (lon == 0, 32 + colat),
        (lon == 15, 40 + colat),
    ]

    field_id = iota((8, 1), 0)
    diffuse = jnp.where(field_id < 3, DIFFUSE[0], jnp.where(field_id == 3, DIFFUSE[3], DIFFUSE[6]))

    def add_row(rnd, dst, dst_off, dt, row, sign, values):
        for t in range(8):
            tile = slice(LANES + t * LANES, LANES + (t + 1) * LANES)
            v = values(t)
            at = ext[rnd, 0, row : row + 1, tile] * (inv_radius * (0.5 * dt * sign))
            st = ext[rnd, 4, row : row + 1, tile] * (inv_radius * (0.5 * dt * sign))
            change = (dt * diffuse * (inv_radius * inv_radius) - at) * v + st * pltpu.roll(v, 4, 0)
            for f in range(7):
                place_at = (f, slice(row, row + 1), slice(dst_off + t * LANES, dst_off + (t + 1) * LANES))
                dst[place_at] += change[f : f + 1]

    def add_col(rnd, dst, dst_off, dt, t, sign, values):
        tile = slice(LANES + t * LANES, LANES + (t + 1) * LANES)
        ap = ext[rnd, 1, :, tile] * (metric_p * (0.5 * dt * sign))
        sp = ext[rnd, 5, :, tile] * (metric_p * (0.5 * dt * sign))
        spread_p = metric_p * metric_p * dt
        vs = [values(f) for f in range(7)]
        for f in range(7):
            change = (DIFFUSE[f] * spread_p - ap) * vs[f]
            if f != 3:
                change = change + sp * vs[(f + 4) % 8]
            place_at = (f, slice(None), slice(dst_off + t * LANES, dst_off + (t + 1) * LANES))
            dst[place_at] += change

    def add_halos(rnd, copies, dst, dst_off, dt):
        def recv_row(side):
            return lambda t: rowrecv[rnd, side, :, t * LANES : (t + 1) * LANES]

        def recv_col(side, goal):
            def values(f):
                moved = pltpu.roll(colrecv[rnd, side, f // 4], 32 * ((goal - f % 4) % 4), 1)
                return jnp.where(group == goal, moved, 0.0)

            return values

        for copy in copies[:2]:
            copy.wait_recv()
        pl.when(colat > 0)(lambda: add_row(rnd, dst, dst_off, dt, 0, -1.0, recv_row(0)))
        pl.when(colat < 7)(lambda: add_row(rnd, dst, dst_off, dt, ROWS - 1, 1.0, recv_row(1)))
        for copy in copies[2:]:
            copy.wait_recv()
        pl.when(lon > 0)(lambda: add_col(rnd, dst, dst_off, dt, 0, -1.0, recv_col(0, 0)))
        pl.when(lon < 15)(lambda: add_col(rnd, dst, dst_off, dt, 7, 1.0, recv_col(1, 3)))

    def clear_border(ref, base):
        for kind, row in ((0, 0), (1, ROWS - 1)):

            @pl.when(edges[kind][0])
            def _():
                for f in range(7):
                    ref[f, row : row + 1, base : base + WIDTH] = jnp.zeros((1, WIDTH), F32)

        for kind, off, goal in ((2, base, 0), (3, base + WIDTH - LANES, 3)):

            @pl.when(edges[kind][0])
            def _():
                for f in range(7):
                    ref[f, :, off : off + LANES] = jnp.where(group == goal, 0.0, ref[f, :, off : off + LANES])

    def add_border(dst, dst_off, dt):
        def ext_row(row):
            def values(t):
                tile = slice(LANES + t * LANES, LANES + (t + 1) * LANES)
                rows = [ext[1, f, row : row + 1, tile] for f in range(7)]
                return jnp.concatenate(rows + [jnp.zeros((1, LANES), F32)], axis=0)

            return values

        def ext_col(t, shift, goal):
            def values(f):
                have = ext[1, f, :, LANES + t * LANES : LANES + (t + 1) * LANES]
                return jnp.where(group == goal, pltpu.roll(have, shift, 1), 0.0)

            return values

        pl.when(colat == 0)(lambda: add_row(1, dst, dst_off, dt, 1, -1.0, ext_row(0)))
        pl.when(colat == 7)(lambda: add_row(1, dst, dst_off, dt, ROWS - 2, 1.0, ext_row(ROWS - 1)))
        pl.when(lon == 0)(lambda: add_col(1, dst, dst_off, dt, 0, -1.0, ext_col(0, 32, 1)))
        pl.when(lon == 15)(lambda: add_col(1, dst, dst_off, dt, 7, 1.0, ext_col(7, 96, 2)))

    def send_points(ref, base, rnd):
        def turn_points(turn):
            found = []
            lhs = lhs_ref[...][:, :96]
            for f in range(7):
                hi, lo = split2(ref[f, :, base : base + WIDTH])
                rows = dot(lhs, jnp.concatenate([hi, hi, lo], axis=0))
                folded = jnp.zeros((HELD, LANES), F32)
                for t in range(8):
                    folded += rows[:, t * LANES : (t + 1) * LANES] * spread[:, t * LANES : (t + 1) * LANES]
                found.append(folded)
            even, left = group % 2 == 0, group < 2

            def fold(a, b, c, d):
                ab = jnp.where(even, a, b) + pltpu.roll(jnp.where(even, b, a), 96, 1)
                cd = jnp.where(even, c, d) + pltpu.roll(jnp.where(even, d, c), 96, 1)
                return jnp.where(left, ab, cd) + pltpu.roll(jnp.where(left, cd, ab), 64, 1)

            halves = [fold(*found[:4]), fold(*found[4:], found[6])]
            for h in range(HUBS):
                for half in range(2):
                    p1send[rnd, turn, h, half * 4 : half * 4 + SLOTS, :] = halves[half][
                        h * SLOTS : (h + 1) * SLOTS
                    ]
            p1recv[rnd, turn, hub] = p1send[rnd, turn, hub]

            for step in PEERS:
                h = peer_hub(step)
                pltpu.make_async_remote_copy(
                    src_ref=p1send.at[rnd, turn, h], dst_ref=p1recv.at[rnd, turn, hub],
                    send_sem=p1_ss.at[rnd, turn], recv_sem=p1_rs.at[rnd, turn],
                    device_id=peer(h), device_id_type=MESH,
                ).start()

        if rounds == 1:
            turn_points(0)
        else:

            @pl.loop(0, rounds)
            def _(turn):
                fill_slots(turn)
                turn_points(turn)

    def wait_bytes(ref, sem):
        pltpu.make_async_copy(ref, ref, sem).wait()

    def relay(rnd):
        def turn_sum(turn):
            wait_bytes(p1recv.at[rnd, turn, pl.ds(0, HUBS - 1)], p1_rs.at[rnd, turn])
            parts = jnp.concatenate(split3(p1recv[rnd, turn].reshape(HUBS * PARCEL, LANES)), axis=0)
            pick = pick_ref[...]
            return dot(jnp.concatenate([pick, pick, pick], axis=1), parts)

        if rounds == 1:
            picked = turn_sum(0)
        else:
            hub_sum[...] = jnp.zeros_like(hub_sum)

            @pl.loop(0, rounds)
            def _(turn):
                fill_picks(turn)
                hub_sum[...] += turn_sum(turn)

            picked = hub_sum[...]
        for q in range(SERVED):
            p2send[rnd, q] = picked[4 * q : 4 * q + 4, :]
        if rnd == 0:
            pl.semaphore_wait(all_in, 1)

        def send(q, kind, to_colat, to_lon):
            pltpu.make_async_remote_copy(
                src_ref=p2send.at[rnd, q], dst_ref=p2recv.at[rnd, kind, pair * 16 + mix],
                send_sem=p2_ss.at[rnd], recv_sem=p2_rs.at[rnd, kind],
                device_id=dict(panel=other, colat=to_colat, lon=to_lon), device_id_type=MESH,
            ).start()

        for i in range(8):
            send(i, 0, 0, 2 * i + 1 - y_lo)
            send(8 + i, 1, 7, 2 * i + 1 - y_lo)

        for y, kind, to_lon in ((1, 2, 0), (0, 3, 15)):

            @pl.when(y_lo == y)
            def _():
                for i in range(8):
                    send(16 + i, kind, i, to_lon)

    def make_turns():
        line = iota((64, 1), 0)
        line_point = 16 * ((line // 2) % 2) + line // 4
        for kind, (here, segment) in enumerate(edges):

            @pl.when(here)
            def _():
                own = angle[pl.ds(pl.multiple_of((segment // 4) * LANES, LANES), LANES)].reshape(1, LANES)
                own = jnp.where(lane == (segment % 4) * 32 + line_point, own, 0.0)
                own = jnp.sum(own, axis=1, keepdims=True)
                cosine, sine = jnp.cos(own), jnp.sin(own)
                turn_cos[kind] = jnp.where(group < 2, cosine, 1.0)
                turn_sin[kind] = jnp.where(group == 0, -sine, jnp.where(group == 1, sine, 0.0))

    def place(rnd, ref, base):
        for kind, (here, segment) in enumerate(edges):

            @pl.when(here)
            def _():
                wait_bytes(p2recv.at[rnd, kind], p2_rs.at[rnd, kind])
                total = p2recv[rnd, kind, 0:16]
                for z in range(1, 4):
                    total = total + p2recv[rnd, kind, z * 16 : (z + 1) * 16]
                for h in range(16):
                    summed[4 * h : 4 * h + 4, :] = total[h]
                x = summed[...]
                swap = jnp.where(group == 0, pltpu.roll(x, 96, 1), pltpu.roll(x, 32, 1))
                summed[...] = turn_cos[kind] * x + turn_sin[kind] * swap
                if kind < 2:
                    quads = [
                        [
                            jnp.concatenate(
                                [summed[pl.ds(4 * g + 2 * p + half, 4, stride=16), :] for p in range(2)], axis=0
                            )
                            for g in range(4)
                        ]
                        for half in range(2)
                    ]
                else:
                    columns = [
                        jnp.concatenate([summed[pl.ds(2 * p + half, 16, stride=4), :] for p in range(2)], axis=0)
                        for half in range(2)
                    ]
                for f in range(7):
                    if kind < 2:
                        row = 0 if kind == 0 else ROWS - 1
                        tiles = jnp.zeros((8, LANES), F32)
                        for g in range(4):
                            moved = pltpu.roll(quads[f // 4][g], 32 * ((g - f % 4) % 4), 1)
                            tiles = jnp.where(group == g, moved, tiles)
                        for t in range(8):
                            ref[f, row : row + 1, base + t * LANES : base + (t + 1) * LANES] = tiles[t : t + 1]
                    else:
                        goal, off = (0, base) if kind == 2 else (3, base + WIDTH - LANES)
                        moved = pltpu.roll(columns[f // 4], 32 * ((goal - f % 4) % 4), 1)
                        now = ref[f, :, off : off + LANES]
                        corner = ((row_id == 0) & (colat == 0)) | ((row_id == ROWS - 1) & (colat == 7))
                        blend = jnp.where(corner, 0.5 * (moved + now), moved)
                        ref[f, :, off : off + LANES] = jnp.where(group == goal, blend, now)

    for f in range(7):
        for rnd in range(2):
            ext[rnd, f, :, :LANES] = jnp.zeros((ROWS, LANES), F32)
            ext[rnd, f, :, LANES + WIDTH :] = jnp.zeros((ROWS, LANES), F32)
    p1send[...] = jnp.zeros(p1send.shape, F32)
    whole_state.wait()
    pack_halo(ext.at[0], LANES, 0)
    pl.semaphore_wait(barrier, 31 + 3 + 1 + 2)
    halos0 = halo_copies(0)
    for copy in halos0:
        copy.start()

    @pl.loop(1, 4)
    def _(f):
        pl.semaphore_signal(ready, inc=1, device_id=across(f), device_id_type=MESH)

    rate(0, ext.at[0], LANES, ext.at[1], LANES, 0.1)
    add_halos(0, halos0, ext.at[1], LANES, 0.1)
    clear_border(ext.at[1], LANES)
    send_points(ext.at[1], LANES, 0)
    pl.semaphore_wait(ready, 3)
    pl.semaphore_signal(all_in, inc=1, device_id=dict(panel=other), device_id_type=MESH)
    pack_halo(ext.at[1], LANES, 1)
    halos1 = halo_copies(1)
    for copy in halos1:
        copy.start()
    relay(0)
    make_turns()
    rate(1, ext.at[0], LANES, out, 0, 0.2)
    add_halos(1, halos1, out, 0, 0.2)
    place(0, ext.at[1], LANES)
    add_border(out, 0, 0.2)
    send_points(out, 0, 1)
    relay(1)
    place(1, out, 0)
    for copy in halos0 + halos1:
        copy.wait_send()
    for rnd in range(2):
        for turn in range(rounds):
            wait_bytes(p1send.at[rnd, turn, pl.ds(0, HUBS - 1)], p1_ss.at[rnd, turn])
        wait_bytes(p2send.at[rnd], p2_ss.at[rnd])


def step(rounds, state, spin, device, drow, dcol, weights, angle):
    vmem = pl.BlockSpec(memory_space=pltpu.VMEM)
    scratch = lambda *shape: pltpu.VMEM(shape, F32)
    return pl.pallas_call(
        functools.partial(step_kernel, rounds),
        out_shape=(
            jax.ShapeDtypeStruct((7, ROWS, WIDTH), F32),
            jax.ShapeDtypeStruct((1, 1), I32),
        ),
        in_specs=[pl.BlockSpec(memory_space=pl.ANY)] * 7,
        out_specs=(vmem, pl.BlockSpec(memory_space=pltpu.SMEM)),
        scratch_shapes=[
            scratch(1, ROWS, COLS),
            pltpu.VMEM((4, POINTS), I32),
            pltpu.VMEM((4, POINTS), I32),
            pltpu.VMEM((4, POINTS), I32),
            scratch(4, POINTS),
            scratch(POINTS),
            scratch(4, 64, LANES),
            scratch(4, 64, LANES),
            scratch(2, 7, ROWS, WIDTH + 2 * LANES),
            scratch(2, 2, 8, WIDTH),
            scratch(2, 2, 8, WIDTH),
            scratch(2, 2, 2, ROWS, LANES),
            scratch(2, 2, 2, ROWS, LANES),
            scratch(2, rounds, HUBS, PARCEL, LANES),
            scratch(2, rounds, HUBS, PARCEL, LANES),
            scratch(2, SERVED, 4, LANES),
            scratch(2, 4, 64, 4, LANES),
            scratch(64, LANES),
            scratch(HELD, WIDTH),
            scratch(ROWS, WIDTH),
            pltpu.VMEM((HELD, LANES), BF16),
            pltpu.VMEM((4 * SERVED, HUBS * PARCEL), BF16),
            scratch(4 * SERVED, LANES),
            pltpu.SemaphoreType.DMA((2, 4)),
            pltpu.SemaphoreType.DMA((2, 4)),
            pltpu.SemaphoreType.DMA((2, rounds)),
            pltpu.SemaphoreType.DMA((2, rounds)),
            pltpu.SemaphoreType.DMA((2,)),
            pltpu.SemaphoreType.DMA((2, 4)),
            pltpu.SemaphoreType.DMA,
            pltpu.SemaphoreType.DMA((6,)),
            pltpu.SemaphoreType.REGULAR,
            pltpu.SemaphoreType.REGULAR,
        ],
        compiler_params=pltpu.CompilerParams(
            collective_id=0 if rounds == 1 else 1, has_side_effects=True, vmem_limit_bytes=48 * 2**20
        ),
        name="dynamo_step" if rounds == 1 else "general_step",
    )(state, spin, device, drow, dcol, weights, angle)


def on_device(state, spin, donor_device, donor_row, donor_col, corner_weights, border_angle):
    args = (state[0], spin, donor_device, donor_row, donor_col, corner_weights, border_angle)
    fast, overfull = step(1, *args)
    turns = -(-POINTS // (HUBS * SLOTS))
    advanced = lax.switch(overfull[0, 0], [lambda: fast, lambda: step(turns, *args)[0]])
    return advanced[None]


def solution(mesh):
    placed = (P("panel", None, "colat", "lon"), P("panel", "colat", "lon"), P(), P(), P(), P(), P())
    return jax.shard_map(
        on_device,
        mesh=mesh,
        in_specs=placed,
        out_specs=P("panel", None, "colat", "lon"),
        check_vma=False,
    )
```

```python
import functools

import jax
import jax.numpy as jnp
from jax import lax
from jax.experimental import pallas as pl
from jax.experimental.pallas import tpu as pltpu
from jax.sharding import PartitionSpec as P

MESH = pl.DeviceIdType.MESH
F32, BF16, I32 = jnp.float32, jnp.bfloat16, jnp.int32
ROWS, COLS, WIDTH, LANES = 32, 32, 1024, 128
POINTS, HUBS, SLOTS, PARCEL = 1536, 32, 3, 8
HELD = HUBS * SLOTS
SERVED = 24
PEERS = sorted(
    [(c, k, y, o) for c in range(4) for k in range(2) for y in range(2) for o in range(2) if c or k or y or o],
    key=lambda s: -(min(s[0], 4 - s[0]) + s[2] + s[3]),
)
DIFFUSE = (0.3, 0.3, 0.3, 0.4, 0.5, 0.5, 0.5)


def iota(shape, dim):
    return lax.broadcasted_iota(I32, shape, dim)


def flag01(cond):
    return jnp.where(cond, 1.0, 0.0).astype(BF16)


def split2(x):
    hi = x.astype(BF16)
    return hi, (x - hi.astype(F32)).astype(BF16)


def split3(x):
    hi, rest = x.astype(BF16), None
    rest = x - hi.astype(F32)
    mid = rest.astype(BF16)
    return hi, mid, (rest - mid.astype(F32)).astype(BF16)


def dot(a, b):
    return lax.dot_general(a, b, (((1,), (0,)), ((), ())), preferred_element_type=F32)


def dot_t(a, b):
    return lax.dot_general(a, b, (((1,), (1,)), ((), ())), preferred_element_type=F32)


def step_kernel(
    rounds,
    state, spin_in, device_in, drow_in, dcol_in, weights_in, angle_in, out, overfull,
    spin, device, drow, dcol, weights, angle, turn_cos, turn_sin, ext, rowsend, rowrecv, colsend, colrecv, p1send, p1recv, p2send, p2recv, summed, spread, spinx,
    lhs_ref, pick_ref, hub_sum, halo_ss, halo_rs, p1_ss, p1_rs, p2_ss, p2_rs, state_sem, table_sems, ready, all_in,
):
    panel, colat, lon = (lax.axis_index(a) for a in ("panel", "colat", "lon"))
    plane, y_lo = lon // 2, lon % 2
    pair, odd = plane // 2, plane % 2
    mix = colat * 2 + odd
    hub = y_lo * 16 + mix
    other = 1 - panel

    barrier = pltpu.get_barrier_semaphore()

    def greet(**where):
        pl.semaphore_signal(barrier, inc=1, device_id=where, device_id_type=MESH)

    def peer(h):
        return dict(colat=(h % 16) // 2, lon=(pair * 2 + h % 2) * 2 + h // 16)

    def peer_hub(step):
        chip, core, side_step, odd_step = step
        to_colat = ((colat // 2 + chip) % 4) * 2 + (colat + core) % 2
        return ((y_lo + side_step) % 2) * 16 + to_colat * 2 + (odd + odd_step) % 2

    def across(f):
        return dict(lon=(((pair + f) % 4) * 2 + odd) * 2 + y_lo)

    whole_state = pltpu.make_async_copy(state, ext.at[0, :, :, pl.ds(LANES, WIDTH)], state_sem)
    tables = [
        pltpu.make_async_copy(source, target, table_sems.at[i])
        for i, (source, target) in enumerate(
            zip(
                (device_in, drow_in, dcol_in, weights_in, spin_in, angle_in),
                (device, drow, dcol, weights, spin, angle),
                strict=True,
            )
        )
    ]
    for copy in tables[:4]:
        copy.start()
    whole_state.start()
    for copy in tables[4:]:
        copy.start()

    for step in PEERS:
        greet(**peer(peer_hub(step)))

    for f in (2, 1, 3):
        greet(**across(f))
    greet(panel=other)
    north, south = (colat + 7) % 8, (colat + 1) % 8
    west, east = (lon + 15) % 16, (lon + 1) % 16
    greet(lon=west)
    greet(lon=east)

    lane = iota((1, LANES), 1)
    group = lane // 32
    shell = lane % 32

    def pack_halo(ref, base, rnd):
        for side, row in ((0, 0), (1, ROWS - 1)):
            for f in range(7):
                rowsend[rnd, side, f : f + 1, :] = ref[f, row : row + 1, base : base + WIDTH]
            rowsend[rnd, side, 7:8, :] = jnp.zeros((1, WIDTH), F32)
        for side, tile, have in ((0, base, 0), (1, base + WIDTH - LANES, 3)):
            for half, fields in ((0, range(4)), (1, range(4, 7))):
                total = jnp.zeros((ROWS, LANES), F32)
                for f in fields:
                    moved = pltpu.roll(ref[f, :, tile : tile + LANES], 32 * ((f % 4 - have) % 4), 1)
                    total = jnp.where(group == f % 4, moved, total)
                colsend[rnd, side, half] = total

    def halo_copies(rnd):
        def copy(src, dst, i, **where):
            return pltpu.make_async_remote_copy(
                src_ref=src, dst_ref=dst, send_sem=halo_ss.at[rnd, i], recv_sem=halo_rs.at[rnd, i],
                device_id=where, device_id_type=MESH,
            )

        return [
            copy(rowsend.at[rnd, 0], rowrecv.at[rnd, 1], 0, colat=north),
            copy(rowsend.at[rnd, 1], rowrecv.at[rnd, 0], 1, colat=south),
            copy(colsend.at[rnd, 0], colrecv.at[rnd, 1], 2, lon=west),
            copy(colsend.at[rnd, 1], colrecv.at[rnd, 0], 3, lon=east),
        ]

    for copy in tables:
        copy.wait()
    grow = (device[0:1, :] // 16) * ROWS + drow[0:1, :]
    gcol = (device[0:1, :] % 16) * COLS + dcol[0:1, :]
    along_row = weights[1:2, :] + weights[3:4, :]
    along_row0 = weights[0:1, :] + weights[2:3, :]
    along_col = weights[2:3, :] + weights[3:4, :]
    along_col0 = weights[0:1, :] + weights[1:2, :]

    def held(rr, cc):
        return (rr >= -1) & (rr < ROWS) & (cc >= -1) & (cc < COLS)

    rr, cc = grow - colat * ROWS, gcol - lon * COLS
    mine_row = jnp.where(held(rr, cc), 1.0, 0.0)
    point = iota((1, POINTS), 1)
    segment_of = point // 32
    side = jnp.where(segment_of < 32, 1 - segment_of % 2, jnp.where(segment_of < 40, 1, 0))
    point_hub = side * 16 + point % 16
    lists = []
    for y in range(2):
        part = jnp.where(side == y, mine_row, 0.0)
        lists += [part[:, t * LANES : (t + 1) * LANES] for t in range(12)] + [jnp.zeros((4, LANES), F32)]
    lists = jnp.concatenate(lists, axis=0).astype(BF16)
    up, down = iota((LANES, LANES), 0), iota((LANES, LANES), 1)
    same = up % 16 == down % 16
    before = dot(lists, flag01(same & (up < down)))
    whole = dot(lists, flag01(same)).astype(BF16)
    up, down = iota((32, 32), 0), iota((32, 32), 1)
    rank = before + dot(flag01((up > down) & (up // 16 == down // 16)), whole)
    ranks = [jnp.concatenate([rank[16 * y + t : 16 * y + t + 1, :] for t in range(12)], axis=1) for y in range(2)]
    rank_row = jnp.where(side == 0, ranks[0], ranks[1])
    slot_row = iota((HELD, 1), 0)
    cell = iota((ROWS, 1), 0)
    row_w = jnp.where(cell == rr, along_row0, 0.0) + jnp.where(cell == rr + 1, along_row, 0.0)
    col_w = jnp.where(cell == cc, along_col0, 0.0) + jnp.where(cell == cc + 1, along_col, 0.0)
    row_hi, row_lo = split2(row_w)
    col_hi, col_lo = split2(col_w)
    row_parts = jnp.concatenate([row_hi, row_lo, row_hi, row_hi * 0], axis=0)
    col_parts = jnp.concatenate([col_hi, col_lo, col_lo * 0, col_lo * 0], axis=0)
    cell4 = iota((LANES, WIDTH), 0)
    expand = flag01((cell4 % 32 == iota((LANES, WIDTH), 1) // 32))

    def fill_slots(turn):
        order = rank_row.astype(I32) - turn * SLOTS
        slot = jnp.where(
            (mine_row > 0.0) & (order >= 0) & (order < SLOTS), point_hub * SLOTS + order, -1
        )
        chosen = flag01(slot == slot_row)
        lhs_ref[...] = dot_t(chosen, row_parts).astype(BF16)
        spread[...] = dot(dot_t(chosen, col_parts).astype(BF16), expand)

    spin_parts = jnp.concatenate(list(split3(spin[0])) + [jnp.zeros((ROWS, COLS), BF16)], axis=1)
    spinx[...] = dot(spin_parts, expand)

    out_row = iota((4 * SERVED, 1), 0)
    served = out_row // 4
    quarter = jnp.where(served < 16, 2 * (served % 2) + 1 - y_lo, served % 4)
    my_lane = 32 * quarter + 16 * ((out_row // 2) % 2) + colat * 2 + odd

    def column(values):
        tiles = [values[:, t * LANES : (t + 1) * LANES] for t in range(12)]
        tall = [jnp.broadcast_to(tile, (8, LANES)) for tile in tiles[:8]]
        tall += [
            jnp.broadcast_to(jnp.where(y_lo == 1, tiles[8 + i], tiles[10 + i]), (16, LANES)) for i in range(2)
        ]
        return jnp.sum(jnp.where(lane == my_lane, jnp.concatenate(tall, axis=0), 0), axis=1, keepdims=True)

    parcel_lane = iota((1, HUBS * PARCEL), 1)
    source = parcel_lane // PARCEL
    s_rr = column(grow) - ((source % 16) // 2) * ROWS
    s_cc = column(gcol) - ((pair * 2 + source % 2) * 2 + source // 16) * COLS
    has = held(s_rr, s_cc)
    count_row, count_col = (iota((4 * SERVED, 4 * SERVED), d) for d in range(2))
    seen = dot(flag01((count_col // 2 < count_row // 2) & (count_col % 2 == 0)), flag01(has))

    def fill_picks(turn):
        slot = seen.astype(I32) - turn * SLOTS
        take = has & (slot == parcel_lane % 4) & (slot < SLOTS) & (out_row % 2 == (parcel_lane % PARCEL) // 4)
        pick_ref[...] = flag01(take)

    if rounds == 1:
        fill_slots(0)
        fill_picks(0)

    every = iota((LANES, 1), 0)
    counts = dot_t(
        flag01(held(grow - (every // 16) * ROWS, gcol - (every % 16) * COLS)),
        flag01(iota((LANES, 1), 0) == point_hub),
    )
    overfull[0, 0] = jnp.where(jnp.max(counts) > SLOTS, 1, 0)

    row_id = iota((ROWS, 1), 0)
    inv_radius = 1.0 / (1.0 + 0.25 * (shell.astype(F32) + 0.5) / 32)
    theta = jnp.pi / 4 + ((colat * ROWS + row_id).astype(F32) + 0.5) * (jnp.pi / 512.0)
    metric_p = inv_radius / jnp.sin(theta)

    def rate(rnd, base_ref, base_off, dst, dst_off, dt):
        mt, mp = inv_radius, metric_p
        mt2, mp2 = mt * mt, mp * mp
        centre = 2.0 * (mt2 + mp2 + 1.0)
        half_t, half_p = (0.5 * dt) * mt, (0.5 * dt) * mp

        @pl.loop(0, 8)
        def _(t):
            off = pl.multiple_of(t * LANES, LANES)

            def tile(f, k):
                return ext[rnd, f, :, pl.ds(pl.multiple_of(off + k * LANES, LANES), LANES)]

            ut, up_, ur, temp, bt, bp, br = (tile(f, 1) for f in range(7))
            fields = (ut, up_, ur, temp, bt, bp, br)
            at, ap, ar = ut * half_t, up_ * half_p, ur * (0.5 * dt)
            st, sp, sr = bt * half_t, bp * half_p, br * (0.5 * dt)
            spin_dt = spinx[:, pl.ds(off, LANES)] * dt
            base, stretch = [], []
            for f, c in enumerate(fields):
                n = jnp.where(row_id == 0, 0.0, pltpu.roll(c, 1, 0))
                s = jnp.where(row_id == ROWS - 1, 0.0, pltpu.roll(c, ROWS - 1, 0))
                w = pltpu.roll(jnp.where(group == 3, tile(f, 0), c), 32, 1)
                e = pltpu.roll(jnp.where(group == 0, tile(f, 2), c), 96, 1)
                u = jnp.where(shell == 31, c, pltpu.roll(c, 127, 1))
                d = jnp.where(shell == 0, c, pltpu.roll(c, 1, 1))
                laplace = mt2 * (s + n) + mp2 * (e + w) + (u + d) - centre * c
                sn, ew, ud = s - n, e - w, u - d
                base.append((DIFFUSE[f] * dt) * laplace - (at * sn + ap * ew + ar * ud))
                stretch.append(st * sn + sp * ew + sr * ud if f != 3 else None)
            add = [
                stretch[4] + spin_dt * up_,
                stretch[5] - spin_dt * ut,
                stretch[6] + dt * temp,
                None,
                stretch[0],
                stretch[1],
                stretch[2],
            ]
            for f in range(7):
                value = base_ref[f, :, pl.ds(pl.multiple_of(base_off + off, LANES), LANES)] + base[f]
                if add[f] is not None:
                    value = value + add[f]
                dst[f, :, pl.ds(pl.multiple_of(dst_off + off, LANES), LANES)] = value

    edges = [
        (colat == 0, lon),
        (colat == 7, 16 + lon),
        (lon == 0, 32 + colat),
        (lon == 15, 40 + colat),
    ]

    field_id = iota((8, 1), 0)
    diffuse = jnp.where(field_id < 3, DIFFUSE[0], jnp.where(field_id == 3, DIFFUSE[3], DIFFUSE[6]))

    def add_row(rnd, dst, dst_off, dt, row, sign, values):
        for t in range(8):
            tile = slice(LANES + t * LANES, LANES + (t + 1) * LANES)
            v = values(t)
            at = ext[rnd, 0, row : row + 1, tile] * (inv_radius * (0.5 * dt * sign))
            st = ext[rnd, 4, row : row + 1, tile] * (inv_radius * (0.5 * dt * sign))
            change = (dt * diffuse * (inv_radius * inv_radius) - at) * v + st * pltpu.roll(v, 4, 0)
            for f in range(7):
                place_at = (f, slice(row, row + 1), slice(dst_off + t * LANES, dst_off + (t + 1) * LANES))
                dst[place_at] += change[f : f + 1]

    def add_col(rnd, dst, dst_off, dt, t, sign, values):
        tile = slice(LANES + t * LANES, LANES + (t + 1) * LANES)
        ap = ext[rnd, 1, :, tile] * (metric_p * (0.5 * dt * sign))
        sp = ext[rnd, 5, :, tile] * (metric_p * (0.5 * dt * sign))
        spread_p = metric_p * metric_p * dt
        vs = [values(f) for f in range(7)]
        for f in range(7):
            change = (DIFFUSE[f] * spread_p - ap) * vs[f]
            if f != 3:
                change = change + sp * vs[(f + 4) % 8]
            place_at = (f, slice(None), slice(dst_off + t * LANES, dst_off + (t + 1) * LANES))
            dst[place_at] += change

    def add_halos(rnd, copies, dst, dst_off, dt):
        def recv_row(side):
            return lambda t: rowrecv[rnd, side, :, t * LANES : (t + 1) * LANES]

        def recv_col(side, goal):
            def values(f):
                moved = pltpu.roll(colrecv[rnd, side, f // 4], 32 * ((goal - f % 4) % 4), 1)
                return jnp.where(group == goal, moved, 0.0)

            return values

        for copy in copies[:2]:
            copy.wait_recv()
        pl.when(colat > 0)(lambda: add_row(rnd, dst, dst_off, dt, 0, -1.0, recv_row(0)))
        pl.when(colat < 7)(lambda: add_row(rnd, dst, dst_off, dt, ROWS - 1, 1.0, recv_row(1)))
        for copy in copies[2:]:
            copy.wait_recv()
        pl.when(lon > 0)(lambda: add_col(rnd, dst, dst_off, dt, 0, -1.0, recv_col(0, 0)))
        pl.when(lon < 15)(lambda: add_col(rnd, dst, dst_off, dt, 7, 1.0, recv_col(1, 3)))

    def clear_border(ref, base):
        for kind, row in ((0, 0), (1, ROWS - 1)):

            @pl.when(edges[kind][0])
            def _():
                for f in range(7):
                    ref[f, row : row + 1, base : base + WIDTH] = jnp.zeros((1, WIDTH), F32)

        for kind, off, goal in ((2, base, 0), (3, base + WIDTH - LANES, 3)):

            @pl.when(edges[kind][0])
            def _():
                for f in range(7):
                    ref[f, :, off : off + LANES] = jnp.where(group == goal, 0.0, ref[f, :, off : off + LANES])

    def add_border(dst, dst_off, dt):
        def ext_row(row):
            def values(t):
                tile = slice(LANES + t * LANES, LANES + (t + 1) * LANES)
                rows = [ext[1, f, row : row + 1, tile] for f in range(7)]
                return jnp.concatenate(rows + [jnp.zeros((1, LANES), F32)], axis=0)

            return values

        def ext_col(t, shift, goal):
            def values(f):
                have = ext[1, f, :, LANES + t * LANES : LANES + (t + 1) * LANES]
                return jnp.where(group == goal, pltpu.roll(have, shift, 1), 0.0)

            return values

        pl.when(colat == 0)(lambda: add_row(1, dst, dst_off, dt, 1, -1.0, ext_row(0)))
        pl.when(colat == 7)(lambda: add_row(1, dst, dst_off, dt, ROWS - 2, 1.0, ext_row(ROWS - 1)))
        pl.when(lon == 0)(lambda: add_col(1, dst, dst_off, dt, 0, -1.0, ext_col(0, 32, 1)))
        pl.when(lon == 15)(lambda: add_col(1, dst, dst_off, dt, 7, 1.0, ext_col(7, 96, 2)))

    def send_points(ref, base, rnd):
        def turn_points(turn):
            found = []
            lhs = lhs_ref[...][:, :96]
            for f in range(7):
                hi, lo = split2(ref[f, :, base : base + WIDTH])
                stacked = jnp.concatenate([hi, hi, lo], axis=0)
                folded = jnp.zeros((HELD, LANES), F32)
                for t in range(0, 8, 2):
                    rows = dot(lhs, stacked[:, t * LANES : (t + 2) * LANES]) * spread[:, t * LANES : (t + 2) * LANES]
                    folded += rows[:, :LANES] + rows[:, LANES:]
                found.append(folded)
            even, left = group % 2 == 0, group < 2

            def fold(a, b, c, d):
                ab = jnp.where(even, a, b) + pltpu.roll(jnp.where(even, b, a), 96, 1)
                cd = jnp.where(even, c, d) + pltpu.roll(jnp.where(even, d, c), 96, 1)
                return jnp.where(left, ab, cd) + pltpu.roll(jnp.where(left, cd, ab), 64, 1)

            halves = [fold(*found[:4]), fold(*found[4:], found[6])]
            for h in range(HUBS):
                for half in range(2):
                    p1send[rnd, turn, h, half * 4 : half * 4 + SLOTS, :] = halves[half][
                        h * SLOTS : (h + 1) * SLOTS
                    ]
            p1recv[rnd, turn, hub] = p1send[rnd, turn, hub]

            for step in PEERS:
                h = peer_hub(step)
                pltpu.make_async_remote_copy(
                    src_ref=p1send.at[rnd, turn, h], dst_ref=p1recv.at[rnd, turn, hub],
                    send_sem=p1_ss.at[rnd, turn], recv_sem=p1_rs.at[rnd, turn],
                    device_id=peer(h), device_id_type=MESH,
                ).start()

        if rounds == 1:
            turn_points(0)
        else:

            @pl.loop(0, rounds)
            def _(turn):
                fill_slots(turn)
                turn_points(turn)

    def wait_bytes(ref, sem):
        pltpu.make_async_copy(ref, ref, sem).wait()

    def relay(rnd):
        def turn_sum(turn):
            wait_bytes(p1recv.at[rnd, turn, pl.ds(0, HUBS - 1)], p1_rs.at[rnd, turn])
            parts = jnp.concatenate(split3(p1recv[rnd, turn].reshape(HUBS * PARCEL, LANES)), axis=0)
            pick = pick_ref[...]
            return dot(jnp.concatenate([pick, pick, pick], axis=1), parts)

        if rounds == 1:
            picked = turn_sum(0)
        else:
            hub_sum[...] = jnp.zeros_like(hub_sum)

            @pl.loop(0, rounds)
            def _(turn):
                fill_picks(turn)
                hub_sum[...] += turn_sum(turn)

            picked = hub_sum[...]
        for q in range(SERVED):
            p2send[rnd, q] = picked[4 * q : 4 * q + 4, :]
        if rnd == 0:
            pl.semaphore_wait(all_in, 1)

        def send(q, kind, to_colat, to_lon):
            pltpu.make_async_remote_copy(
                src_ref=p2send.at[rnd, q], dst_ref=p2recv.at[rnd, kind, pair * 16 + mix],
                send_sem=p2_ss.at[rnd], recv_sem=p2_rs.at[rnd, kind],
                device_id=dict(panel=other, colat=to_colat, lon=to_lon), device_id_type=MESH,
            ).start()

        for away in (4, 3, 5, 2, 6, 1, 7, 0):
            i = (plane + away) % 8
            send(i, 0, 0, 2 * i + 1 - y_lo)
            send(8 + i, 1, 7, 2 * i + 1 - y_lo)

        for y, kind, to_lon in ((1, 2, 0), (0, 3, 15)):

            @pl.when(y_lo == y)
            def _():
                for i in range(8):
                    send(16 + i, kind, i, to_lon)

    def make_turns():
        line = iota((64, 1), 0)
        line_point = 16 * ((line // 2) % 2) + line // 4
        for kind, (here, segment) in enumerate(edges):

            @pl.when(here)
            def _():
                own = angle[pl.ds(pl.multiple_of((segment // 4) * LANES, LANES), LANES)].reshape(1, LANES)
                own = jnp.where(lane == (segment % 4) * 32 + line_point, own, 0.0)
                own = jnp.sum(own, axis=1, keepdims=True)
                cosine, sine = jnp.cos(own), jnp.sin(own)
                turn_cos[kind] = jnp.where(group < 2, cosine, 1.0)
                turn_sin[kind] = jnp.where(group == 0, -sine, jnp.where(group == 1, sine, 0.0))

    def place(rnd, ref, base):
        for kind, (here, segment) in enumerate(edges):

            @pl.when(here)
            def _():
                wait_bytes(p2recv.at[rnd, kind], p2_rs.at[rnd, kind])
                total = p2recv[rnd, kind, 0:16]
                for z in range(1, 4):
                    total = total + p2recv[rnd, kind, z * 16 : (z + 1) * 16]
                for h in range(16):
                    summed[4 * h : 4 * h + 4, :] = total[h]
                x = summed[...]
                swap = jnp.where(group == 0, pltpu.roll(x, 96, 1), pltpu.roll(x, 32, 1))
                summed[...] = turn_cos[kind] * x + turn_sin[kind] * swap
                if kind < 2:
                    quads = [
                        [
                            jnp.concatenate(
                                [summed[pl.ds(4 * g + 2 * p + half, 4, stride=16), :] for p in range(2)], axis=0
                            )
                            for g in range(4)
                        ]
                        for half in range(2)
                    ]
                else:
                    columns = [
                        jnp.concatenate([summed[pl.ds(2 * p + half, 16, stride=4), :] for p in range(2)], axis=0)
                        for half in range(2)
                    ]
                for f in range(7):
                    if kind < 2:
                        row = 0 if kind == 0 else ROWS - 1
                        tiles = jnp.zeros((8, LANES), F32)
                        for g in range(4):
                            moved = pltpu.roll(quads[f // 4][g], 32 * ((g - f % 4) % 4), 1)
                            tiles = jnp.where(group == g, moved, tiles)
                        for t in range(8):
                            ref[f, row : row + 1, base + t * LANES : base + (t + 1) * LANES] = tiles[t : t + 1]
                    else:
                        goal, off = (0, base) if kind == 2 else (3, base + WIDTH - LANES)
                        moved = pltpu.roll(columns[f // 4], 32 * ((goal - f % 4) % 4), 1)
                        now = ref[f, :, off : off + LANES]
                        corner = ((row_id == 0) & (colat == 0)) | ((row_id == ROWS - 1) & (colat == 7))
                        blend = jnp.where(corner, 0.5 * (moved + now), moved)
                        ref[f, :, off : off + LANES] = jnp.where(group == goal, blend, now)

    for f in range(7):
        for rnd in range(2):
            ext[rnd, f, :, :LANES] = jnp.zeros((ROWS, LANES), F32)
            ext[rnd, f, :, LANES + WIDTH :] = jnp.zeros((ROWS, LANES), F32)
    p1send[...] = jnp.zeros(p1send.shape, F32)
    whole_state.wait()
    pack_halo(ext.at[0], LANES, 0)
    pl.semaphore_wait(barrier, 31 + 3 + 1 + 2)
    halos0 = halo_copies(0)
    for copy in halos0[2:] + halos0[:2]:
        copy.start()

    for f in (2, 1, 3):
        pl.semaphore_signal(ready, inc=1, device_id=across(f), device_id_type=MESH)

    rate(0, ext.at[0], LANES, ext.at[1], LANES, 0.1)
    add_halos(0, halos0, ext.at[1], LANES, 0.1)
    clear_border(ext.at[1], LANES)
    send_points(ext.at[1], LANES, 0)
    pl.semaphore_wait(ready, 3)
    pl.semaphore_signal(all_in, inc=1, device_id=dict(panel=other), device_id_type=MESH)
    pack_halo(ext.at[1], LANES, 1)
    halos1 = halo_copies(1)
    for copy in halos1:
        copy.start()
    relay(0)
    make_turns()
    rate(1, ext.at[0], LANES, out, 0, 0.2)
    add_halos(1, halos1, out, 0, 0.2)
    place(0, ext.at[1], LANES)
    add_border(out, 0, 0.2)
    send_points(out, 0, 1)
    relay(1)
    place(1, out, 0)
    for copy in halos0 + halos1:
        copy.wait_send()
    for rnd in range(2):
        for turn in range(rounds):
            wait_bytes(p1send.at[rnd, turn, pl.ds(0, HUBS - 1)], p1_ss.at[rnd, turn])
        wait_bytes(p2send.at[rnd], p2_ss.at[rnd])


def step(rounds, state, spin, device, drow, dcol, weights, angle):
    vmem = pl.BlockSpec(memory_space=pltpu.VMEM)
    scratch = lambda *shape: pltpu.VMEM(shape, F32)
    return pl.pallas_call(
        functools.partial(step_kernel, rounds),
        out_shape=(
            jax.ShapeDtypeStruct((7, ROWS, WIDTH), F32),
            jax.ShapeDtypeStruct((1, 1), I32),
        ),
        in_specs=[pl.BlockSpec(memory_space=pl.ANY)] * 7,
        out_specs=(vmem, pl.BlockSpec(memory_space=pltpu.SMEM)),
        scratch_shapes=[
            scratch(1, ROWS, COLS),
            pltpu.VMEM((4, POINTS), I32),
            pltpu.VMEM((4, POINTS), I32),
            pltpu.VMEM((4, POINTS), I32),
            scratch(4, POINTS),
            scratch(POINTS),
            scratch(4, 64, LANES),
            scratch(4, 64, LANES),
            scratch(2, 7, ROWS, WIDTH + 2 * LANES),
            scratch(2, 2, 8, WIDTH),
            scratch(2, 2, 8, WIDTH),
            scratch(2, 2, 2, ROWS, LANES),
            scratch(2, 2, 2, ROWS, LANES),
            scratch(2, rounds, HUBS, PARCEL, LANES),
            scratch(2, rounds, HUBS, PARCEL, LANES),
            scratch(2, SERVED, 4, LANES),
            scratch(2, 4, 64, 4, LANES),
            scratch(64, LANES),
            scratch(HELD, WIDTH),
            scratch(ROWS, WIDTH),
            pltpu.VMEM((HELD, LANES), BF16),
            pltpu.VMEM((4 * SERVED, HUBS * PARCEL), BF16),
            scratch(4 * SERVED, LANES),
            pltpu.SemaphoreType.DMA((2, 4)),
            pltpu.SemaphoreType.DMA((2, 4)),
            pltpu.SemaphoreType.DMA((2, rounds)),
            pltpu.SemaphoreType.DMA((2, rounds)),
            pltpu.SemaphoreType.DMA((2,)),
            pltpu.SemaphoreType.DMA((2, 4)),
            pltpu.SemaphoreType.DMA,
            pltpu.SemaphoreType.DMA((6,)),
            pltpu.SemaphoreType.REGULAR,
            pltpu.SemaphoreType.REGULAR,
        ],
        compiler_params=pltpu.CompilerParams(
            collective_id=0 if rounds == 1 else 1, has_side_effects=True, vmem_limit_bytes=48 * 2**20
        ),
        name="dynamo_step" if rounds == 1 else "general_step",
    )(state, spin, device, drow, dcol, weights, angle)


def on_device(state, spin, donor_device, donor_row, donor_col, corner_weights, border_angle):
    args = (state[0], spin, donor_device, donor_row, donor_col, corner_weights, border_angle)
    fast, overfull = step(1, *args)
    turns = -(-POINTS // (HUBS * SLOTS))
    advanced = lax.switch(overfull[0, 0], [lambda: fast, lambda: step(turns, *args)[0]])
    return advanced[None]


def solution(mesh):
    placed = (P("panel", None, "colat", "lon"), P("panel", "colat", "lon"), P(), P(), P(), P(), P())
    return jax.shard_map(
        on_device,
        mesh=mesh,
        in_specs=placed,
        out_specs=P("panel", None, "colat", "lon"),
        check_vma=False,
    )
```
